32 devices in a mesh: batch: 4 (over x, core), seq: 8 (over z, y).
Axes of the slice: x: 2, y: 2, z: 4, core: 2. Of those that a mesh axis runs over, the one named last changes fastest.
Arguments:
- token_ids: int32 [4, 2048], P('batch', 'seq'), may hold values from 0 to 151935, as said below
- row_lengths: int32 [4], replicated, may hold values from 1280 to 2048, as said below
- prompt_lengths: int32 [4], replicated, may hold values from 128 to 511
- picks: int32 [4, 256], P('batch', 'seq'), may hold values from 0 to 254, as said below
- old_logp: float32 [4, 256], P('batch', 'seq'), may hold values from -18 to -10
- ref_logp: float32 [4, 256], P('batch', 'seq'), may hold values from -18 to -10
- rewards: float32 [4], replicated, may hold values from -4 to 4
- embed: float32 [151936, 896], P(('batch', 'seq'))
- embed_m: float32 [151936, 896], P(('batch', 'seq')), may hold values from -3.33786e-06 to 3.33786e-06
- embed_v: float32 [151936, 896], P(('batch', 'seq')), may hold values from 1.09236845e-13 to 1.7213079e-12
- w_qkv: float32 [896, 1152], P('seq'), may hold values from -0.1875 to 0.1875
- w_qkv_m: float32 [896, 1152], P('seq'), may hold values from -6.67572e-06 to 6.67572e-06
- w_qkv_v: float32 [896, 1152], P('seq'), may hold values from 4.3694738e-13 to 6.9514355e-12
- w_out: float32 [896, 896], P('seq'), may hold values from -0.75 to 0.75
- w_out_m: float32 [896, 896], P('seq'), may hold values from -6.67572e-06 to 6.67572e-06
- w_out_v: float32 [896, 896], P('seq'), may hold values from 4.3694738e-13 to 6.9514355e-12
- w_gateup: float32 [896, 9728], P('seq'), may hold values from -0.1875 to 0.1875
- w_gateup_m: float32 [896, 9728], P('seq'), may hold values from -6.67572e-06 to 6.67572e-06
- w_gateup_v: float32 [896, 9728], P('seq'), may hold values from 4.3694738e-13 to 6.9514355e-12
- w_down: float32 [4864, 896], P('seq'), may hold values from -0.078125 to 0.078125
- w_down_m: float32 [4864, 896], P('seq'), may hold values from -6.67572e-06 to 6.67572e-06
- w_down_v: float32 [4864, 896], P('seq'), may hold values from 4.3694738e-13 to 6.9514355e-12
- gains: float32 [3, 896], replicated, may hold values from 0.48 to 2.25
- gains_m: float32 [3, 896], replicated, may hold values from -6.1035156e-05 to 6.1035156e-05
- gains_v: float32 [3, 896], replicated, may hold values from 4.369474e-11 to 6.9514355e-10
- bias: float32 [1152], replicated, may hold values from -3 to 3
- bias_m: float32 [1152], replicated, may hold values from -3.0517578e-05 to 3.0517578e-05
- bias_v: float32 [1152], replicated, may hold values from 1.0923685e-11 to 1.7213078e-10
Outputs:
- loss_sum: float32 [], replicated
- token_count: float32 [], replicated
- grad_norm: float32 [], replicated
- embed_new: float32 [151936, 896], P(('batch', 'seq'))
- embed_m_new: float32 [151936, 896], P(('batch', 'seq'))
- embed_v_new: float32 [151936, 896], P(('batch', 'seq'))
- w_qkv_new: float32 [896, 1152], P('seq')
- w_qkv_m_new: float32 [896, 1152], P('seq')
- w_qkv_v_new: float32 [896, 1152], P('seq')
- w_out_new: float32 [896, 896], P('seq')
- w_out_m_new: float32 [896, 896], P('seq')
- w_out_v_new: float32 [896, 896], P('seq')
- w_gateup_new: float32 [896, 9728], P('seq')
- w_gateup_m_new: float32 [896, 9728], P('seq')
- w_gateup_v_new: float32 [896, 9728], P('seq')
- w_down_new: float32 [4864, 896], P('seq')
- w_down_m_new: float32 [4864, 896], P('seq')
- w_down_v_new: float32 [4864, 896], P('seq')
- gains_new: float32 [3, 896], replicated
- gains_m_new: float32 [3, 896], replicated
- gains_v_new: float32 [3, 896], replicated
- bias_new: float32 [1152], replicated
- bias_m_new: float32 [1152], replicated
- bias_v_new: float32 [1152], replicated
The draws below stay inside these ranges and needn't reach their ends.
Inputs may be any that keep to these rules, and one draw needn't show every extreme that they name: `token_ids`: among the 256 tokens of one device, at most 16 have ids in any one owner's table rows (aligned ranges of 4748 ids), for every owner; on every device some owner receives exactly 16. `row_lengths`: one row has length 2048 in every draw. `picks`: the 32 offsets of one device are distinct.
All inputs are finite; a program needn't handle non-finite values.
Results may differ from the reference program's by a relative error of at most 0.03.
Values may be sent and summed in bfloat16 or wider, within the bound.
No kernel may reach another device: no remote copies, remote signals or barrier semaphores. Data moves between devices by JAX's collectives and lax.ppermute only.
A program may use at most 224 MiB of HBM per device.

```python
import math
import jax
import jax.numpy as jnp
from jax import lax

D = 896
H = 14
KV = 2
HD = 64
FF = 4864
V = 151936
CH = 256
PICK = 32
STEP = 5
B = 4
L = 2048
OWNERS = 32
VROWS = 4748
CAP = 16
QKV = 1152
PARAMS = 151047936
N_SEQ = 8


def draw_token_ids(key, part):
    key = jax.random.fold_in(key, 11)
    pool = OWNERS * CAP

    def one_block(block_key):
        first, second, third, fourth = jax.random.split(block_key, 4)
        order = jax.random.permutation(first, pool)
        favored = jax.random.randint(second, (), 0, OWNERS)
        slots = jnp.arange(pool, dtype=jnp.int32)
        rank = jnp.where(order // CAP == favored, slots, slots + pool)
        front = order[jnp.argsort(rank, stable=True)][:CH]
        owners_here = jax.random.permutation(third, front) // CAP
        return owners_here * VROWS + jax.random.randint(fourth, (CH,), 0, VROWS)
    blocks = jax.vmap(one_block)(jax.random.split(key, OWNERS))
    return blocks.reshape(B, L).astype(jnp.int32)


def draw_row_lengths(key, part):
    key = jax.random.fold_in(key, 12)
    first, second = jax.random.split(key)
    lengths = jax.random.randint(first, (B,), 5 * L // 8, L + 1)
    longest = jax.random.randint(second, (), 0, B)
    return jnp.where(jnp.arange(B) == longest, L, lengths).astype(jnp.int32)


def draw_picks(key, part):
    key = jax.random.fold_in(key, 13)
    first, second = jax.random.split(key)
    orders = jax.vmap(lambda inner: jax.random.permutation(inner, CH - 1))(jax.random.split(first, OWNERS))
    favored = jax.random.randint(second, (), 0, OWNERS)
    slots = jnp.arange(CH - 1, dtype=jnp.int32)[None, :]
    ends = (orders == 0) | (orders == CH - 2)
    rank = jnp.where(ends, slots, slots + CH)
    moved = jnp.take_along_axis(orders, jnp.argsort(rank, axis=1, stable=True), axis=1)
    blocks = jnp.where((jnp.arange(OWNERS) == favored)[:, None], moved, orders)[:, :PICK]
    return blocks.reshape(B, N_SEQ * PICK).astype(jnp.int32)


def draw_embed(key, part):
    key = jax.random.fold_in(key, 14)
    place = jnp.arange(V, dtype=jnp.float32)[:, None] / V
    base = jax.random.normal(key, (V, D), jnp.float32)
    rise = 1.0 + 2.0 * place
    return base * rise * D ** (-0.5)


def draw_gains(key, part):
    key = jax.random.fold_in(key, 15)
    rise = 0.6 + 1.2 * jnp.arange(D, dtype=jnp.float32) / D
    return rise[None, :] * jax.random.uniform(key, (3, D), jnp.float32, 0.8, 1.25)


def with_ends(entries, rng, low, high):
    longest = entries.shape.index(max(entries.shape))
    spots = []
    for shift in (0, 1):
        where = [jax.random.randint(jax.random.fold_in(rng, axis), (), 0, length) for axis, length in enumerate(entries.shape)]
        where[longest] = (where[longest] + shift) % entries.shape[longest]
        spots.append(tuple(where))
    return entries.at[spots[0]].set(low).at[spots[1]].set(high)


def shard_levels(key, extent, pieces, least, largest):
    level, own = 1.0, jax.random.fold_in(key, 6)
    for axis_at, parts in pieces:
        draws = jnp.exp(jax.random.uniform(jax.random.fold_in(own, axis_at), (parts,), jnp.float32, least / len(pieces), largest / len(pieces)))
        level = level * jnp.repeat(draws, extent[axis_at] // parts).reshape([-1 if axis == axis_at else 1 for axis in range(len(extent))])
    return level


def centred(key, shape, width, limit, pieces=(), kind=jnp.bfloat16):
    result = jax.random.normal(key, shape, jnp.float32) * width
    if len(pieces) > 0:
        result = shard_levels(key, shape, pieces, -0.22, 0.18) * result
    return jnp.clip(result, min=-limit, max=limit).astype(kind)


def setup_inputs(seed: int = 0) -> dict:
    streams_of = jax.random.split(jax.random.key(seed), 29)
    token_ids = draw_token_ids(jax.random.fold_in(streams_of[28], 71), 0)
    row_lengths = draw_row_lengths(jax.random.fold_in(streams_of[28], 71), 0)
    prompt_lengths = with_ends(jax.random.randint(streams_of[2], (B,), L // 16, L // 4), jax.random.fold_in(streams_of[2], 1), L // 16, (L // 4) - 1).astype(jnp.int32)
    picks = draw_picks(jax.random.fold_in(streams_of[28], 71), 0)
    old_logp = jnp.clip(-18.0 + 8.0 * jax.random.uniform(streams_of[4], (B, N_SEQ * PICK), jnp.float32) ** shard_levels(streams_of[4], (B, N_SEQ * PICK), ((0, 4), (1, 8)), -0.2, 0.2), -18.0, -10.0)
    ref_logp = jnp.clip(-18.0 + 8.0 * jax.random.uniform(streams_of[5], (B, N_SEQ * PICK), jnp.float32) ** shard_levels(streams_of[5], (B, N_SEQ * PICK), ((0, 4), (1, 8)), -0.2, 0.2), -18.0, -10.0)
    rewards = centred(streams_of[6], (B,), 1.0, 4.0, (), jnp.float32)
    embed = draw_embed(jax.random.fold_in(streams_of[28], 71), 0)
    embed_m = centred(streams_of[8], (V, D), (0.0028 * PARAMS ** -0.5), 3.337860107421875e-06, ((0, 32),), jnp.float32)
    embed_v = jnp.clip(jnp.exp(math.log(1.7213078835551232e-12) - 2.7573213 * jax.random.uniform(streams_of[9], (V, D), jnp.float32) ** shard_levels(streams_of[9], (V, D), ((0, 32),), -0.2, 0.2)), 1.092368451011301e-13, 1.7213078835551232e-12)
    w_qkv = centred(streams_of[10], (D, QKV), D ** -0.5, 0.1875, ((0, 8),), jnp.float32)
    w_qkv_m = centred(streams_of[11], (D, QKV), (0.0055 * PARAMS ** -0.5), 6.67572021484375e-06, ((0, 8),), jnp.float32)
    w_qkv_v = jnp.clip(jnp.exp(math.log(6.951435520957672e-12) - 2.7668907 * jax.random.uniform(streams_of[12], (D, QKV), jnp.float32) ** shard_levels(streams_of[12], (D, QKV), ((0, 8),), -0.2, 0.2)), 4.369473804045204e-13, 6.951435520957672e-12)
    w_out = centred(streams_of[13], (D, D), (D // 16) ** -0.5, 0.75, ((0, 8),), jnp.float32)
    w_out_m = centred(streams_of[14], (D, D), (0.0055 * PARAMS ** -0.5), 6.67572021484375e-06, ((0, 8),), jnp.float32)
    w_out_v = jnp.clip(jnp.exp(math.log(6.951435520957672e-12) - 2.7668907 * jax.random.uniform(streams_of[15], (D, D), jnp.float32) ** shard_levels(streams_of[15], (D, D), ((0, 8),), -0.2, 0.2)), 4.369473804045204e-13, 6.951435520957672e-12)
    w_gateup = centred(streams_of[16], (D, 2 * FF), D ** -0.5, 0.1875, ((0, 8),), jnp.float32)
    w_gateup_m = centred(streams_of[17], (D, 2 * FF), (0.0055 * PARAMS ** -0.5), 6.67572021484375e-06, ((0, 8),), jnp.float32)
    w_gateup_v = jnp.clip(jnp.exp(math.log(6.951435520957672e-12) - 2.7668907 * jax.random.uniform(streams_of[18], (D, 2 * FF), jnp.float32) ** shard_levels(streams_of[18], (D, 2 * FF), ((0, 8),), -0.2, 0.2)), 4.369473804045204e-13, 6.951435520957672e-12)
    w_down = centred(streams_of[19], (FF, D), FF ** -0.5, 0.078125, ((0, 8),), jnp.float32)
    w_down_m = centred(streams_of[20], (FF, D), (0.0055 * PARAMS ** -0.5), 6.67572021484375e-06, ((0, 8),), jnp.float32)
    w_down_v = jnp.clip(jnp.exp(math.log(6.951435520957672e-12) - 2.7668907 * jax.random.uniform(streams_of[21], (FF, D), jnp.float32) ** shard_levels(streams_of[21], (FF, D), ((0, 8),), -0.2, 0.2)), 4.369473804045204e-13, 6.951435520957672e-12)
    gains = draw_gains(jax.random.fold_in(streams_of[28], 71), 0)
    gains_m = centred(streams_of[23], (3, D), (0.055 * PARAMS ** -0.5), 6.103515625e-05, (), jnp.float32)
    gains_v = jnp.clip(jnp.exp(jax.random.uniform(streams_of[24], (3, D), jnp.float32, math.log(4.369473879939356e-11), math.log(6.951435538304906e-10))), 4.369473879939356e-11, 6.951435538304906e-10)
    bias = centred(streams_of[25], (QKV,), 0.5, 3.0, (), jnp.float32)
    bias_m = centred(streams_of[26], (QKV,), (0.0275 * PARAMS ** -0.5), 3.0517578125e-05, (), jnp.float32)
    bias_v = jnp.clip(jnp.exp(jax.random.uniform(streams_of[27], (QKV,), jnp.float32, math.log(1.092368469984839e-11), math.log(1.7213078185029929e-10))), 1.092368469984839e-11, 1.7213078185029929e-10)
    return {"token_ids": token_ids, "row_lengths": row_lengths, "prompt_lengths": prompt_lengths, "picks": picks, "old_logp": old_logp, "ref_logp": ref_logp, "rewards": rewards, "embed": embed, "embed_m": embed_m, "embed_v": embed_v, "w_qkv": w_qkv, "w_qkv_m": w_qkv_m, "w_qkv_v": w_qkv_v, "w_out": w_out, "w_out_m": w_out_m, "w_out_v": w_out_v, "w_gateup": w_gateup, "w_gateup_m": w_gateup_m, "w_gateup_v": w_gateup_v, "w_down": w_down, "w_down_m": w_down_m, "w_down_v": w_down_v, "gains": gains, "gains_m": gains_m, "gains_v": gains_v, "bias": bias, "bias_m": bias_m, "bias_v": bias_v}


NORM_EPS = 1e-06
ROPE_BASE = 1000000.0
NEG_BIG = -1e+30
EPS_LOW = 0.8
EPS_HIGH = 0.28
BETA_KL = 0.1
CLIP_NORM = 0.05
BETA_ONE = 0.9
BETA_TWO = 0.95
ADAM_EPS = 1e-08
DECAY = 0.1
LR_MATRIX = 0.02
LR_OUT = 0.12
LR_GAIN = 1.0
LR_BIAS = 0.5
HIGH = lax.Precision.HIGHEST

@jax.custom_vjp
def low(v):
    return lax.optimization_barrier(v.astype(jnp.bfloat16)).astype(jnp.float32)

@jax.custom_vjp
def low_back(v):
    return v

def low_keep(v):
    return (low(v), None)

def low_pass(kept, grad):
    return (grad,)

def back_keep(v):
    return (v, None)

def back_low(kept, grad):
    return (low(grad),)
low.defvjp(low_keep, low_pass)
low_back.defvjp(back_keep, back_low)

def norm_rows(values, gain):
    return values * lax.rsqrt(lax.optimization_barrier(jnp.mean(values * values, axis=-1, keepdims=True)) + NORM_EPS) * gain

def rotate(values, places, sign):
    half_width = values.shape[-1] // 2
    frequency = ROPE_BASE ** (-2.0 * jnp.arange(half_width, dtype=jnp.float32) / values.shape[-1])
    angles = places.astype(jnp.float32)[:, None] * frequency[None, :]
    cosine = jnp.cos(angles)[:, None, :]
    sine_part = sign * jnp.sin(angles)[:, None, :]
    front = values[..., :half_width]
    back_half = values[..., half_width:]
    return jnp.concatenate([front * cosine - back_half * sine_part, back_half * cosine + front * sine_part], axis=-1)

def matmul(left, right):
    return jnp.dot(left, right, precision=HIGH)

def layer(stream_zero, low_weights, params, places):
    length = stream_zero.shape[0]
    normed_one = low(norm_rows(stream_zero, params['gains'][0]))
    mixed_qkv = low_back(matmul(normed_one, low_weights['w_qkv']) + params['bias'])
    queries = low(rotate(mixed_qkv[:, :H * HD].reshape(length, H, HD), places, 1.0)).reshape(length, KV, H // KV, HD)
    keys = low(rotate(mixed_qkv[:, H * HD:(H + KV) * HD].reshape(length, KV, HD), places, 1.0))
    values = low(mixed_qkv[:, (H + KV) * HD:].reshape(length, KV, HD))
    span = min(512, length)

    def query_block(block_index):
        offset = block_index * span
        query_piece = lax.dynamic_slice_in_dim(queries, offset, span, 0)
        raw = jnp.einsum('cgrd,kgd->cgrk', query_piece, keys, precision=HIGH) * HD ** (-0.5)
        allowed = jnp.arange(length, dtype=jnp.int32)[None, :] <= (offset + jnp.arange(span, dtype=jnp.int32))[:, None]
        scores = low_back(jnp.where(allowed[:, None, None, :], raw, NEG_BIG))
        chance = low(jax.nn.softmax(scores, axis=-1))
        return jnp.einsum('cgrk,kgd->cgrd', chance, values, precision=HIGH)
    attended = lax.map(jax.checkpoint(query_block), jnp.arange(length // span, dtype=jnp.int32))
    attended = low(low_back(attended.reshape(length, H * HD)))
    stream_one = stream_zero + low_back(matmul(attended, low_weights['w_out']))
    normed_two = low(norm_rows(stream_one, params['gains'][1]))
    gate_up = low_back(matmul(normed_two, low_weights['w_gateup']))
    hidden = low(jax.nn.silu(gate_up[:, :FF]) * gate_up[:, FF:])
    return stream_one + low_back(matmul(hidden, low_weights['w_down']))

def forward(params, token_ids, chosen):
    table = low(params['embed'])
    low_weights = {}
    for weight_name in ('w_qkv', 'w_out', 'w_gateup', 'w_down'):
        low_weights[weight_name] = low(params[weight_name])
    places = jnp.arange(L, dtype=jnp.int32)

    def one_row(carry, row_input):
        row_tokens, row_chosen = row_input
        stream = layer(jnp.take(table, row_tokens, axis=0), low_weights, params, places)
        finals = low(norm_rows(jnp.take(stream, row_chosen, axis=0), params['gains'][2]))
        return (carry, finals)
    carry, finals = lax.scan(jax.checkpoint(one_row), jnp.zeros((), jnp.float32), (token_ids, chosen))
    finals = finals.reshape(-1, D)
    targets = jnp.take_along_axis(token_ids, chosen + 1, axis=1).reshape(-1)
    span = min(512, finals.shape[0])

    def head_block(block_input):
        row_set, wanted = block_input
        logits = low_back(jnp.dot(row_set, table.T, precision=HIGH))
        return jnp.take_along_axis(jax.nn.log_softmax(logits, axis=-1), wanted[:, None], axis=1)[:, 0]
    logp = lax.map(jax.checkpoint(head_block), (finals.reshape(-1, span, D), targets.reshape(-1, span)))
    return logp.reshape(-1)

def adam(weight, moment, second, gradient, learn_rate, decay_rate):
    moment = BETA_ONE * moment + (1.0 - BETA_ONE) * gradient
    second = BETA_TWO * second + (1.0 - BETA_TWO) * gradient * gradient
    corrected = moment / (1.0 - BETA_ONE ** STEP)
    scaled = second / (1.0 - BETA_TWO ** STEP)
    return (weight - learn_rate * (corrected / (jnp.sqrt(scaled) + ADAM_EPS) + decay_rate * weight), moment, second)

def reference(token_ids, row_lengths, prompt_lengths, picks, old_logp, ref_logp, rewards, embed, embed_m, embed_v, w_qkv, w_qkv_m, w_qkv_v, w_out, w_out_m, w_out_v, w_gateup, w_gateup_m, w_gateup_v, w_down, w_down_m, w_down_v, gains, gains_m, gains_v, bias, bias_m, bias_v):
    params = {'embed': embed, 'w_qkv': w_qkv, 'w_out': w_out, 'w_gateup': w_gateup, 'w_down': w_down, 'gains': gains, 'bias': bias}
    chosen = (picks.reshape(B, N_SEQ, PICK) + (jnp.arange(N_SEQ, dtype=jnp.int32) * CH)[None, :, None]).reshape(B, N_SEQ * PICK)
    logp, pull_back = jax.vjp(lambda inner: forward(inner, token_ids, chosen), params)
    live_mask = ((chosen >= prompt_lengths[:, None]) & (chosen + 1 < row_lengths[:, None])).astype(jnp.float32).reshape(-1)
    advantage = jnp.repeat(rewards - jnp.mean(rewards), N_SEQ * PICK)
    old_flat = old_logp.reshape(-1)
    ref_flat = ref_logp.reshape(-1)
    clip_weight = jnp.clip(jnp.exp(logp - old_flat), 1.0 - EPS_LOW, 1.0 + EPS_HIGH)
    token_count = jnp.maximum(jnp.sum(live_mask), 1.0)

    def token_loss(values):
        return live_mask * (-clip_weight * advantage * values + 0.5 * BETA_KL * (values - ref_flat) ** 2)
    loss_sum = jnp.sum(token_loss(logp))
    cotangent = jax.grad(lambda values: jnp.sum(token_loss(values)) / token_count)(logp)
    grads, = pull_back(cotangent)
    squares = jnp.zeros((), jnp.float32)
    for weight_name in ('embed', 'w_qkv', 'w_out', 'w_gateup', 'w_down', 'gains', 'bias'):
        squares = squares + jnp.sum(grads[weight_name] * grads[weight_name])
    grad_norm = jnp.sqrt(squares)
    factor = jnp.minimum(1.0, CLIP_NORM / (grad_norm + 1e-06))
    embed_new = adam(embed, embed_m, embed_v, grads['embed'] * factor, LR_MATRIX, DECAY)
    qkv_new = adam(w_qkv, w_qkv_m, w_qkv_v, grads['w_qkv'] * factor, LR_MATRIX, DECAY)
    out_new = adam(w_out, w_out_m, w_out_v, grads['w_out'] * factor, LR_OUT, DECAY)
    gateup_new = adam(w_gateup, w_gateup_m, w_gateup_v, grads['w_gateup'] * factor, LR_MATRIX, DECAY)
    down_new = adam(w_down, w_down_m, w_down_v, grads['w_down'] * factor, LR_MATRIX, DECAY)
    gains_new = adam(gains, gains_m, gains_v, grads['gains'] * factor, LR_GAIN, 0.0)
    bias_new = adam(bias, bias_m, bias_v, grads['bias'] * factor, LR_BIAS, 0.0)
    return (loss_sum, token_count, grad_norm, embed_new[0], embed_new[1], embed_new[2], qkv_new[0], qkv_new[1], qkv_new[2], out_new[0], out_new[1], out_new[2], gateup_new[0], gateup_new[1], gateup_new[2], down_new[0], down_new[1], down_new[2], gains_new[0], gains_new[1], gains_new[2], bias_new[0], bias_new[1], bias_new[2])
```

```python
import jax
import jax.numpy as jnp
from jax import lax
from jax.sharding import PartitionSpec as P

H = 14
KV = 2
HD = 64
FF = 4864
STEP = 5


NORM_EPS = 1e-06
ROPE_BASE = 1000000.0
NEG_BIG = -1e30
EPS_LOW = 0.8
EPS_HIGH = 0.28
BETA_KL = 0.1
CLIP_NORM = 0.05
BETA_ONE = 0.9
BETA_TWO = 0.95
ADAM_EPS = 1e-08
DECAY = 0.1
LR_MATRIX = 0.02
LR_OUT = 0.12
LR_GAIN = 1.0
LR_BIAS = 0.5


def norm_rows(values, gain):
    return values * lax.rsqrt(jnp.mean(values * values, axis=-1, keepdims=True) + NORM_EPS) * gain


def rotate(values, places, sign):
    half_width = values.shape[-1] // 2
    frequency = ROPE_BASE ** (-2.0 * jnp.arange(half_width, dtype=jnp.float32) / values.shape[-1])
    angles = places.astype(jnp.float32)[:, None] * frequency[None, :]
    cosine = jnp.cos(angles)[:, None, :]
    sine_part = sign * jnp.sin(angles)[:, None, :]
    front = values[..., :half_width]
    back_half = values[..., half_width:]
    return jnp.concatenate(
        [front * cosine - back_half * sine_part, back_half * cosine + front * sine_part], axis=-1
    )


def bit_groups(size, spans):
    stages, low = [], 0
    bits = size.bit_length() - 1
    for span in spans:
        span = min(span, bits - low)
        if span > 0:
            stages.append([mask << low for mask in range(1, 1 << span)])
            low += span
    while low < bits:
        span = min(2, bits - low)
        stages.append([mask << low for mask in range(1, 1 << span)])
        low += span
    return stages


def partner(value, axis, mask):
    size = lax.axis_size(axis)
    return lax.ppermute(value, axis, [(place, place ^ mask) for place in range(size)])


def spread(value, stages):
    held = value[None]
    for axis, masks in stages:
        held = jnp.concatenate([held] + [partner(held, axis, mask) for mask in masks])
    return held


def collect(blocks, stages):
    held = blocks
    for axis, masks in reversed(stages):
        count = len(masks) + 1
        held = held.reshape((count, held.shape[0] // count) + held.shape[1:])
        total = held[0].astype(jnp.float32)
        for place, mask in enumerate(masks):
            total = total + partner(held[place + 1], axis, mask).astype(jnp.float32)
        held = total.astype(jnp.bfloat16)
    return held[0]


def offsets_of(stages):
    offsets = [0]
    for _, masks in stages:
        offsets = offsets + [offset ^ mask for mask in masks for offset in offsets]
    return offsets


def exchange(value, axes):
    return lax.all_to_all(value, axes, split_axis=0, concat_axis=0, tiled=True)


def exchange_copies(value, axes):
    size = lax.axis_size(axes)
    return exchange(jnp.broadcast_to(value[None], (size,) + value.shape), axes)


def halve(value, axis, mask):
    own = (lax.axis_index(axis) & mask) != 0
    keep = jnp.where(own, value[1], value[0])
    send = jnp.where(own, value[0], value[1])
    return (
        keep.astype(jnp.float32) + partner(send, axis, mask).astype(jnp.float32)
    ).astype(jnp.bfloat16)


def double(value, axis, mask):
    own = (lax.axis_index(axis) & mask) != 0
    other = partner(value, axis, mask)
    return jnp.stack([jnp.where(own, other, value), jnp.where(own, value, other)])


def batch_scatter(value):
    size = lax.axis_size("batch")
    masks = []
    mask = 1
    while mask < size:
        masks.append(mask)
        mask *= 2
    held = value.reshape((2,) * len(masks) + (value.shape[0] // size,) + value.shape[1:])
    for depth, mask in enumerate(masks):
        held = halve(jnp.moveaxis(held, len(masks) - 1 - depth, 0), "batch", mask)
    return held


def batch_gather(value):
    size = lax.axis_size("batch")
    held = value
    mask = size // 2
    depth = 0
    while mask:
        held = double(held, "batch", mask)
        held = jnp.moveaxis(held, 0, depth)
        depth += 1
        mask //= 2
    return held.reshape((value.shape[0] * size,) + value.shape[1:])


def one_hot(places, size, dtype):
    return (places[:, None] == jnp.arange(size, dtype=jnp.int32)[None, :]).astype(dtype)


def place_rows(picker, values):
    return lax.dot_general(
        picker,
        values,
        (((0,), (0,)), ((), ())),
        precision=lax.Precision.HIGHEST,
        preferred_element_type=jnp.float32,
    )


def take_rows(picker, values):
    return jnp.dot(picker, values, preferred_element_type=jnp.float32)


def dot_tn(left, right):
    return lax.dot_general(
        left, right, (((0,), (0,)), ((), ())), preferred_element_type=jnp.float32
    )


def dot_nt(left, right):
    return lax.dot_general(
        left, right, (((1,), (1,)), ((), ())), preferred_element_type=jnp.float32
    )


def adam(weight, moment, second, gradient, learn_rate, decay_rate):
    moment = BETA_ONE * moment + (1.0 - BETA_ONE) * gradient
    second = BETA_TWO * second + (1.0 - BETA_TWO) * gradient * gradient
    corrected = moment / (1.0 - BETA_ONE**STEP)
    scaled = second / (1.0 - BETA_TWO**STEP)
    return (
        weight - learn_rate * (corrected / (jnp.sqrt(scaled) + ADAM_EPS) + decay_rate * weight),
        moment,
        second,
    )


def per_device(
    token_ids,
    row_lengths,
    prompt_lengths,
    picks,
    old_logp,
    ref_logp,
    rewards,
    embed,
    embed_m,
    embed_v,
    w_qkv,
    w_qkv_m,
    w_qkv_v,
    w_out,
    w_out_m,
    w_out_v,
    w_gateup,
    w_gateup_m,
    w_gateup_v,
    w_down,
    w_down_m,
    w_down_v,
    gains,
    gains_m,
    gains_v,
    bias,
    bias_m,
    bias_v,
):
    both = ("batch", "seq")
    owners = lax.axis_size(both)
    owner_index = lax.axis_index(both)
    seq_index = lax.axis_index("seq")
    row_index = lax.axis_index("batch")
    batch_count = lax.axis_size("batch")
    seq_count = lax.axis_size("seq")
    core_mask = 1
    low = jnp.bfloat16
    f32 = jnp.float32
    token_list = token_ids[0]
    local_len = token_list.shape[0]
    vrows, width = embed.shape
    shard = w_qkv.shape[0]
    ff_part = FF // seq_count
    capacity = max(2, 2 * local_len // owners)
    seq_stages = [("seq", masks) for masks in reversed(bit_groups(seq_count, (1, 2)))]
    batch_stages = [("batch", masks) for masks in reversed(bit_groups(batch_count, (1, 1)))]
    all_stages = seq_stages + batch_stages

    local_picks = picks[0]
    n_picks = local_picks.shape[0]
    pick_places = seq_index * local_len + local_picks
    live_mask = (
        (pick_places >= prompt_lengths[row_index]) & (pick_places + 1 < row_lengths[row_index])
    ).astype(f32)
    live_here = jnp.sum(live_mask).astype(jnp.int32)

    owner_of = token_list // vrows
    order = jnp.arange(local_len, dtype=jnp.int32)
    slot_of = jnp.sum(
        ((owner_of[:, None] == owner_of[None, :]) & (order[None, :] < order[:, None])).astype(
            jnp.int32
        ),
        axis=1,
    )
    place_of = owner_of * capacity + slot_of
    request_grid = jnp.arange(owners * capacity, dtype=jnp.int32)
    requests = jnp.sum(
        jnp.where(
            request_grid[:, None] == place_of[None, :],
            (token_list - owner_of * vrows)[None, :],
            0,
        ),
        axis=1,
    )
    message = jnp.concatenate(
        [
            requests.reshape(owners, capacity),
            jnp.broadcast_to(live_here[None, None], (owners, 1)),
        ],
        axis=1,
    )
    received = exchange(message, both)
    wanted = received[:, :capacity].reshape(-1)
    token_count = jnp.maximum(jnp.sum(received[:, capacity]).astype(f32), 1.0)
    found = jnp.take(embed, wanted, axis=0).astype(low).reshape(owners, capacity, width)
    returned = exchange(found, both).reshape(owners * capacity, width)
    placer = one_hot(place_of, owners * capacity, low)
    x_zero = take_rows(placer, returned).astype(low)
    stream_zero = x_zero.astype(f32)

    w_kv_low = w_qkv[:, H * HD :].astype(low)
    w_q_low = w_qkv[:, : H * HD].astype(low)
    w_out_low = w_out.astype(low)
    w_kv_full = lax.all_gather(w_kv_low, "seq", axis=0, tiled=True)
    w_q_full = lax.all_gather(w_q_low, "seq", axis=0, tiled=True)
    w_out_full = lax.all_gather(w_out_low, "seq", axis=0, tiled=True)
    half = shard // 2
    core = lax.axis_index("batch") & core_mask
    my_half = lax.dynamic_slice_in_dim(w_gateup, core * half, half, 0).astype(low)
    pieces = jnp.transpose(my_half.reshape(half, 2, seq_count, ff_part), (2, 0, 1, 3)).reshape(
        seq_count, half, 2 * ff_part
    )
    half_cols = exchange(pieces, "seq")
    w_gu = jnp.moveaxis(double(half_cols, "batch", core_mask), 0, 1).reshape(width, 2 * ff_part)
    w_down_low = w_down.astype(low)

    places = seq_index * local_len + order
    normed_one = norm_rows(stream_zero, gains[0]).astype(low)
    kv = jnp.dot(normed_one, w_kv_full, preferred_element_type=f32) + bias[H * HD :]
    keys = rotate(kv[:, : KV * HD].reshape(local_len, KV, HD), places, 1.0).reshape(
        local_len, KV * HD
    )
    kv_low = jnp.concatenate([keys, kv[:, KV * HD :]], axis=1).astype(low)
    kv_all = spread(kv_low, seq_stages).reshape(seq_count * local_len, 2 * KV * HD)
    key_places = (
        (seq_index ^ jnp.array(offsets_of(seq_stages), jnp.int32))[:, None] * local_len
        + order[None, :]
    ).reshape(-1)
    picker = one_hot(local_picks, local_len, low)
    targeter = one_hot(local_picks + 1, local_len, low)
    picked_zero = take_rows(picker, x_zero)
    target_rows = take_rows(targeter, x_zero)
    normed_picked = take_rows(picker, normed_one).astype(low)
    queries = jnp.dot(normed_picked, w_q_full, preferred_element_type=f32) + bias[: H * HD]
    queries = rotate(queries.reshape(n_picks, H, HD), pick_places, 1.0).astype(low)
    group = H // KV
    grouped = jnp.transpose(queries.reshape(n_picks, KV, group, HD), (1, 0, 2, 3)).reshape(
        KV, n_picks * group, HD
    )
    length = kv_all.shape[0]
    keys3 = jnp.transpose(kv_all[:, : KV * HD].reshape(length, KV, HD), (1, 0, 2))
    values3 = jnp.transpose(kv_all[:, KV * HD :].reshape(length, KV, HD), (1, 0, 2))
    scores = jnp.einsum("gqd,gkd->gqk", grouped, keys3, preferred_element_type=f32) * HD ** (-0.5)
    allowed = key_places[None, :] <= jnp.repeat(pick_places, group)[:, None]
    scores = jnp.where(allowed[None], scores, NEG_BIG)
    top = jnp.max(scores, axis=-1, keepdims=True)
    raised = jnp.exp(scores - top)
    chance = raised / jnp.sum(raised, axis=-1, keepdims=True)
    chance_low = chance.astype(low)
    attended = jnp.einsum("gqk,gkd->gqd", chance_low, values3, preferred_element_type=f32)
    mixed = (
        jnp.transpose(attended.reshape(KV, n_picks, group, HD), (1, 0, 2, 3))
        .reshape(n_picks, H * HD)
        .astype(low)
    )
    stream_one = picked_zero + jnp.dot(mixed, w_out_full, preferred_element_type=f32)

    normed_two = norm_rows(stream_one, gains[1]).astype(low)
    normed_two_all = spread(normed_two, seq_stages).reshape(seq_count * n_picks, width)
    gate_up = jnp.dot(normed_two_all, w_gu, preferred_element_type=f32)
    gate_part = gate_up[:, :ff_part]
    up_part = gate_up[:, ff_part:]
    hidden = (jax.nn.silu(gate_part) * up_part).astype(low)
    down_part = jnp.dot(hidden, w_down_low, preferred_element_type=f32).astype(low)
    stream_two = stream_one + collect(
        down_part.reshape(seq_count, n_picks, width), seq_stages
    ).astype(f32)

    final = norm_rows(stream_two, gains[2]).astype(low)
    all_final = spread(final, all_stages).reshape(owners * n_picks, width)
    table = embed.astype(low)
    logits = dot_nt(all_final, table)
    local_high = jnp.max(logits, axis=1, keepdims=True)
    raised_head = jnp.exp(logits - local_high)
    local_sum = jnp.sum(raised_head, axis=1, keepdims=True)
    raised_low = raised_head.astype(low)
    mean_row = jnp.dot(raised_low, table, preferred_element_type=f32) / local_sum
    held_row = mean_row.astype(low).reshape(owners, n_picks, width)
    held_log = (local_high + jnp.log(local_sum)).reshape(owners, n_picks, 1)
    for axis, masks in reversed(all_stages):
        count = len(masks) + 1
        rows = held_row.reshape((count, held_row.shape[0] // count) + held_row.shape[1:])
        logs = held_log.reshape((count, held_log.shape[0] // count) + held_log.shape[1:])
        others_rows = [rows[0]] + [
            partner(rows[at + 1], axis, mask) for at, mask in enumerate(masks)
        ]
        others_logs = [logs[0]] + [
            partner(logs[at + 1], axis, mask) for at, mask in enumerate(masks)
        ]
        highest = others_logs[0]
        for other in others_logs[1:]:
            highest = jnp.maximum(highest, other)
        shares = [jnp.exp(other - highest) for other in others_logs]
        summed = sum(shares[1:], shares[0])
        mixed_rows = sum(
            (
                share * other.astype(f32)
                for share, other in zip(shares[1:], others_rows[1:])
            ),
            shares[0] * others_rows[0].astype(f32),
        )
        held_row = (mixed_rows / summed).astype(low)
        held_log = highest + jnp.log(summed)
    mean_rows = held_row[0].astype(f32)
    log_total = held_log[0][:, 0]
    target_logit = jnp.sum(final.astype(f32) * target_rows, axis=1)
    logp = target_logit - log_total
    advantage = rewards[row_index] - jnp.mean(rewards)
    clip_weight = jnp.clip(jnp.exp(logp - old_logp[0]), 1.0 - EPS_LOW, 1.0 + EPS_HIGH)
    loss_here = jnp.sum(
        live_mask
        * (-clip_weight * advantage * logp + 0.5 * BETA_KL * (logp - ref_logp[0]) ** 2)
    )
    coefficient = (
        live_mask * (-clip_weight * advantage + BETA_KL * (logp - ref_logp[0])) / token_count
    )
    grad_final = coefficient[:, None] * (target_rows - mean_rows)
    pair = spread(jnp.stack([coefficient, log_total], axis=1), all_stages).reshape(
        owners * n_picks, 2
    )
    scaled_final = (
        all_final.astype(f32) * (-pair[:, :1] * jnp.exp(local_high - pair[:, 1:]))
    ).astype(low)
    grad_head = dot_tn(raised_low, scaled_final)

    unused, pull_final = jax.vjp(norm_rows, stream_two, gains[2])
    grad_two, grad_gain_two = pull_final(grad_final)
    branch_all = spread(grad_two.astype(low), seq_stages).reshape(seq_count * n_picks, width)
    grad_hidden = dot_nt(branch_all, w_down_low)
    grad_down = dot_tn(hidden, branch_all).astype(low)
    sigmoid_gate = jax.nn.sigmoid(gate_part)
    grad_gate = grad_hidden * up_part * sigmoid_gate * (1.0 + gate_part * (1.0 - sigmoid_gate))
    grad_up = grad_hidden * gate_part * sigmoid_gate
    grad_gu = jnp.concatenate([grad_gate, grad_up], axis=1).astype(low)
    grad_normed_two = collect(
        dot_nt(grad_gu, w_gu).astype(low).reshape(seq_count, n_picks, width), seq_stages
    ).astype(f32)
    grad_gu_w = dot_tn(normed_two_all, grad_gu).astype(low)
    unused, pull_two = jax.vjp(norm_rows, stream_one, gains[1])
    part_one, grad_gain_one = pull_two(grad_normed_two)
    grad_one = grad_two + part_one
    mixed_grad = grad_one.astype(low)
    grad_mixed = dot_nt(mixed_grad, w_out_full).astype(low)
    grad_grouped = jnp.transpose(
        grad_mixed.reshape(n_picks, KV, group, HD), (1, 0, 2, 3)
    ).reshape(KV, n_picks * group, HD)
    inner = jnp.sum(grad_grouped.astype(f32) * attended, axis=-1, keepdims=True)
    grad_chance = jnp.einsum("gqd,gkd->gqk", grad_grouped, values3, preferred_element_type=f32)
    grad_scores = (chance * (grad_chance - inner)).astype(low)
    grad_query = jnp.einsum(
        "gqk,gkd->gqd", grad_scores, keys3, preferred_element_type=f32
    ) * HD ** (-0.5)
    grad_keys = jnp.einsum(
        "gqk,gqd->kgd", grad_scores, grouped, preferred_element_type=f32
    ) * HD ** (-0.5)
    grad_values = jnp.einsum("gqk,gqd->kgd", chance_low, grad_grouped, preferred_element_type=f32)
    grad_kv = jnp.concatenate(
        [grad_keys.reshape(length, KV * HD), grad_values.reshape(length, KV * HD)], axis=1
    ).astype(low)
    own_kv = collect(grad_kv.reshape(seq_count, local_len, 2 * KV * HD), seq_stages).astype(f32)
    query_pre = jnp.transpose(grad_query.reshape(KV, n_picks, group, HD), (1, 0, 2, 3))
    query_pre = (
        rotate(query_pre.reshape(n_picks, H, HD), pick_places, -1.0)
        .reshape(n_picks, H * HD)
        .astype(low)
    )
    key_pre = rotate(own_kv[:, : KV * HD].reshape(local_len, KV, HD), places, -1.0)
    kv_pre = jnp.concatenate(
        [key_pre.reshape(local_len, KV * HD), own_kv[:, KV * HD :]], axis=1
    ).astype(low)
    grad_bias = jnp.concatenate(
        [jnp.sum(query_pre.astype(f32), axis=0), jnp.sum(kv_pre.astype(f32), axis=0)]
    )
    picker_f32 = picker.astype(f32)
    grad_normed_one = dot_nt(kv_pre, w_kv_full) + place_rows(
        picker_f32, dot_nt(query_pre, w_q_full)
    )
    unused, pull_one = jax.vjp(norm_rows, stream_zero, gains[0])
    part_zero, grad_gain_zero = pull_one(grad_normed_one)
    grad_zero = part_zero + place_rows(
        jnp.concatenate([picker_f32, targeter.astype(f32)], axis=0),
        jnp.concatenate([grad_one, coefficient[:, None] * final.astype(f32)], axis=0),
    )
    sendback = dot_tn(placer, grad_zero.astype(low)).astype(low)
    arrived = exchange(sendback.reshape(owners, capacity, width), both).reshape(-1, width)
    grad_embed = grad_head.at[wanted].add(arrived.astype(f32))

    def columns_out(value):
        rows = value.shape[0]
        cut = jnp.transpose(value.reshape(rows, seq_count, shard), (1, 0, 2))
        return exchange(cut, "seq").reshape(seq_count * rows, shard)

    def rows_out(value):
        return exchange_copies(value, "seq").reshape(seq_count * value.shape[0], -1)

    grad_q_w = dot_tn(columns_out(normed_picked), rows_out(query_pre))
    grad_out_w = dot_tn(columns_out(mixed), rows_out(mixed_grad))
    grad_kv_w = jnp.sum(
        exchange(
            dot_tn(normed_one, kv_pre).astype(low).reshape(seq_count, shard, 2 * KV * HD), "seq"
        ).astype(f32),
        axis=0,
    )
    small = jnp.concatenate([grad_q_w, grad_kv_w, grad_out_w], axis=1).astype(low)
    small = batch_gather(batch_scatter(small)).astype(f32)
    gu_quarter = batch_scatter(grad_gu_w)
    gu_rows = width // batch_count
    gu_cut = gu_quarter
    grad_gu_all = batch_gather(gu_cut).reshape(seq_count, shard, 2 * ff_part)
    gu_shard = exchange(grad_gu_all, "seq")
    gu_shard = jnp.transpose(
        gu_shard.reshape(seq_count, shard, 2, ff_part), (1, 2, 0, 3)
    ).reshape(shard, 2 * FF)
    shards = (
        small[:, : (H + 2 * KV) * HD],
        small[:, (H + 2 * KV) * HD :],
        gu_shard.astype(f32),
        batch_gather(batch_scatter(grad_down)).astype(f32),
    )
    shard_squares = (
        jnp.sum(shards[0] * shards[0])
        + jnp.sum(shards[1] * shards[1])
        + jnp.sum(shards[2] * shards[2])
        + jnp.sum(shards[3] * shards[3])
    )
    local_squares = jnp.sum(grad_embed * grad_embed) + shard_squares / batch_count
    summary = jnp.concatenate(
        [
            jnp.stack([local_squares, loss_here]),
            grad_gain_zero,
            grad_gain_one,
            grad_gain_two,
            grad_bias,
        ]
    )
    summary = jnp.sum(exchange_copies(summary, both), axis=0)
    squares, loss_sum = summary[0], summary[1]
    grad_gains = summary[2 : 2 + 3 * width].reshape(3, width)
    grad_bias_all = summary[2 + 3 * width :]
    grad_norm = jnp.sqrt(
        squares + jnp.sum(grad_gains * grad_gains) + jnp.sum(grad_bias_all * grad_bias_all)
    )
    factor = jnp.minimum(1.0, CLIP_NORM / (grad_norm + 1e-06))
    embed_new = adam(embed, embed_m, embed_v, grad_embed * factor, LR_MATRIX, DECAY)
    qkv_new = adam(w_qkv, w_qkv_m, w_qkv_v, shards[0] * factor, LR_MATRIX, DECAY)
    out_new = adam(w_out, w_out_m, w_out_v, shards[1] * factor, LR_OUT, DECAY)
    gateup_new = adam(w_gateup, w_gateup_m, w_gateup_v, shards[2] * factor, LR_MATRIX, DECAY)
    down_new = adam(w_down, w_down_m, w_down_v, shards[3] * factor, LR_MATRIX, DECAY)
    gains_new = adam(gains, gains_m, gains_v, grad_gains * factor, LR_GAIN, 0.0)
    bias_new = adam(bias, bias_m, bias_v, grad_bias_all * factor, LR_BIAS, 0.0)
    return (
        loss_sum,
        token_count,
        grad_norm,
        *embed_new,
        *qkv_new,
        *out_new,
        *gateup_new,
        *down_new,
        *gains_new,
        *bias_new,
    )


def solution(mesh):
    in_specs = (
        P("batch", "seq"),
        P(),
        P(),
        P("batch", "seq"),
        P("batch", "seq"),
        P("batch", "seq"),
        P(),
        P(("batch", "seq"), None),
        P(("batch", "seq"), None),
        P(("batch", "seq"), None),
        P("seq", None),
        P("seq", None),
        P("seq", None),
        P("seq", None),
        P("seq", None),
        P("seq", None),
        P("seq", None),
        P("seq", None),
        P("seq", None),
        P("seq", None),
        P("seq", None),
        P("seq", None),
        P(),
        P(),
        P(),
        P(),
        P(),
        P(),
    )
    out_specs = (
        P(),
        P(),
        P(),
        P(("batch", "seq"), None),
        P(("batch", "seq"), None),
        P(("batch", "seq"), None),
        P("seq", None),
        P("seq", None),
        P("seq", None),
        P("seq", None),
        P("seq", None),
        P("seq", None),
        P("seq", None),
        P("seq", None),
        P("seq", None),
        P("seq", None),
        P("seq", None),
        P("seq", None),
        P(),
        P(),
        P(),
        P(),
        P(),
        P(),
    )
    return jax.shard_map(
        per_device, mesh=mesh, in_specs=in_specs, out_specs=out_specs, check_vma=False
    )
```

```python
import functools

import jax
import jax.numpy as jnp
from jax import lax
from jax.experimental import pallas as pl
from jax.experimental.pallas import tpu as pltpu
from jax.sharding import PartitionSpec as P

H = 14
KV = 2
HD = 64
FF = 4864
STEP = 5


NORM_EPS = 1e-06
ROPE_BASE = 1000000.0
NEG_BIG = -1e30
EPS_LOW = 0.8
EPS_HIGH = 0.28
BETA_KL = 0.1
CLIP_NORM = 0.05
BETA_ONE = 0.9
BETA_TWO = 0.95
ADAM_EPS = 1e-08
DECAY = 0.1
LR_MATRIX = 0.02
LR_OUT = 0.12
LR_GAIN = 1.0
LR_BIAS = 0.5


def norm_rows(values, gain):
    return values * lax.rsqrt(jnp.mean(values * values, axis=-1, keepdims=True) + NORM_EPS) * gain


def partner(value, axis, mask):
    size = lax.axis_size(axis)
    return lax.ppermute(value, axis, [(place, place ^ mask) for place in range(size)])


def masks_of(size):
    masks, mask = [], 1
    while mask < size:
        masks.append(mask)
        mask *= 2
    return masks


def bit_of(axis, mask):
    return (lax.axis_index(axis) & mask) != 0


def xor_order(blocks, axis):
    bits = masks_of(blocks.shape[0])
    held = blocks.reshape((2,) * len(bits) + blocks.shape[1:])
    for at, bit in enumerate(reversed(bits)):
        held = jnp.where(bit_of(axis, bit), jnp.flip(held, at), held)
    return held.reshape(blocks.shape)


def after(value, *first):
    return lax.optimization_barrier((value, first))[0]


def together(*values):
    return lax.optimization_barrier(values)


def seq_stages_of(size):
    bits = masks_of(size)
    stages, rest = [], bits[1:]
    while rest:
        pair, rest = rest[:2], rest[2:]
        stages.append([pair[0], pair[1], pair[0] ^ pair[1]] if len(pair) == 2 else pair)
    return stages + [bits[:1]]


def spread(value, axis, stages):
    held = value[None]
    for masks in stages:
        held = jnp.concatenate([held] + [partner(held, axis, mask) for mask in masks])
    return held


def to_xor_order(blocks, axis, stages):
    bits = masks_of(blocks.shape[0])
    turned = xor_order(blocks, axis).reshape((2,) * len(bits) + blocks.shape[1:])
    place = {bit: at for at, bit in enumerate(reversed(bits))}
    order = [place[mask] for masks in reversed(stages) for mask in reversed(masks) if mask in bits]
    rest = list(range(len(bits), turned.ndim))
    return jnp.transpose(turned, order + rest).reshape(blocks.shape)


def to_index_order(blocks, axis, stages):
    bits = masks_of(blocks.shape[0])
    place = {bit: at for at, bit in enumerate(reversed(bits))}
    order = [place[mask] for masks in reversed(stages) for mask in reversed(masks) if mask in bits]
    back = [order.index(at) for at in range(len(bits))]
    held = blocks.reshape((2,) * len(bits) + blocks.shape[1:])
    held = jnp.transpose(held, back + list(range(len(bits), held.ndim)))
    return xor_order(held.reshape(blocks.shape), axis)


def exchange(value, axes):
    return lax.all_to_all(value, axes, split_axis=0, concat_axis=0, tiled=True)


def exchange_copies(value, axes):
    size = lax.axis_size(axes)
    return exchange(jnp.broadcast_to(value[None], (size,) + value.shape), axes)


def total_of(parts):
    total = parts[0].astype(jnp.float32)
    for part in parts[1:]:
        total = total + part.astype(jnp.float32)
    return total.astype(jnp.bfloat16)


def cut(first, second, axis, mask):
    own = bit_of(axis, mask)
    return jnp.where(own, second, first), partner(jnp.where(own, first, second), axis, mask)


def halve(first, second, axis, mask):
    return total_of(cut(first, second, axis, mask))


def double(value, axis, mask):
    own = bit_of(axis, mask)
    other = partner(value, axis, mask)
    return jnp.where(own, other, value), jnp.where(own, value, other)


def all_sum(value):
    for axis in ("batch", "seq"):
        for mask in masks_of(lax.axis_size(axis)):
            value = value + partner(value, axis, mask)
    return value


def sum_seq(blocks):
    held = blocks
    for mask in reversed(masks_of(blocks.shape[0])):
        half = held.shape[0] // 2
        held = halve(held[:half], held[half:], "seq", mask)
    return held[0]


def dot_nn(left, right):
    return jnp.dot(left, right, preferred_element_type=jnp.float32)


def dot_tn(left, right):
    return lax.dot_general(
        left, right, (((0,), (0,)), ((), ())), preferred_element_type=jnp.float32
    )


def dot_nt(left, right):
    return lax.dot_general(
        left, right, (((1,), (1,)), ((), ())), preferred_element_type=jnp.float32
    )


def squares_of(value):
    value = value.astype(jnp.float32)
    return jnp.sum(value * value)


def adam(weight, moment, second, gradient, learn_rate, decay_rate):
    moment = BETA_ONE * moment + (1.0 - BETA_ONE) * gradient
    second = BETA_TWO * second + (1.0 - BETA_TWO) * gradient * gradient
    corrected = moment / (1.0 - BETA_ONE**STEP)
    scaled = second / (1.0 - BETA_TWO**STEP)
    return (
        weight - learn_rate * (corrected / (jnp.sqrt(scaled) + ADAM_EPS) + decay_rate * weight),
        moment,
        second,
    )


LOW = jnp.bfloat16
F32 = jnp.float32
LANES = 128


def iota(shape, dim):
    return lax.broadcasted_iota(jnp.int32, shape, dim)


def in_hbm(*arrays):
    return tuple(pltpu.with_memory_space_constraint(array, pltpu.HBM) for array in arrays)


def like(shape, dtype=jnp.float32):
    return jax.ShapeDtypeStruct(shape, dtype)


def in_vmem(body, outs, args, name, flops=0, exps=0, limit=16, kept=(), scratch=()):
    moved = sum(a.size * a.dtype.itemsize for a in args) + sum(
        o.size * o.dtype.itemsize for o in outs
    )
    whole = lambda rank: lambda step: (0,) * rank
    near = pl.BlockSpec(memory_space=pltpu.VMEM)
    return pl.pallas_call(
        body,
        grid=(1,),
        in_specs=[
            pl.BlockSpec(a.shape, whole(a.ndim)) if at in kept else near
            for at, a in enumerate(args)
        ],
        out_specs=[near] * len(outs),
        out_shape=outs,
        scratch_shapes=scratch,
        compiler_params=pltpu.CompilerParams(vmem_limit_bytes=limit * 2**20),
        cost_estimate=pl.CostEstimate(flops=flops, bytes_accessed=moved, transcendentals=exps),
        name=name,
    )(*[in_hbm(a)[0] if at in kept else a for at, a in enumerate(args)])


def upright(row):
    count = row.shape[1]
    square = jnp.broadcast_to(row.astype(F32), (count, count))
    return jnp.sum(
        jnp.where(iota((count, count), 0) == iota((count, count), 1), square, 0.0),
        axis=1,
        keepdims=True,
    )


def turned(values, cosine, sine):
    tiles = []
    for at in range(0, values.shape[1], LANES):
        tile = values[:, at : at + LANES]
        front = iota(tile.shape, 1) % HD < HD // 2
        swapped = jnp.where(
            front, pltpu.roll(tile, LANES - HD // 2, 1), pltpu.roll(tile, HD // 2, 1)
        )
        tiles.append(tile * cosine + swapped * sine)
    return tiles[0] if len(tiles) == 1 else jnp.concatenate(tiles, axis=1)


def norm_back(values, gain, grad):
    inverse = lax.rsqrt(jnp.mean(values * values, axis=-1, keepdims=True) + NORM_EPS)
    scaled = grad * gain
    inner = jnp.mean(values * scaled, axis=-1, keepdims=True)
    into = inverse * scaled - values * (inverse * inverse * inverse * inner)
    return into, jnp.sum(grad * values * inverse, axis=0, keepdims=True)


def placed(pick_columns, values):
    high = values.astype(LOW)
    rest = (values - high.astype(F32)).astype(LOW)
    return dot_nn(pick_columns, high) + dot_nn(pick_columns, rest)


def coded(value):
    high = value.astype(LOW).astype(F32)
    middle = (value - high).astype(LOW).astype(F32)
    return high, middle, (value - high - middle).astype(LOW).astype(F32)


def coded_lanes(columns):
    parts = [part for column in columns for part in coded(column)]
    lane = iota((columns[0].shape[0], LANES), 1)
    tail = jnp.zeros(lane.shape, F32)
    for at, part in enumerate(parts):
        tail = jnp.where(lane == at, part, tail)
    return tail.astype(LOW)


def decoded(tail, at):
    tail = tail.astype(F32)
    lane = iota(tail.shape, tail.ndim - 1)
    return jnp.sum(
        jnp.where((lane >= 3 * at) & (lane < 3 * at + 3), tail, 0.0), axis=-1, keepdims=True
    )


def request_body(vrows, capacity, tokens_ref, requests_ref, placer_ref):
    row = tokens_ref[...].astype(F32)
    column = upright(tokens_ref[...])
    count = row.shape[1]
    owner_row = jnp.floor((row + 0.5) / vrows)
    owner = jnp.floor((column + 0.5) / vrows)
    earlier = (owner == owner_row) & (iota((count, count), 1) < iota((count, count), 0))
    slot = jnp.sum(jnp.where(earlier, 1.0, 0.0), axis=1, keepdims=True)
    hit = (owner * capacity + slot) == iota(placer_ref.shape, 1).astype(F32)
    placer_ref[...] = jnp.where(hit, 1.0, 0.0).astype(LOW)
    requests_ref[...] = jnp.sum(
        jnp.where(hit, column - owner * vrows, 0.0), axis=0, keepdims=True
    ).astype(jnp.int32)


def embed_body(
    rows_ref, placer_ref, w_ref, bias_ref, gain_ref, cos_ref, sin_ref, x_ref, normed_ref, kv_ref
):
    x_zero = dot_nn(placer_ref[...], rows_ref[...])
    x_ref[...] = x_zero.astype(LOW)
    normed = norm_rows(x_zero, gain_ref[...]).astype(LOW)
    normed_ref[...] = normed
    kv = dot_nn(normed, w_ref[...]) + bias_ref[...]
    width = KV * HD
    keys = turned(kv[:, :width], cos_ref[...], sin_ref[...]).astype(LOW)
    values = kv[:, width:].astype(LOW)
    for at in range(kv_ref.shape[0]):
        kv_ref[at, :, :width] = keys
        kv_ref[at, :, width:] = values


def pick_columns_of(picks, slots, shift):
    return jnp.where(
        iota((slots, picks.shape[1]), 0) == picks + shift, 1.0, 0.0
    ).astype(LOW)


def pick_body(
    x_ref, normed_ref, picks_ref, w_ref, bias_ref, cos_ref, sin_ref,
    picked_ref, target_ref, picked_normed_ref, query_ref,
):
    slots = x_ref.shape[0]
    here = pick_columns_of(picks_ref[...], slots, 0)
    after = pick_columns_of(picks_ref[...], slots, 1)
    picked_ref[...] = dot_tn(here, x_ref[...])
    target_ref[...] = dot_tn(after, x_ref[...])
    normed = dot_tn(here, normed_ref[...]).astype(LOW)
    picked_normed_ref[...] = normed
    query = dot_nn(normed, w_ref[...]) + bias_ref[...]
    query_ref[...] = turned(query, cos_ref[...], sin_ref[...]).astype(LOW)


def stacked_heads(values, first, count):
    return jnp.concatenate(
        [values[:, (first + at) * HD : (first + at + 1) * HD] for at in range(count)], axis=0
    )


CHUNK = 2048


def scores_of(queries, keys, places, count, start):
    scores = dot_nt(queries, keys) * HD ** (-0.5)
    reach = jnp.concatenate([places] * count, axis=0) - start
    return jnp.where(iota(scores.shape, 1) <= reach, scores, NEG_BIG)


def key_slices(kv_ref, head, start, size):
    rows = pl.ds(start, size)
    return (
        kv_ref[rows, head * HD : (head + 1) * HD],
        kv_ref[rows, (KV + head) * HD : (KV + head + 1) * HD],
    )


def over_keys(length, body, carry):
    if length <= CHUNK:
        return body(0, carry)
    return lax.fori_loop(
        0, length // CHUNK, lambda at, held: body(pl.multiple_of(at * CHUNK, CHUNK), held), carry
    )


def softmax_parts(queries, kv_ref, head, places, count):
    length = kv_ref.shape[0]
    size = min(length, CHUNK)
    if length <= CHUNK:

        def chances(start):
            scores = scores_of(queries, key_slices(kv_ref, head, 0, size)[0], places, count, 0)
            raised = jnp.exp(scores - jnp.max(scores, axis=1, keepdims=True))
            return raised * (1.0 / jnp.sum(raised, axis=1, keepdims=True))

        return chances

    def statistics(start, held):
        top, summed = held
        keys = key_slices(kv_ref, head, start, size)[0]
        scores = scores_of(queries, keys, places, count, start)
        now = jnp.maximum(top, jnp.max(scores, axis=1, keepdims=True))
        raised = jnp.exp(scores - now)
        return now, summed * jnp.exp(top - now) + jnp.sum(raised, axis=1, keepdims=True)

    rows = queries.shape[0]
    top, summed = over_keys(
        length, statistics, (jnp.full((rows, 1), NEG_BIG, F32), jnp.zeros((rows, 1), F32))
    )

    def chances_at(start):
        keys = key_slices(kv_ref, head, start, size)[0]
        return jnp.exp(scores_of(queries, keys, places, count, start) - top) * (1.0 / summed)

    return chances_at


def attend_body(
    query_ref, kv_ref, place_ref, w_ref, picked_ref, gain_ref,
    mixed_ref, attended_ref, one_ref, normed_ref,
):
    places = upright(place_ref[...]).astype(jnp.int32)
    picks = places.shape[0]
    group = H // KV
    length = kv_ref.shape[0]
    size = min(length, CHUNK)
    for head in range(KV):
        queries = stacked_heads(query_ref[...], head * group, group)
        chances = softmax_parts(queries, kv_ref, head, places, group)

        def add(start, total):
            values = key_slices(kv_ref, head, start, size)[1]
            return total + dot_nn(chances(start).astype(LOW), values)

        out = over_keys(length, add, jnp.zeros(queries.shape, F32))
        for at in range(group):
            spot = (head * group + at) * HD
            attended_ref[:, spot : spot + HD] = out[at * picks : (at + 1) * picks]
    mixed = attended_ref[...].astype(LOW)
    mixed_ref[...] = mixed
    one = picked_ref[...] + dot_nn(mixed, w_ref[...])
    one_ref[...] = one
    normed = norm_rows(one, gain_ref[...]).astype(LOW)
    for at in range(normed_ref.shape[0]):
        normed_ref[at] = normed


def feed_body(normed_ref, gate_w_ref, up_w_ref, down_w_ref, gate_ref, up_ref, hidden_ref, out_ref):
    normed = normed_ref[...]
    gate = dot_nn(normed, gate_w_ref[...])
    up = dot_nn(normed, up_w_ref[...])
    gate_ref[...] = gate
    up_ref[...] = up
    hidden = (gate * (1.0 / (1.0 + jnp.exp(-gate))) * up).astype(LOW)
    hidden_ref[...] = hidden
    out_ref[...] = dot_nn(hidden, down_w_ref[...]).astype(LOW)


def feed_sum_body(parts_ref, one_ref, gain_ref, two_ref, final_ref):
    two = one_ref[...] + jnp.sum(parts_ref[...].astype(F32), axis=0)
    two_ref[...] = two
    final_ref[...] = norm_rows(two, gain_ref[...]).astype(LOW)


def head_body(
    vrows, rows_ref, other_ref, table_ref, raised_ref, tops_ref, own_ref, send_ref, top, summed, total
):
    step = pl.program_id(0)
    block = table_ref.shape[0]
    width = table_ref.shape[1]
    half = own_ref.shape[0]

    @pl.when(step == 0)
    def _():
        top[...] = jnp.full(top.shape, NEG_BIG, F32)
        summed[...] = jnp.zeros(summed.shape, F32)
        total[...] = jnp.zeros(total.shape, F32)

    left = vrows - step * block
    entries = jnp.where(iota((block, 1), 0) < left, table_ref[...], 0.0).astype(LOW)
    inside = iota((1, block), 1) < left
    part = min(256, half)
    pieces = []
    for ref, start in ((rows_ref, 0), (other_ref, half)):
        tokens = ref[...].reshape(half, width)
        pieces += [
            (slice(start + at, start + at + part), tokens[at : at + part])
            for at in range(0, half, part)
        ]
    logits_of = [dot_nt(tokens, entries) for _, tokens in pieces]
    for (piece, _), logits in zip(pieces, logits_of):
        logits = jnp.where(inside, logits, NEG_BIG)
        before = top[piece, :1]
        now = jnp.maximum(before, jnp.max(logits, axis=1, keepdims=True))
        raised = jnp.exp(logits - now)
        shrink = jnp.exp(before - now)
        low = raised.astype(LOW)
        raised_ref[piece] = low
        summed[piece] = summed[piece] * shrink + jnp.sum(raised, axis=1, keepdims=True)
        total[piece] = total[piece] * shrink + dot_nn(low, entries)
        top[piece] = jnp.broadcast_to(now, (part, LANES))
        column = iota((part, LANES), 1) == step
        tops_ref[piece] = jnp.where(column, now, tops_ref[piece])

    @pl.when(step == pl.num_programs(0) - 1)
    def _():
        for ref, at in ((own_ref, 0), (send_ref, half)):
            here = slice(at, at + half)
            ref[:, :width] = (total[here] / summed[here, :1]).astype(LOW)
            ref[:, width:] = coded_lanes([top[here, :1] + jnp.log(summed[here, :1])])


def head_part(rows, other, group, table, block):
    seqs, _, picks, width = rows.shape
    half = seqs * picks
    vrows = table.shape[0]
    steps = -(-vrows // block)
    whole = lambda step: (0, 0)
    states = pl.BlockSpec((seqs, 1, picks, width), lambda step: (0, group, 0, 0))
    mean = pl.BlockSpec((half, width + LANES), whole)
    return pl.pallas_call(
        functools.partial(head_body, vrows),
        grid=(steps,),
        in_specs=[states, states, pl.BlockSpec((block, width), lambda step: (step, 0))],
        out_specs=[
            pl.BlockSpec((2 * half, block), lambda step: (0, step)),
            pl.BlockSpec((2 * half, LANES), whole),
            mean,
            mean,
        ],
        out_shape=[
            pltpu.HBM((2 * half, steps * block), LOW),
            like((2 * half, LANES)),
            like((half, width + LANES), LOW),
            like((half, width + LANES), LOW),
        ],
        scratch_shapes=[
            pltpu.VMEM((2 * half, LANES), F32),
            pltpu.VMEM((2 * half, LANES), F32),
            pltpu.VMEM((2 * half, width), F32),
        ],
        compiler_params=pltpu.CompilerParams(vmem_limit_bytes=(28 if half <= 256 else 60) * 2**20),
        cost_estimate=pl.CostEstimate(
            flops=8 * half * vrows * width,
            bytes_accessed=vrows * width * 4 + half * vrows * 4,
            transcendentals=2 * half * vrows,
        ),
        name="head_part",
    )(rows, other, *in_hbm(table))


def merge_values(parts):
    highest = parts[0][1]
    for _, log in parts[1:]:
        highest = jnp.maximum(highest, log)
    summed, total = 0.0, 0.0
    for mean, log in parts:
        share = jnp.exp(log - highest)
        summed = summed + share
        total = total + share * mean
    return total * (1.0 / summed), highest + jnp.log(summed)


def merge_body(*refs):
    out_ref = refs[-1]
    width = out_ref.shape[1] - LANES
    mean, log = merge_values(
        [(ref[:, :width].astype(F32), decoded(ref[:, width:], 0)) for ref in refs[:-1]]
    )
    out_ref[:, :width] = mean.astype(LOW)
    out_ref[:, width:] = coded_lanes([log])


def loss_body(
    parts_ref, final_ref, target_ref, two_ref, gain_ref, live_ref, old_ref, ref_ref, advantage_ref,
    message_ref, grad_ref, gain_grad_ref, added_ref, loss_ref,
):
    width = final_ref.shape[1]
    mean, log_total = merge_values(
        [
            (parts_ref[at, :, :width].astype(F32), decoded(parts_ref[at, :, width:], 0))
            for at in range(parts_ref.shape[0])
        ]
    )
    final = final_ref[...].astype(F32)
    target = target_ref[...]
    live = upright(live_ref[...])
    to_ref = jnp.sum(final * target, axis=1, keepdims=True) - log_total
    logp = to_ref
    to_ref = logp - upright(ref_ref[...])
    advantage = advantage_ref[...]
    weight = jnp.clip(jnp.exp(logp - upright(old_ref[...])), 1.0 - EPS_LOW, 1.0 + EPS_HIGH)
    coefficient = live * (-weight * advantage + BETA_KL * to_ref)
    loss = live * (-weight * advantage * logp + 0.5 * BETA_KL * to_ref * to_ref)
    loss_ref[...] = jnp.broadcast_to(jnp.sum(loss, axis=0, keepdims=True), loss_ref.shape)
    added_ref[...] = coefficient * final
    grad, gain_grad_ref[...] = norm_back(
        two_ref[...], gain_ref[...], coefficient * (target - mean)
    )
    grad_ref[...] = grad
    low = grad.astype(LOW)
    tail = coded_lanes([log_total, coefficient])
    for at in range(message_ref.shape[0]):
        message_ref[at, :, :width] = low
        message_ref[at, :, width:] = tail


def feed_back_body(
    message_ref, hidden_ref, gate_ref, up_ref, gate_w_ref, up_w_ref, down_w_ref,
    grad_gate_ref, grad_up_ref, out_ref,
):
    width = out_ref.shape[1]
    grad_hidden = dot_nt(message_ref[:, :width], down_w_ref[...])
    gate = gate_ref[...]
    up = up_ref[...]
    sigmoid = 1.0 / (1.0 + jnp.exp(-gate))
    grad_gate = (grad_hidden * up * sigmoid * (1.0 + gate * (1.0 - sigmoid))).astype(LOW)
    grad_up = (grad_hidden * gate * sigmoid).astype(LOW)
    grad_gate_ref[...] = grad_gate
    grad_up_ref[...] = grad_up
    out_ref[...] = (
        dot_nt(grad_gate, gate_w_ref[...]) + dot_nt(grad_up, up_w_ref[...])
    ).astype(LOW)


def one_back_body(parts_ref, one_ref, grad_two_ref, gain_ref, grad_ref, low_ref, gain_grad_ref):
    into, gain_grad_ref[...] = norm_back(
        one_ref[...], gain_ref[...], jnp.sum(parts_ref[...].astype(F32), axis=0)
    )
    grad = grad_two_ref[...] + into
    grad_ref[...] = grad
    low_ref[...] = grad.astype(LOW)


def attend_back_body(
    grad_ref, w_ref, query_ref, kv_ref, place_ref, attended_ref, cos_ref, sin_ref,
    kv_grad_ref, query_pre_ref, bias_ref, query_grad,
):
    places = upright(place_ref[...]).astype(jnp.int32)
    picks = places.shape[0]
    into = dot_nt(grad_ref[...], w_ref[...]).astype(LOW)
    group = H // KV
    length = kv_ref.shape[0]
    size = min(length, CHUNK)
    for head in range(KV):
        queries = stacked_heads(query_ref[...], head * group, group)
        grads = stacked_heads(into, head * group, group)
        inner = jnp.sum(
            grads.astype(F32) * stacked_heads(attended_ref[...], head * group, group),
            axis=1,
            keepdims=True,
        )
        chances = softmax_parts(queries, kv_ref, head, places, group)

        def add(start, total):
            keys, values = key_slices(kv_ref, head, start, size)
            chance = chances(start)
            scores = (chance * (dot_nt(grads, values) - inner)).astype(LOW)
            rows = pl.ds(start, size)
            kv_grad_ref[rows, head * HD : (head + 1) * HD] = (
                dot_tn(scores, queries) * HD ** (-0.5)
            ).astype(LOW)
            kv_grad_ref[rows, (KV + head) * HD : (KV + head + 1) * HD] = dot_tn(
                chance.astype(LOW), grads
            ).astype(LOW)
            return total + dot_nn(scores, keys) * HD ** (-0.5)

        query_part = over_keys(length, add, jnp.zeros(queries.shape, F32))
        for at in range(group):
            spot = (head * group + at) * HD
            query_grad[:, spot : spot + HD] = query_part[at * picks : (at + 1) * picks]
    query_pre = turned(query_grad[...], cos_ref[...], -sin_ref[...]).astype(LOW)
    query_pre_ref[...] = query_pre
    bias_ref[...] = jnp.sum(query_pre.astype(F32), axis=0, keepdims=True)


def zero_back_body(
    parts_ref, cos_ref, sin_ref, kv_w_ref, query_pre_ref, q_w_ref, picks_ref, x_ref, gain_ref,
    grad_one_ref, added_ref, placer_ref,
    kv_pre_ref, back_ref, gain_grad_ref, bias_ref,
):
    width = KV * HD
    slots = x_ref.shape[0]
    own = jnp.sum(parts_ref[...].astype(F32), axis=0)
    kv_pre_ref[:, :width] = turned(own[:, :width], cos_ref[...], -sin_ref[...]).astype(LOW)
    kv_pre_ref[:, width:] = own[:, width:].astype(LOW)
    kv_pre = kv_pre_ref[...]
    bias_ref[...] = jnp.sum(kv_pre.astype(F32), axis=0, keepdims=True)
    here = pick_columns_of(picks_ref[...], slots, 0)
    after = pick_columns_of(picks_ref[...], slots, 1)
    grad_normed = dot_nt(kv_pre, kv_w_ref[...]) + placed(
        here, dot_nt(query_pre_ref[...], q_w_ref[...])
    )
    into, gain_grad_ref[...] = norm_back(x_ref[...].astype(F32), gain_ref[...], grad_normed)
    grad = into + placed(here, grad_one_ref[...]) + placed(after, added_ref[...])
    back_ref[...] = dot_tn(placer_ref[...], grad.astype(LOW)).astype(LOW)


def layer_grads_body(
    core_ref, normed_ref, gate_ref, up_ref, hidden_ref, message_ref,
    own_ref, send_ref, own_down_ref, send_down_ref,
):
    second = core_ref[0] > 0
    gate, up = gate_ref[...], up_ref[...]
    normed = normed_ref[...]
    own_ref[...] = dot_tn(normed, jnp.where(second, up, gate)).astype(LOW)
    send_ref[...] = dot_tn(normed, jnp.where(second, gate, up)).astype(LOW)
    half = own_down_ref.shape[0]
    grads = message_ref[:, : own_down_ref.shape[1]]
    front, back = hidden_ref[:, :half], hidden_ref[:, half : 2 * half]
    own_down_ref[...] = dot_tn(jnp.where(second, back, front), grads).astype(LOW)
    send_down_ref[...] = dot_tn(jnp.where(second, front, back), grads).astype(LOW)


def summary_body(arrived_ref, rows_ref, names_ref, out_ref):
    arrived = arrived_ref[...]
    names = names_ref[...].astype(F32)
    cross = jnp.sum(arrived.astype(F32) * rows_ref[...].astype(F32), axis=0, keepdims=True)
    same = jnp.where(upright(names_ref[...]) == names, dot_nt(arrived, arrived), 0.0)
    out_ref[...] = 2.0 * jnp.sum(cross, axis=1, keepdims=True) + jnp.sum(
        jnp.sum(same, axis=0, keepdims=True), axis=1, keepdims=True
    )


def head_grad_body(
    span, first, far_ref, near_ref, far_tops_ref, near_tops_ref, rows_ref, other_ref, tails_ref, tails_other_ref,
    grad_ref, squares_ref,
):
    step = pl.program_id(0)
    block = step + first
    width = grad_ref.shape[1]
    half = far_ref.shape[0] // 2
    grad = 0.0
    for group, raised_ref, tops_ref in ((1, far_ref, far_tops_ref), (0, near_ref, near_tops_ref)):
        for at, (states_ref, tail_ref) in enumerate(
            ((rows_ref, tails_ref), (other_ref, tails_other_ref))
        ):
            here = slice(at * half, (at + 1) * half)
            tops = tops_ref[here]
            top = jnp.sum(
                jnp.where(iota(tops.shape, 1) == block // span, tops, 0.0), axis=1, keepdims=True
            )
            tail = tail_ref[group]
            scale = -decoded(tail, 1) * jnp.exp(top - decoded(tail, 0))
            states = states_ref[:, group].reshape(half, width).astype(F32)
            grad = grad + dot_tn(raised_ref[here], (states * scale).astype(LOW))
    grad_ref[...] = grad.astype(LOW)

    @pl.when(step == 0)
    def _():
        squares_ref[...] = jnp.zeros(squares_ref.shape, F32)

    squares_ref[...] += jnp.sum(grad * grad, axis=0, keepdims=True)


def head_grad(far, near, rows, other, tails, tails_other, vrows, block, span, first, steps, held):
    width = rows.shape[-1]
    tokens = far[0].shape[0]
    whole = lambda count: lambda step: (0,) * count
    raised = pl.BlockSpec((tokens, block), lambda step: (0, step + first))
    fixed = lambda array: pl.BlockSpec(array.shape, whole(array.ndim))
    return pl.pallas_call(
        lambda *refs: head_grad_body(span, first, *refs[:8], *refs[-2:]),
        grid=(steps,),
        in_specs=[
            raised,
            raised,
            fixed(far[1]),
            fixed(near[1]),
            fixed(rows),
            fixed(other),
            fixed(tails),
            fixed(tails_other),
        ]
        + [pl.BlockSpec(memory_space=pl.ANY)] * len(held),
        out_specs=[
            pl.BlockSpec((block, width), lambda step: (step + first, 0)),
            pl.BlockSpec((8, width), whole(2)),
        ],
        out_shape=[pltpu.HBM((vrows, width), LOW), like((8, width))],
        input_output_aliases={8 + at: at for at in range(len(held))},
        compiler_params=pltpu.CompilerParams(vmem_limit_bytes=(28 if tokens <= 512 else 60) * 2**20),
        cost_estimate=pl.CostEstimate(
            flops=4 * tokens * steps * block * width,
            bytes_accessed=steps * block * (4 * tokens + 2 * width),
            transcendentals=0,
        ),
        name="head_grad",
    )(*in_hbm(far[0], near[0], far[1], near[1], rows, other, tails, tails_other), *held)


def table_adam_body(first, scale_ref, names_ref, added_ref, grad_ref, w_ref, m_ref, v_ref, *refs):
    w_out, m_out, v_out = refs[-3:]
    rows = grad_ref.shape[0]
    here = iota((rows, names_ref.shape[1]), 0) + (pl.program_id(0) + first) * rows
    picker = jnp.where(here == names_ref[...], 1.0, 0.0).astype(LOW)
    grad = grad_ref[...].astype(F32) + dot_nn(picker, added_ref[...])
    w_out[...], m_out[...], v_out[...] = adam(
        w_ref[...], m_ref[...], v_ref[...], grad * scale_ref[0], LR_MATRIX, DECAY
    )


def table_adam(scale, names, added, grad, weight, moment, second, rows, first, steps, held):
    vrows, width = weight.shape
    whole = lambda step: (0, 0)
    here = pl.BlockSpec((rows, width), lambda step: (step + first, 0))
    return pl.pallas_call(
        functools.partial(table_adam_body, first),
        grid=(steps,),
        in_specs=[
            pl.BlockSpec(memory_space=pltpu.SMEM),
            pl.BlockSpec((1, names.shape[1]), whole),
            pl.BlockSpec(added.shape, whole),
            here,
            here,
            here,
            here,
        ]
        + [pl.BlockSpec(memory_space=pl.ANY)] * len(held),
        out_specs=[here, here, here],
        out_shape=[pltpu.HBM((vrows, width), F32)] * 3,
        input_output_aliases={7 + at: at for at in range(len(held))},
        compiler_params=pltpu.CompilerParams(vmem_limit_bytes=44 * 2**20),
        cost_estimate=pl.CostEstimate(
            flops=2 * names.shape[1] * steps * rows * width,
            bytes_accessed=steps * rows * width * 26,
            transcendentals=steps * rows * width,
        ),
        name="table_adam",
    )(scale, names, added, *in_hbm(grad, weight, moment, second), *held)


def per_device(
    token_ids,
    row_lengths,
    prompt_lengths,
    picks,
    old_logp,
    ref_logp,
    rewards,
    embed,
    embed_m,
    embed_v,
    w_qkv,
    w_qkv_m,
    w_qkv_v,
    w_out,
    w_out_m,
    w_out_v,
    w_gateup,
    w_gateup_m,
    w_gateup_v,
    w_down,
    w_down_m,
    w_down_v,
    gains,
    gains_m,
    gains_v,
    bias,
    bias_m,
    bias_v,
):
    both = ("batch", "seq")
    owners = lax.axis_size(both)
    seq_index = lax.axis_index("seq")
    row_index = lax.axis_index("batch")
    batch_count = lax.axis_size("batch")
    seq_count = lax.axis_size("seq")
    core_mask, far_mask = 1, 2
    on_core, on_far = bit_of("batch", core_mask), bit_of("batch", far_mask)
    low = LOW
    f32 = F32
    local_len = token_ids.shape[1]
    vrows, width = embed.shape
    shard = w_qkv.shape[0]
    half = shard // 2
    ff_part = FF // seq_count
    ff_wide = -(-ff_part // LANES) * LANES
    capacity = max(2, 2 * local_len // owners)
    kv_width = KV * HD
    q_width = H * HD
    n_picks = picks.shape[1]
    row_count = seq_count * n_picks

    requests, placer = in_vmem(
        functools.partial(request_body, vrows, capacity),
        [like((1, owners * capacity), jnp.int32), like((local_len, owners * capacity), low)],
        [token_ids],
        "requests",
    )
    sent_requests = exchange(requests.reshape(owners, capacity), both)

    core_row = lax.axis_index("batch") & core_mask
    qkv_cut = -(-(q_width + 2 * kv_width) // (2 * LANES)) * LANES
    out_cut = -(-width // (2 * LANES)) * LANES + LANES

    def part_of(value, columns):
        start = jnp.where(on_core, value.shape[1] - columns, 0)
        return lax.dynamic_slice(value, (jnp.where(on_far, half, 0), start), (half, columns)).astype(low)

    def widened(value):
        return jnp.pad(value, [(0, 0)] * (value.ndim - 1) + [(0, ff_wide - ff_part)])

    proj_parts = lax.all_gather(
        jnp.concatenate([part_of(w_qkv, qkv_cut), part_of(w_out, out_cut)], axis=1), "seq", axis=0
    )
    stages = seq_stages_of(seq_count)
    w_kv_full = spread(w_qkv[:, q_width:].astype(low), "seq", stages)
    pieces = jnp.transpose(part_of(w_gateup, FF).reshape(half, seq_count, ff_part), (1, 0, 2))
    pieces = xor_order(widened(pieces), "seq")
    w_down_low = jnp.pad(w_down.astype(low), ((0, ff_wide - ff_part), (0, 0)))
    sent_requests, pieces, w_down_low, w_kv_full = together(
        sent_requests, pieces, w_down_low, w_kv_full
    )
    w_kv_full = to_index_order(w_kv_full, "seq", stages).reshape(width, 2 * kv_width)

    def far_rows(value):
        return jnp.stack(double(value, "batch", far_mask), axis=1).reshape(width, -1)

    def core_columns(value, whole):
        first, second = double(value, "batch", core_mask)
        return jnp.concatenate([first, second[:, 2 * value.shape[1] - whole :]], axis=1)

    wanted = sent_requests.reshape(-1)
    found = embed.at[wanted].get(mode="promise_in_bounds").astype(low)
    returned = exchange(found.reshape(owners, capacity, width), both)
    pieces = [pieces[0]] + [partner(pieces[at], "seq", at) for at in range(1, seq_count)]
    returned, pieces, proj_parts, w_kv_full = together(returned, pieces, proj_parts, w_kv_full)
    returned = returned.reshape(owners * capacity, width)
    w_q_far = far_rows(proj_parts[..., :qkv_cut])
    w_q_full = core_columns(w_q_far, q_width + 2 * kv_width)[:, :q_width]
    out_short = out_cut - LANES
    out_parts = proj_parts[..., qkv_cut:]
    out_parts = jnp.where(on_core, out_parts[..., LANES:], out_parts[..., :out_short])
    w_out_far = far_rows(out_parts)

    places = seq_index * local_len + jnp.arange(local_len, dtype=jnp.int32)
    pick_places = seq_index * local_len + picks
    row_names = jnp.arange(batch_count, dtype=jnp.int32) == row_index
    prompt_here = jnp.sum(jnp.where(row_names, prompt_lengths, 0))
    length_here = jnp.sum(jnp.where(row_names, row_lengths, 0))
    live = ((pick_places >= prompt_here) & (pick_places + 1 < length_here)).astype(f32)
    advantage = (
        jnp.sum(jnp.where(row_names, rewards, 0.0)) - jnp.mean(rewards)
    ).reshape(1, 1)

    def rope_factors(slots):
        lane = jnp.arange(LANES, dtype=jnp.int32)
        frequency = ROPE_BASE ** (-2.0 * (lane % (HD // 2)).astype(f32) / HD)
        angles = slots.astype(f32)[:, None] * frequency[None, :]
        sign = jnp.where(lane % HD < HD // 2, -1.0, 1.0)
        return jnp.cos(angles), jnp.sin(angles) * sign[None, :]

    slot_cos, slot_sin = rope_factors(places)
    pick_cos, pick_sin = rope_factors(pick_places[0])
    bias_row = bias.reshape(1, -1)

    x_zero, normed_one, kv_low = in_vmem(
        embed_body,
        [like((local_len, width), low), like((local_len, width), low), like((seq_count, local_len, 2 * kv_width), low)],
        [returned, placer, w_kv_full, bias_row[:, q_width:], gains[:1], slot_cos, slot_sin],
        "keys_values",
        flops=2 * local_len * width * (owners * capacity + 2 * kv_width),
    )
    kv_all = exchange(kv_low, "seq")
    w_out_full = core_columns(w_out_far, width)
    gu_columns = xor_order(jnp.stack(pieces), "seq")
    picked_zero, target_rows, normed_picked, queries = in_vmem(
        pick_body,
        [
            like((n_picks, width)),
            like((n_picks, width)),
            like((n_picks, width), low),
            like((n_picks, q_width), low),
        ],
        [x_zero, normed_one, picks, w_q_full, bias_row[:, :q_width], pick_cos, pick_sin],
        "scored_queries",
        flops=2 * n_picks * width * (q_width + 3 * local_len),
    )
    kv_all, picked_zero, target_rows, normed_picked, queries, w_out_full, gu_columns = together(
        kv_all, picked_zero, target_rows, normed_picked, queries, w_out_full, gu_columns
    )
    gu_columns = far_rows(gu_columns)
    kv_all = kv_all.reshape(seq_count * local_len, 2 * kv_width)
    length = kv_all.shape[0]
    limit = 24
    mixed, attended, stream_one, normed_two = in_vmem(
        attend_body,
        [
            like((n_picks, q_width), low),
            like((n_picks, q_width)),
            like((n_picks, width)),
            like((seq_count, n_picks, width), low),
        ],
        [queries, kv_all, pick_places, w_out_full, picked_zero, gains[1:2]],
        "attention",
        flops=4 * n_picks * q_width * length + 2 * n_picks * q_width * width,
        exps=n_picks * H * length,
        limit=limit,
    )


    def shard_columns(value):
        return jnp.transpose(value.reshape(n_picks, seq_count, shard), (1, 0, 2))

    w_gate, w_up = double(gu_columns, "batch", core_mask)
    normed_two_all, w_gate, w_up, column_pieces = together(
        exchange(normed_two, "seq"),
        w_gate,
        w_up,
        jnp.concatenate([shard_columns(normed_picked), shard_columns(mixed)], axis=1),
    )
    normed_two_all = normed_two_all.reshape(row_count, width)
    gate_part, up_part, hidden, down_part = in_vmem(
        feed_body,
        [
            like((row_count, ff_wide)),
            like((row_count, ff_wide)),
            like((row_count, ff_wide), low),
            like((row_count, width), low),
        ],
        [normed_two_all, w_gate, w_up, w_down_low],
        "feed_forward",
        flops=6 * row_count * width * ff_part,
        limit=24,
        kept=(3,),
    )
    stream_two, final = in_vmem(
        feed_sum_body,
        [like((n_picks, width)), like((n_picks, width), low)],
        [exchange(down_part.reshape(seq_count, n_picks, width), "seq"), stream_one, gains[2:]],
        "final_norm",
    )

    near = jnp.stack([final, partner(final, "batch", far_mask)])
    rows = exchange_copies(near, "seq")
    other = partner(rows, "batch", core_mask)
    block = 1024

    gathered_columns = exchange(after(column_pieces, rows), "seq")

    def merge(*parts):
        return in_vmem(merge_body, [like(parts[0].shape, low)], parts, "merge_means")[0]

    far, gathered_columns = together(head_part(rows, other, 1, embed, block), gathered_columns)
    far_mean = merge(far[2], partner(far[3], "batch", core_mask))
    near_part, far_mean = together(
        head_part(after(rows, far_mean), other, 0, embed, block),
        partner(far_mean, "batch", far_mask),
    )
    means = merge(near_part[2], partner(near_part[3], "batch", core_mask), far_mean)
    mean_parts, gathered_columns = together(
        exchange(means.reshape(seq_count, n_picks, width + LANES), "seq"),
        to_xor_order(gathered_columns, "seq", stages),
    )
    message, grad_two, grad_gain_two, added, loss_here = in_vmem(
        loss_body,
        [
            like((seq_count, n_picks, width + LANES), low),
            like((n_picks, width)),
            like((1, width)),
            like((n_picks, width)),
            like((1, LANES)),
        ],
        [
            mean_parts,
            final,
            target_rows,
            stream_two,
            gains[2:],
            live,
            old_logp,
            ref_logp,
            advantage,
        ],
        "loss",
        kept=(2, 3, 4, 5, 6, 7),
    )

    messages = exchange(message, "seq").reshape(row_count, width + LANES)
    grad_gate, grad_up, normed_part = in_vmem(
        feed_back_body,
        [
            like((row_count, ff_wide), low),
            like((row_count, ff_wide), low),
            like((row_count, width), low),
        ],
        [messages, hidden, gate_part, up_part, w_gate, w_up, w_down_low],
        "feed_forward_back",
        flops=6 * row_count * width * ff_part,
        limit=28,
        kept=(1, 2, 3, 4, 5, 6),
    )
    normed_part = exchange(normed_part.reshape(seq_count, n_picks, width), "seq")

    layer_grads = in_vmem(
        layer_grads_body,
        [
            like((width, ff_wide), low),
            like((width, ff_wide), low),
            like((ff_part // 2, width), low),
            like((ff_part // 2, width), low),
        ],
        [
            core_row.reshape(1),
            normed_two_all,
            grad_gate,
            grad_up,
            hidden,
            messages,
        ],
        "layer_grads",
        flops=6 * row_count * width * ff_part,
        limit=24,
        kept=(1, 2, 3, 4, 5),
    )
    tails = messages[:, width:]
    tails = jnp.stack([tails, partner(tails, "batch", far_mask)])
    tails_other = partner(tails, "batch", core_mask)
    head_blocks = -(-vrows // (block // 2))
    head_args = (far, near_part, rows, other, tails, tails_other, vrows, block // 2, 2)
    head_cut = -(-head_blocks * 3 // 10)
    grad_head, head_squares = head_grad(*head_args, 0, head_cut, ())
    normed_part, layer_grads, grad_head, head_squares = together(
        normed_part, layer_grads, grad_head, head_squares
    )
    gu_own, gu_send, down_own, down_send = layer_grads
    gu_other = partner(gu_send, "batch", core_mask)
    down_other = partner(down_send, "batch", core_mask)
    grad_one, grad_one_low, grad_gain_one = in_vmem(
        one_back_body,
        [like((n_picks, width)), like((n_picks, width), low), like((1, width))],
        [
            normed_part,
            stream_one,
            grad_two,
            gains[1:2],
        ],
        "second_norm_back",
        kept=(1, 2, 3),
    )
    kv_grad, query_pre, query_bias = in_vmem(
        attend_back_body,
        [
            like((length, 2 * kv_width), low),
            like((n_picks, q_width), low),
            like((1, q_width)),
        ],
        [grad_one_low, w_out_full, queries, kv_all, pick_places, attended, pick_cos, pick_sin],
        "attention_back",
        flops=10 * n_picks * q_width * length,
        exps=n_picks * H * length,
        limit=limit + 4,
        kept=(1, 2, 3, 4, 5, 6, 7),
        scratch=[pltpu.VMEM((n_picks, q_width), f32)],
    )
    own_parts = exchange(kv_grad.reshape(seq_count, local_len, 2 * kv_width), "seq")

    def far_cut(value):
        return cut(value[..., 0, :, :], value[..., 1, :, :], "batch", far_mask)

    def far_sides(value):
        front, back = value[..., 0, :, :], value[..., 1, :, :]
        return jnp.where(on_far, back, front), jnp.where(on_far, front, back)

    gu_parts = far_sides(total_of([gu_own, gu_other]).reshape(seq_count, 2, half, ff_wide))
    down_parts = far_sides(total_of([down_own, down_other]).reshape(2, -1, width))
    grad_head, more_squares = head_grad(
        *head_args[:2], after(rows, kv_grad), *head_args[3:],
        head_cut, head_blocks - head_cut, (grad_head,),
    )
    late_rows = spread(jnp.concatenate([query_pre, grad_one_low], axis=0), "seq", stages)
    own_parts, gu_parts, down_parts, grad_head, more_squares, late_rows = together(
        own_parts, gu_parts, down_parts, grad_head, more_squares, late_rows
    )
    gu_parts = gu_parts[0], partner(gu_parts[1], "batch", far_mask)
    down_parts = down_parts[0], partner(down_parts[1], "batch", far_mask)
    kv_pre, sendback, grad_gain_zero, kv_bias = in_vmem(
        zero_back_body,
        [
            like((local_len, 2 * kv_width), low),
            like((owners * capacity, width), low),
            like((1, width)),
            like((1, 2 * kv_width)),
        ],
        [
            own_parts,
            slot_cos,
            slot_sin,
            w_kv_full,
            query_pre,
            w_q_full,
            picks,
            x_zero,
            gains[:1],
            grad_one,
            added,
            placer,
        ],
        "first_norm_back",
        kept=(1, 2, 3, 4, 5, 6, 7, 8, 9, 10, 11),
        flops=2 * local_len * width * (2 * kv_width + owners * capacity + 6 * n_picks),
    )
    gu_part, down_part_w = total_of(gu_parts), total_of(down_parts)

    grad_head, sendback = together(grad_head, sendback)
    arrived = exchange(sendback.reshape(owners, capacity, width), both)
    head_rows = grad_head.at[wanted].get(mode="promise_in_bounds")
    q_half = dot_tn(
        gathered_columns[:, :n_picks].reshape(row_count, shard),
        late_rows[:, :n_picks].reshape(row_count, q_width),
    )
    out_half = dot_tn(
        gathered_columns[:, n_picks:].reshape(row_count, shard),
        late_rows[:, n_picks:].reshape(row_count, width),
    )
    proj_part = halve(q_half.astype(low), out_half.astype(low), "batch", core_mask)
    proj_part = total_of(far_cut(proj_part.reshape(2, half, width)))
    kv_w_grad = dot_tn(normed_one, kv_pre).astype(low)
    kv_part = halve(kv_w_grad[:, :kv_width], kv_w_grad[:, kv_width:], "batch", core_mask)
    kv_part = sum_seq(total_of(far_cut(kv_part.reshape(seq_count, 2, half, kv_width))))
    own_squares = (
        squares_of(gu_part)
        + squares_of(down_part_w)
        + squares_of(proj_part)
        + squares_of(kv_part)
        + jnp.sum(head_squares[0])
        + jnp.sum(more_squares[0])
    )
    arrived, head_rows, own_squares, gu_part, down_part_w, proj_part, kv_part = together(
        arrived, head_rows, own_squares, gu_part, down_part_w, proj_part, kv_part
    )
    arrived = arrived.reshape(-1, width)
    row_squares = in_vmem(
        summary_body, [like((1, 1))], [arrived, head_rows, wanted[None]], "row_squares"
    )
    own_squares = own_squares + row_squares[0][0, 0]
    summary = jnp.concatenate(
        [
            grad_gain_zero[0],
            grad_gain_one[0],
            grad_gain_two[0],
            query_bias[0],
            kv_bias[0],
            jnp.stack([own_squares, loss_here[0, 0], jnp.sum(live)]),
            jnp.zeros((LANES - 3,), f32),
        ]
    ).reshape(-1, LANES)
    summary = jnp.sum(exchange_copies(summary, both), axis=0).reshape(-1)
    grad_gains = summary[: 3 * width].reshape(3, width)
    grad_bias_all = summary[3 * width : -LANES]
    squares, loss_sum = summary[-LANES], summary[1 - LANES]
    token_count = jnp.maximum(summary[2 - LANES], 1.0)
    grad_norm = (
        jnp.sqrt(
            squares + jnp.sum(grad_gains * grad_gains) + jnp.sum(grad_bias_all * grad_bias_all)
        )
        / token_count
    )
    factor = jnp.minimum(1.0, CLIP_NORM / (grad_norm + 1e-06)) / token_count

    block = 608
    blocks = -(-vrows // block)
    cuts = [0, -(-blocks * 3 // 8), -(-blocks * 6 // 8), blocks]

    def update_rows(at, held, first):
        return table_adam(
            after(factor.reshape(1), first),
            wanted[None],
            arrived,
            grad_head,
            embed,
            embed_m,
            embed_v,
            block,
            cuts[at],
            cuts[at + 1] - cuts[at],
            held,
        )

    def both_halves(value, axis, mask, at):
        return jnp.concatenate(double(value, axis, mask), axis=at)

    gu_rows = exchange(after(gu_part, factor), "seq")
    gu_rows, embed_new, down_part_w, proj_part, kv_part = together(
        gu_rows, update_rows(0, (), factor), down_part_w, proj_part, kv_part
    )
    gu_rows = jnp.transpose(gu_rows[..., :ff_part], (1, 0, 2)).reshape(half, FF)
    gu_far = both_halves(gu_rows, "batch", far_mask, 0)
    down_all = jnp.stack(double(down_part_w, "batch", far_mask), axis=0)
    small = both_halves(jnp.concatenate([proj_part, kv_part], axis=1), "batch", far_mask, 0)
    gu_far, down_all, small, embed_new = together(
        gu_far, down_all, small, update_rows(1, tuple(embed_new), gu_rows)
    )
    gu_all = both_halves(gu_far, "batch", core_mask, 1)
    down_all = jnp.stack(double(down_all, "batch", core_mask), axis=0).reshape(w_down.shape)
    first_small, second_small = double(small, "batch", core_mask)
    qkv_all = jnp.concatenate(
        [first_small[:, :width], first_small[:, width:], second_small[:, width:]], axis=1
    )
    out_all = second_small[:, :width]
    gu_all, down_all, qkv_all, out_all, embed_new = together(
        gu_all, down_all, qkv_all, out_all, update_rows(2, tuple(embed_new), gu_far)
    )

    def update(weight, moment, second, gradient, rate):
        return adam(weight, moment, second, gradient.astype(f32) * factor, rate, DECAY)

    qkv_new = update(w_qkv, w_qkv_m, w_qkv_v, qkv_all, LR_MATRIX)
    out_new = update(w_out, w_out_m, w_out_v, out_all, LR_OUT)
    gateup_new = update(w_gateup, w_gateup_m, w_gateup_v, gu_all, LR_MATRIX)
    down_new = update(w_down, w_down_m, w_down_v, down_all, LR_MATRIX)
    gains_new = adam(gains, gains_m, gains_v, grad_gains * factor, LR_GAIN, 0.0)
    bias_new = adam(bias, bias_m, bias_v, grad_bias_all * factor, LR_BIAS, 0.0)
    return (
        loss_sum,
        token_count,
        grad_norm,
        *embed_new,
        *qkv_new,
        *out_new,
        *gateup_new,
        *down_new,
        *gains_new,
        *bias_new,
    )


def solution(mesh):
    in_specs = (
        P("batch", "seq"),
        P(),
        P(),
        P("batch", "seq"),
        P("batch", "seq"),
        P("batch", "seq"),
        P(),
        P(("batch", "seq"), None),
        P(("batch", "seq"), None),
        P(("batch", "seq"), None),
        P("seq", None),
        P("seq", None),
        P("seq", None),
        P("seq", None),
        P("seq", None),
        P("seq", None),
        P("seq", None),
        P("seq", None),
        P("seq", None),
        P("seq", None),
        P("seq", None),
        P("seq", None),
        P(),
        P(),
        P(),
        P(),
        P(),
        P(),
    )
    out_specs = (
        P(),
        P(),
        P(),
        P(("batch", "seq"), None),
        P(("batch", "seq"), None),
        P(("batch", "seq"), None),
        P("seq", None),
        P("seq", None),
        P("seq", None),
        P("seq", None),
        P("seq", None),
        P("seq", None),
        P("seq", None),
        P("seq", None),
        P("seq", None),
        P("seq", None),
        P("seq", None),
        P("seq", None),
        P(),
        P(),
        P(),
        P(),
        P(),
        P(),
    )
    return jax.shard_map(
        per_device, mesh=mesh, in_specs=in_specs, out_specs=out_specs, check_vma=False
    )
```

```python
import functools

import jax
import jax.numpy as jnp
from jax import lax
from jax.experimental import pallas as pl
from jax.experimental.pallas import tpu as pltpu
from jax.sharding import PartitionSpec as P

H = 14
KV = 2
HD = 64
FF = 4864
STEP = 5


NORM_EPS = 1e-06
ROPE_BASE = 1000000.0
NEG_BIG = -1e30
EPS_LOW = 0.8
EPS_HIGH = 0.28
BETA_KL = 0.1
CLIP_NORM = 0.05
BETA_ONE = 0.9
BETA_TWO = 0.95
ADAM_EPS = 1e-08
DECAY = 0.1
LR_MATRIX = 0.02
LR_OUT = 0.12
LR_GAIN = 1.0
LR_BIAS = 0.5


def norm_rows(values, gain):
    return values * lax.rsqrt(jnp.mean(values * values, axis=-1, keepdims=True) + NORM_EPS) * gain


def partner(value, axis, mask):
    size = lax.axis_size(axis)
    return lax.ppermute(value, axis, [(place, place ^ mask) for place in range(size)])


def masks_of(size):
    masks, mask = [], 1
    while mask < size:
        masks.append(mask)
        mask *= 2
    return masks


def bit_of(axis, mask):
    return (lax.axis_index(axis) & mask) != 0


def xor_order(blocks, axis):
    bits = masks_of(blocks.shape[0])
    held = blocks.reshape((2,) * len(bits) + blocks.shape[1:])
    for at, bit in enumerate(reversed(bits)):
        held = jnp.where(bit_of(axis, bit), jnp.flip(held, at), held)
    return held.reshape(blocks.shape)


def after(value, *first):
    return lax.optimization_barrier((value, first))[0]


def together(*values):
    return lax.optimization_barrier(values)


def seq_stages_of(size):
    bits = masks_of(size)
    stages, rest = [], bits[1:]
    while rest:
        pair, rest = rest[:2], rest[2:]
        stages.append([pair[0], pair[1], pair[0] ^ pair[1]] if len(pair) == 2 else pair)
    return stages + [bits[:1]]


def spread(value, axis, stages):
    held = value[None]
    for masks in stages:
        held = jnp.concatenate([held] + [partner(held, axis, mask) for mask in masks])
    return held


def to_xor_order(blocks, axis, stages):
    bits = masks_of(blocks.shape[0])
    turned = xor_order(blocks, axis).reshape((2,) * len(bits) + blocks.shape[1:])
    place = {bit: at for at, bit in enumerate(reversed(bits))}
    order = [place[mask] for masks in reversed(stages) for mask in reversed(masks) if mask in bits]
    rest = list(range(len(bits), turned.ndim))
    return jnp.transpose(turned, order + rest).reshape(blocks.shape)


def to_index_order(blocks, axis, stages):
    bits = masks_of(blocks.shape[0])
    place = {bit: at for at, bit in enumerate(reversed(bits))}
    order = [place[mask] for masks in reversed(stages) for mask in reversed(masks) if mask in bits]
    back = [order.index(at) for at in range(len(bits))]
    held = blocks.reshape((2,) * len(bits) + blocks.shape[1:])
    held = jnp.transpose(held, back + list(range(len(bits), held.ndim)))
    return xor_order(held.reshape(blocks.shape), axis)


def exchange(value, axes):
    return lax.all_to_all(value, axes, split_axis=0, concat_axis=0, tiled=True)


def exchange_copies(value, axes):
    size = lax.axis_size(axes)
    return exchange(jnp.broadcast_to(value[None], (size,) + value.shape), axes)


def total_of(parts):
    total = parts[0].astype(jnp.float32)
    for part in parts[1:]:
        total = total + part.astype(jnp.float32)
    return total.astype(jnp.bfloat16)


def cut(first, second, axis, mask):
    own = bit_of(axis, mask)
    return jnp.where(own, second, first), partner(jnp.where(own, first, second), axis, mask)


def halve(first, second, axis, mask):
    return total_of(cut(first, second, axis, mask))


def collect(blocks, axis, stages):
    held = blocks
    for masks in reversed(stages):
        count = len(masks) + 1
        held = held.reshape((count, held.shape[0] // count) + held.shape[1:])
        held = total_of(
            [held[0]] + [partner(held[at + 1], axis, mask) for at, mask in enumerate(masks)]
        )
    return held[0]


def ordered(value, other, axis, mask):
    own = bit_of(axis, mask)
    return jnp.where(own, other, value), jnp.where(own, value, other)


def double(value, axis, mask):
    return ordered(value, partner(value, axis, mask), axis, mask)


def dot_nn(left, right):
    return jnp.dot(left, right, preferred_element_type=jnp.float32)


def dot_tn(left, right):
    return lax.dot_general(
        left, right, (((0,), (0,)), ((), ())), preferred_element_type=jnp.float32
    )


def dot_nt(left, right):
    return lax.dot_general(
        left, right, (((1,), (1,)), ((), ())), preferred_element_type=jnp.float32
    )


def squares_of(value):
    value = value.astype(jnp.float32)
    return jnp.sum(value * value)


def adam(weight, moment, second, gradient, learn_rate, decay_rate):
    moment = BETA_ONE * moment + (1.0 - BETA_ONE) * gradient
    second = BETA_TWO * second + (1.0 - BETA_TWO) * gradient * gradient
    corrected = moment / (1.0 - BETA_ONE**STEP)
    scaled = second / (1.0 - BETA_TWO**STEP)
    return (
        weight - learn_rate * (corrected / (jnp.sqrt(scaled) + ADAM_EPS) + decay_rate * weight),
        moment,
        second,
    )


LOW = jnp.bfloat16
F32 = jnp.float32
LANES = 128


def iota(shape, dim):
    return lax.broadcasted_iota(jnp.int32, shape, dim)


def in_hbm(*arrays):
    return tuple(pltpu.with_memory_space_constraint(array, pltpu.HBM) for array in arrays)


def like(shape, dtype=jnp.float32):
    return jax.ShapeDtypeStruct(shape, dtype)


def in_vmem(body, outs, args, name, flops=0, exps=0, limit=16, kept=(), scratch=()):
    moved = sum(a.size * a.dtype.itemsize for a in args) + sum(
        o.size * o.dtype.itemsize for o in outs
    )
    whole = lambda rank: lambda step: (0,) * rank
    near = pl.BlockSpec(memory_space=pltpu.VMEM)
    return pl.pallas_call(
        body,
        grid=(1,),
        in_specs=[
            pl.BlockSpec(a.shape, whole(a.ndim)) if at in kept else near
            for at, a in enumerate(args)
        ],
        out_specs=[near] * len(outs),
        out_shape=outs,
        scratch_shapes=scratch,
        compiler_params=pltpu.CompilerParams(vmem_limit_bytes=limit * 2**20),
        cost_estimate=pl.CostEstimate(flops=flops, bytes_accessed=moved, transcendentals=exps),
        name=name,
    )(*[in_hbm(a)[0] if at in kept else a for at, a in enumerate(args)])


def upright(row):
    count = row.shape[1]
    square = jnp.broadcast_to(row.astype(F32), (count, count))
    return jnp.sum(
        jnp.where(iota((count, count), 0) == iota((count, count), 1), square, 0.0),
        axis=1,
        keepdims=True,
    )


def turned(values, cosine, sine):
    tiles = []
    for at in range(0, values.shape[1], LANES):
        tile = values[:, at : at + LANES]
        front = iota(tile.shape, 1) % HD < HD // 2
        swapped = jnp.where(
            front, pltpu.roll(tile, LANES - HD // 2, 1), pltpu.roll(tile, HD // 2, 1)
        )
        tiles.append(tile * cosine + swapped * sine)
    return tiles[0] if len(tiles) == 1 else jnp.concatenate(tiles, axis=1)


def norm_back(values, gain, grad):
    inverse = lax.rsqrt(jnp.mean(values * values, axis=-1, keepdims=True) + NORM_EPS)
    scaled = grad * gain
    inner = jnp.mean(values * scaled, axis=-1, keepdims=True)
    into = inverse * scaled - values * (inverse * inverse * inverse * inner)
    return into, jnp.sum(grad * values * inverse, axis=0, keepdims=True)


def placed(pick_columns, values):
    high = values.astype(LOW)
    rest = (values - high.astype(F32)).astype(LOW)
    return dot_nn(pick_columns, high) + dot_nn(pick_columns, rest)


def coded(value):
    high = value.astype(LOW).astype(F32)
    middle = (value - high).astype(LOW).astype(F32)
    return high, middle, (value - high - middle).astype(LOW).astype(F32)


def coded_lanes(columns):
    parts = [part for column in columns for part in coded(column)]
    lane = iota((columns[0].shape[0], LANES), 1)
    tail = jnp.zeros(lane.shape, F32)
    for at, part in enumerate(parts):
        tail = jnp.where(lane == at, part, tail)
    return tail.astype(LOW)


def decoded(tail, at):
    tail = tail.astype(F32)
    lane = iota(tail.shape, tail.ndim - 1)
    return jnp.sum(
        jnp.where((lane >= 3 * at) & (lane < 3 * at + 3), tail, 0.0), axis=-1, keepdims=True
    )


def request_body(vrows, capacity, tokens_ref, requests_ref, placer_ref):
    row = tokens_ref[...].astype(F32)
    column = upright(tokens_ref[...])
    count = row.shape[1]
    owner_row = jnp.floor((row + 0.5) / vrows)
    owner = jnp.floor((column + 0.5) / vrows)
    earlier = (owner == owner_row) & (iota((count, count), 1) < iota((count, count), 0))
    slot = jnp.sum(jnp.where(earlier, 1.0, 0.0), axis=1, keepdims=True)
    hit = (owner * capacity + slot) == iota(placer_ref.shape, 1).astype(F32)
    placer_ref[...] = jnp.where(hit, 1.0, 0.0).astype(LOW)
    requests_ref[...] = jnp.sum(
        jnp.where(hit, column - owner * vrows, 0.0), axis=0, keepdims=True
    ).astype(jnp.int32)


def embed_body(
    rows_ref, placer_ref, w_ref, bias_ref, gain_ref, cos_ref, sin_ref, x_ref, normed_ref, kv_ref
):
    x_zero = dot_nn(placer_ref[...], rows_ref[...])
    x_ref[...] = x_zero.astype(LOW)
    normed = norm_rows(x_zero, gain_ref[...]).astype(LOW)
    normed_ref[...] = normed
    kv = dot_nn(normed, w_ref[...]) + bias_ref[...]
    width = KV * HD
    keys = turned(kv[:, :width], cos_ref[...], sin_ref[...]).astype(LOW)
    values = kv[:, width:].astype(LOW)
    for at in range(kv_ref.shape[0]):
        kv_ref[at, :, :width] = keys
        kv_ref[at, :, width:] = values


def pick_columns_of(picks, slots, shift):
    return jnp.where(
        iota((slots, picks.shape[1]), 0) == picks + shift, 1.0, 0.0
    ).astype(LOW)


def pick_body(
    x_ref, normed_ref, picks_ref, w_ref, bias_ref, cos_ref, sin_ref,
    picked_ref, target_ref, picked_normed_ref, query_ref,
):
    slots = x_ref.shape[0]
    here = pick_columns_of(picks_ref[...], slots, 0)
    after = pick_columns_of(picks_ref[...], slots, 1)
    picked_ref[...] = dot_tn(here, x_ref[...])
    target_ref[...] = dot_tn(after, x_ref[...])
    normed = dot_tn(here, normed_ref[...]).astype(LOW)
    picked_normed_ref[...] = normed
    query = dot_nn(normed, w_ref[...]) + bias_ref[...]
    query_ref[...] = turned(query, cos_ref[...], sin_ref[...]).astype(LOW)


def stacked_heads(values, first, count):
    return jnp.concatenate(
        [values[:, (first + at) * HD : (first + at + 1) * HD] for at in range(count)], axis=0
    )


CHUNK = 2048


def scores_of(queries, keys, places, count, start):
    scores = dot_nt(queries, keys) * HD ** (-0.5)
    reach = jnp.concatenate([places] * count, axis=0) - start
    return jnp.where(iota(scores.shape, 1) <= reach, scores, NEG_BIG)


def key_slices(kv_ref, head, start, size):
    rows = pl.ds(start, size)
    return (
        kv_ref[rows, head * HD : (head + 1) * HD],
        kv_ref[rows, (KV + head) * HD : (KV + head + 1) * HD],
    )


def over_keys(length, body, carry):
    if length <= CHUNK:
        return body(0, carry)
    return lax.fori_loop(
        0, length // CHUNK, lambda at, held: body(pl.multiple_of(at * CHUNK, CHUNK), held), carry
    )


def softmax_parts(queries, kv_ref, head, places, count):
    length = kv_ref.shape[0]
    size = min(length, CHUNK)
    if length <= CHUNK:

        def chances(start):
            scores = scores_of(queries, key_slices(kv_ref, head, 0, size)[0], places, count, 0)
            raised = jnp.exp(scores - jnp.max(scores, axis=1, keepdims=True))
            return raised * (1.0 / jnp.sum(raised, axis=1, keepdims=True))

        return chances

    def statistics(start, held):
        top, summed = held
        keys = key_slices(kv_ref, head, start, size)[0]
        scores = scores_of(queries, keys, places, count, start)
        now = jnp.maximum(top, jnp.max(scores, axis=1, keepdims=True))
        raised = jnp.exp(scores - now)
        return now, summed * jnp.exp(top - now) + jnp.sum(raised, axis=1, keepdims=True)

    rows = queries.shape[0]
    top, summed = over_keys(
        length, statistics, (jnp.full((rows, 1), NEG_BIG, F32), jnp.zeros((rows, 1), F32))
    )

    def chances_at(start):
        keys = key_slices(kv_ref, head, start, size)[0]
        return jnp.exp(scores_of(queries, keys, places, count, start) - top) * (1.0 / summed)

    return chances_at


def attend_body(
    query_ref, kv_ref, place_ref, w_ref, picked_ref, gain_ref,
    mixed_ref, attended_ref, one_ref, normed_ref,
):
    places = upright(place_ref[...]).astype(jnp.int32)
    picks = places.shape[0]
    group = H // KV
    length = kv_ref.shape[0]
    size = min(length, CHUNK)
    for head in range(KV):
        queries = stacked_heads(query_ref[...], head * group, group)
        chances = softmax_parts(queries, kv_ref, head, places, group)

        def add(start, total):
            values = key_slices(kv_ref, head, start, size)[1]
            return total + dot_nn(chances(start).astype(LOW), values)

        out = over_keys(length, add, jnp.zeros(queries.shape, F32))
        for at in range(group):
            spot = (head * group + at) * HD
            attended_ref[:, spot : spot + HD] = out[at * picks : (at + 1) * picks]
    mixed = attended_ref[...].astype(LOW)
    mixed_ref[...] = mixed
    one = picked_ref[...] + dot_nn(mixed, w_ref[...])
    one_ref[...] = one
    normed = norm_rows(one, gain_ref[...]).astype(LOW)
    for at in range(normed_ref.shape[0]):
        normed_ref[at] = normed


def feed_body(normed_ref, gate_w_ref, up_w_ref, down_w_ref, gate_ref, up_ref, hidden_ref, out_ref):
    normed = normed_ref[...]
    gate = dot_nn(normed, gate_w_ref[...])
    up = dot_nn(normed, up_w_ref[...])
    gate_ref[...] = gate
    up_ref[...] = up
    hidden = (gate * (1.0 / (1.0 + jnp.exp(-gate))) * up).astype(LOW)
    hidden_ref[...] = hidden
    out_ref[...] = dot_nn(hidden, down_w_ref[...]).astype(LOW)


def feed_sum_body(parts_ref, one_ref, gain_ref, two_ref, final_ref):
    two = one_ref[...] + jnp.sum(parts_ref[...].astype(F32), axis=0)
    two_ref[...] = two
    final_ref[...] = norm_rows(two, gain_ref[...]).astype(LOW)


def head_body(
    vrows, rows_ref, other_ref, table_ref, raised_ref, tops_ref, own_ref, send_ref, top, summed, total
):
    step = pl.program_id(0)
    block = table_ref.shape[0]
    width = table_ref.shape[1]
    half = own_ref.shape[0]

    @pl.when(step == 0)
    def _():
        top[...] = jnp.full(top.shape, NEG_BIG, F32)
        summed[...] = jnp.zeros(summed.shape, F32)
        total[...] = jnp.zeros(total.shape, F32)

    left = vrows - step * block
    entries = jnp.where(iota((block, 1), 0) < left, table_ref[...], 0.0).astype(LOW)
    inside = iota((1, block), 1) < left
    part = min(256, half)
    pieces = []
    for ref, start in ((rows_ref, 0), (other_ref, half)):
        tokens = ref[...].reshape(half, width)
        pieces += [
            (slice(start + at, start + at + part), tokens[at : at + part])
            for at in range(0, half, part)
        ]
    logits_of = [dot_nt(tokens, entries) for _, tokens in pieces]
    for (piece, _), logits in zip(pieces, logits_of):
        logits = jnp.where(inside, logits, NEG_BIG)
        before = top[piece, :1]
        now = jnp.maximum(before, jnp.max(logits, axis=1, keepdims=True))
        raised = jnp.exp(logits - now)
        shrink = jnp.exp(before - now)
        low = raised.astype(LOW)
        raised_ref[piece] = low
        summed[piece] = summed[piece] * shrink + jnp.sum(raised, axis=1, keepdims=True)
        total[piece] = total[piece] * shrink + dot_nn(low, entries)
        top[piece] = jnp.broadcast_to(now, (part, LANES))
        column = iota((part, LANES), 1) == step
        tops_ref[piece] = jnp.where(column, now, tops_ref[piece])

    @pl.when(step == pl.num_programs(0) - 1)
    def _():
        for ref, at in ((own_ref, 0), (send_ref, half)):
            here = slice(at, at + half)
            ref[:, :width] = (total[here] / summed[here, :1]).astype(LOW)
            ref[:, width:] = coded_lanes([top[here, :1] + jnp.log(summed[here, :1])])


def head_part(rows, other, group, table, block):
    seqs, _, picks, width = rows.shape
    half = seqs * picks
    vrows = table.shape[0]
    steps = -(-vrows // block)
    whole = lambda step: (0, 0)
    states = pl.BlockSpec((seqs, 1, picks, width), lambda step: (0, group, 0, 0))
    mean = pl.BlockSpec((half, width + LANES), whole)
    return pl.pallas_call(
        functools.partial(head_body, vrows),
        grid=(steps,),
        in_specs=[states, states, pl.BlockSpec((block, width), lambda step: (step, 0))],
        out_specs=[
            pl.BlockSpec((2 * half, block), lambda step: (0, step)),
            pl.BlockSpec((2 * half, LANES), whole),
            mean,
            mean,
        ],
        out_shape=[
            pltpu.HBM((2 * half, steps * block), LOW),
            like((2 * half, LANES)),
            like((half, width + LANES), LOW),
            like((half, width + LANES), LOW),
        ],
        scratch_shapes=[
            pltpu.VMEM((2 * half, LANES), F32),
            pltpu.VMEM((2 * half, LANES), F32),
            pltpu.VMEM((2 * half, width), F32),
        ],
        compiler_params=pltpu.CompilerParams(vmem_limit_bytes=(28 if half <= 256 else 60) * 2**20),
        cost_estimate=pl.CostEstimate(
            flops=8 * half * vrows * width,
            bytes_accessed=vrows * width * 4 + half * vrows * 4,
            transcendentals=2 * half * vrows,
        ),
        name="head_part",
    )(rows, other, *in_hbm(table))


def merge_values(parts):
    highest = parts[0][1]
    for _, log in parts[1:]:
        highest = jnp.maximum(highest, log)
    summed, total = 0.0, 0.0
    for mean, log in parts:
        share = jnp.exp(log - highest)
        summed = summed + share
        total = total + share * mean
    return total * (1.0 / summed), highest + jnp.log(summed)


def merge_body(*refs):
    out_ref = refs[-1]
    width = out_ref.shape[1] - LANES
    mean, log = merge_values(
        [(ref[:, :width].astype(F32), decoded(ref[:, width:], 0)) for ref in refs[:-1]]
    )
    out_ref[:, :width] = mean.astype(LOW)
    out_ref[:, width:] = coded_lanes([log])


def loss_body(
    parts_ref, final_ref, target_ref, two_ref, gain_ref, live_ref, old_ref, ref_ref, advantage_ref,
    message_ref, grad_ref, gain_grad_ref, added_ref, loss_ref,
):
    width = final_ref.shape[1]
    mean, log_total = merge_values(
        [
            (parts_ref[at, :, :width].astype(F32), decoded(parts_ref[at, :, width:], 0))
            for at in range(parts_ref.shape[0])
        ]
    )
    final = final_ref[...].astype(F32)
    target = target_ref[...]
    live = upright(live_ref[...])
    to_ref = jnp.sum(final * target, axis=1, keepdims=True) - log_total
    logp = to_ref
    to_ref = logp - upright(ref_ref[...])
    advantage = advantage_ref[...]
    weight = jnp.clip(jnp.exp(logp - upright(old_ref[...])), 1.0 - EPS_LOW, 1.0 + EPS_HIGH)
    coefficient = live * (-weight * advantage + BETA_KL * to_ref)
    loss = live * (-weight * advantage * logp + 0.5 * BETA_KL * to_ref * to_ref)
    loss_ref[...] = jnp.broadcast_to(jnp.sum(loss, axis=0, keepdims=True), loss_ref.shape)
    added_ref[...] = coefficient * final
    grad, gain_grad_ref[...] = norm_back(
        two_ref[...], gain_ref[...], coefficient * (target - mean)
    )
    grad_ref[...] = grad
    low = grad.astype(LOW)
    tail = coded_lanes([log_total, coefficient])
    for at in range(message_ref.shape[0]):
        message_ref[at, :, :width] = low
        message_ref[at, :, width:] = tail


def feed_back_body(
    message_ref, hidden_ref, gate_ref, up_ref, gate_w_ref, up_w_ref, down_w_ref,
    grad_gate_ref, grad_up_ref, out_ref,
):
    width = out_ref.shape[1]
    grad_hidden = dot_nt(message_ref[:, :width], down_w_ref[...])
    gate = gate_ref[...]
    up = up_ref[...]
    sigmoid = 1.0 / (1.0 + jnp.exp(-gate))
    grad_gate = (grad_hidden * up * sigmoid * (1.0 + gate * (1.0 - sigmoid))).astype(LOW)
    grad_up = (grad_hidden * gate * sigmoid).astype(LOW)
    grad_gate_ref[...] = grad_gate
    grad_up_ref[...] = grad_up
    out_ref[...] = (
        dot_nt(grad_gate, gate_w_ref[...]) + dot_nt(grad_up, up_w_ref[...])
    ).astype(LOW)


def one_back_body(parts_ref, one_ref, grad_two_ref, gain_ref, grad_ref, low_ref, gain_grad_ref):
    into, gain_grad_ref[...] = norm_back(
        one_ref[...], gain_ref[...], jnp.sum(parts_ref[...].astype(F32), axis=0)
    )
    grad = grad_two_ref[...] + into
    grad_ref[...] = grad
    low_ref[...] = grad.astype(LOW)


def attend_back_body(
    grad_ref, w_ref, query_ref, kv_ref, place_ref, attended_ref, cos_ref, sin_ref,
    kv_grad_ref, query_pre_ref, bias_ref, query_grad,
):
    places = upright(place_ref[...]).astype(jnp.int32)
    picks = places.shape[0]
    into = dot_nt(grad_ref[...], w_ref[...]).astype(LOW)
    group = H // KV
    length = kv_ref.shape[0]
    size = min(length, CHUNK)
    for head in range(KV):
        queries = stacked_heads(query_ref[...], head * group, group)
        grads = stacked_heads(into, head * group, group)
        inner = jnp.sum(
            grads.astype(F32) * stacked_heads(attended_ref[...], head * group, group),
            axis=1,
            keepdims=True,
        )
        chances = softmax_parts(queries, kv_ref, head, places, group)

        def add(start, total):
            keys, values = key_slices(kv_ref, head, start, size)
            chance = chances(start)
            scores = (chance * (dot_nt(grads, values) - inner)).astype(LOW)
            rows = pl.ds(start, size)
            kv_grad_ref[rows, head * HD : (head + 1) * HD] = (
                dot_tn(scores, queries) * HD ** (-0.5)
            ).astype(LOW)
            kv_grad_ref[rows, (KV + head) * HD : (KV + head + 1) * HD] = dot_tn(
                chance.astype(LOW), grads
            ).astype(LOW)
            return total + dot_nn(scores, keys) * HD ** (-0.5)

        query_part = over_keys(length, add, jnp.zeros(queries.shape, F32))
        for at in range(group):
            spot = (head * group + at) * HD
            query_grad[:, spot : spot + HD] = query_part[at * picks : (at + 1) * picks]
    query_pre = turned(query_grad[...], cos_ref[...], -sin_ref[...]).astype(LOW)
    query_pre_ref[...] = query_pre
    bias_ref[...] = jnp.sum(query_pre.astype(F32), axis=0, keepdims=True)


def zero_back_body(
    parts_ref, cos_ref, sin_ref, kv_w_ref, query_pre_ref, q_w_ref, picks_ref, x_ref, gain_ref,
    grad_one_ref, added_ref, placer_ref,
    kv_pre_ref, back_ref, gain_grad_ref, bias_ref,
):
    width = KV * HD
    slots = x_ref.shape[0]
    own = jnp.sum(parts_ref[...].astype(F32), axis=0)
    kv_pre_ref[:, :width] = turned(own[:, :width], cos_ref[...], -sin_ref[...]).astype(LOW)
    kv_pre_ref[:, width:] = own[:, width:].astype(LOW)
    kv_pre = kv_pre_ref[...]
    bias_ref[...] = jnp.sum(kv_pre.astype(F32), axis=0, keepdims=True)
    here = pick_columns_of(picks_ref[...], slots, 0)
    after = pick_columns_of(picks_ref[...], slots, 1)
    grad_normed = dot_nt(kv_pre, kv_w_ref[...]) + placed(
        here, dot_nt(query_pre_ref[...], q_w_ref[...])
    )
    into, gain_grad_ref[...] = norm_back(x_ref[...].astype(F32), gain_ref[...], grad_normed)
    grad = into + placed(here, grad_one_ref[...]) + placed(after, added_ref[...])
    back_ref[...] = dot_tn(placer_ref[...], grad.astype(LOW)).astype(LOW)


def layer_grads_body(
    core_ref, normed_ref, gate_ref, up_ref, hidden_ref, message_ref,
    own_ref, send_ref, own_down_ref, send_down_ref,
):
    second = core_ref[0] > 0
    gate, up = gate_ref[...], up_ref[...]
    normed = normed_ref[...]
    own_ref[...] = dot_tn(normed, jnp.where(second, up, gate)).astype(LOW)
    send_ref[...] = dot_tn(normed, jnp.where(second, gate, up)).astype(LOW)
    half = own_down_ref.shape[0]
    grads = message_ref[:, : own_down_ref.shape[1]]
    front, back = hidden_ref[:, :half], hidden_ref[:, half : 2 * half]
    own_down_ref[...] = dot_tn(jnp.where(second, back, front), grads).astype(LOW)
    send_down_ref[...] = dot_tn(jnp.where(second, front, back), grads).astype(LOW)


def summary_body(arrived_ref, rows_ref, names_ref, out_ref):
    arrived = arrived_ref[...]
    names = names_ref[...].astype(F32)
    cross = jnp.sum(arrived.astype(F32) * rows_ref[...].astype(F32), axis=0, keepdims=True)
    same = jnp.where(upright(names_ref[...]) == names, dot_nt(arrived, arrived), 0.0)
    out_ref[...] = 2.0 * jnp.sum(cross, axis=1, keepdims=True) + jnp.sum(
        jnp.sum(same, axis=0, keepdims=True), axis=1, keepdims=True
    )


def norm_body(parts_ref, totals_ref, stats_ref):
    totals = jnp.sum(parts_ref[...], axis=0)
    totals_ref[...] = totals
    last = totals.shape[0] - 1
    own = totals[last:]
    lane = iota(own.shape, 1)

    def entry(at):
        return jnp.sum(jnp.where(lane == at, own, 0.0), axis=1, keepdims=True)

    others = jnp.where(iota(totals.shape, 0) < last, totals * totals, 0.0)
    squares = entry(0) + jnp.sum(
        jnp.sum(others, axis=0, keepdims=True), axis=1, keepdims=True
    )
    count = jnp.maximum(entry(2), 1.0)
    norm = jnp.sqrt(squares) / count
    factor = jnp.minimum(1.0, CLIP_NORM / (norm + 1e-06)) / count
    out = jnp.where(lane == 0, entry(1), jnp.where(lane == 1, count, norm))
    stats_ref[...] = jnp.where(lane == 3, factor, out)


def head_grad_body(
    span, first, far_ref, near_ref, far_tops_ref, near_tops_ref, rows_ref, other_ref, tails_ref, tails_other_ref,
    grad_ref, squares_ref,
):
    step = pl.program_id(0)
    block = step + first
    width = grad_ref.shape[1]
    half = far_ref.shape[0] // 2
    grad = 0.0
    for group, raised_ref, tops_ref in ((1, far_ref, far_tops_ref), (0, near_ref, near_tops_ref)):
        for at, (states_ref, tail_ref) in enumerate(
            ((rows_ref, tails_ref), (other_ref, tails_other_ref))
        ):
            here = slice(at * half, (at + 1) * half)
            tops = tops_ref[here]
            top = jnp.sum(
                jnp.where(iota(tops.shape, 1) == block // span, tops, 0.0), axis=1, keepdims=True
            )
            tail = tail_ref[group]
            scale = -decoded(tail, 1) * jnp.exp(top - decoded(tail, 0))
            states = states_ref[:, group].reshape(half, width).astype(F32)
            grad = grad + dot_tn(raised_ref[here], (states * scale).astype(LOW))
    grad_ref[...] = grad.astype(LOW)

    @pl.when(step == 0)
    def _():
        squares_ref[...] = jnp.zeros(squares_ref.shape, F32)

    squares_ref[...] += jnp.sum(grad * grad, axis=0, keepdims=True)


def head_grad(far, near, rows, other, tails, tails_other, vrows, block, span, first, steps, held):
    width = rows.shape[-1]
    tokens = far[0].shape[0]
    whole = lambda count: lambda step: (0,) * count
    raised = pl.BlockSpec((tokens, block), lambda step: (0, step + first))
    fixed = lambda array: pl.BlockSpec(array.shape, whole(array.ndim))
    return pl.pallas_call(
        lambda *refs: head_grad_body(span, first, *refs[:8], *refs[-2:]),
        grid=(steps,),
        in_specs=[
            raised,
            raised,
            fixed(far[1]),
            fixed(near[1]),
            fixed(rows),
            fixed(other),
            fixed(tails),
            fixed(tails_other),
        ]
        + [pl.BlockSpec(memory_space=pl.ANY)] * len(held),
        out_specs=[
            pl.BlockSpec((block, width), lambda step: (step + first, 0)),
            pl.BlockSpec((8, width), whole(2)),
        ],
        out_shape=[pltpu.HBM((vrows, width), LOW), like((8, width))],
        input_output_aliases={8 + at: at for at in range(len(held))},
        compiler_params=pltpu.CompilerParams(vmem_limit_bytes=(28 if tokens <= 512 else 60) * 2**20),
        cost_estimate=pl.CostEstimate(
            flops=4 * tokens * steps * block * width,
            bytes_accessed=steps * block * (4 * tokens + 2 * width),
            transcendentals=0,
        ),
        name="head_grad",
    )(*in_hbm(far[0], near[0], far[1], near[1], rows, other, tails, tails_other), *held)


def table_adam_body(first, scale_ref, names_ref, added_ref, grad_ref, w_ref, m_ref, v_ref, *refs):
    w_out, m_out, v_out = refs[-3:]
    rows = grad_ref.shape[0]
    here = iota((rows, names_ref.shape[1]), 0) + (pl.program_id(0) + first) * rows
    picker = jnp.where(here == names_ref[...], 1.0, 0.0).astype(LOW)
    grad = grad_ref[...].astype(F32) + dot_nn(picker, added_ref[...])
    w_out[...], m_out[...], v_out[...] = adam(
        w_ref[...], m_ref[...], v_ref[...], grad * scale_ref[0], LR_MATRIX, DECAY
    )


def table_adam(scale, names, added, grad, weight, moment, second, rows, first, steps, held):
    vrows, width = weight.shape
    whole = lambda step: (0, 0)
    here = pl.BlockSpec((rows, width), lambda step: (step + first, 0))
    return pl.pallas_call(
        functools.partial(table_adam_body, first),
        grid=(steps,),
        in_specs=[
            pl.BlockSpec(memory_space=pltpu.SMEM),
            pl.BlockSpec((1, names.shape[1]), whole),
            pl.BlockSpec(added.shape, whole),
            here,
            here,
            here,
            here,
        ]
        + [pl.BlockSpec(memory_space=pl.ANY)] * len(held),
        out_specs=[here, here, here],
        out_shape=[pltpu.HBM((vrows, width), F32)] * 3,
        input_output_aliases={7 + at: at for at in range(len(held))},
        compiler_params=pltpu.CompilerParams(vmem_limit_bytes=44 * 2**20),
        cost_estimate=pl.CostEstimate(
            flops=2 * names.shape[1] * steps * rows * width,
            bytes_accessed=steps * rows * width * 26,
            transcendentals=steps * rows * width,
        ),
        name="table_adam",
    )(scale, names, added, *in_hbm(grad, weight, moment, second), *held)


def per_device(
    token_ids,
    row_lengths,
    prompt_lengths,
    picks,
    old_logp,
    ref_logp,
    rewards,
    embed,
    embed_m,
    embed_v,
    w_qkv,
    w_qkv_m,
    w_qkv_v,
    w_out,
    w_out_m,
    w_out_v,
    w_gateup,
    w_gateup_m,
    w_gateup_v,
    w_down,
    w_down_m,
    w_down_v,
    gains,
    gains_m,
    gains_v,
    bias,
    bias_m,
    bias_v,
):
    both = ("batch", "seq")
    owners = lax.axis_size(both)
    seq_index = lax.axis_index("seq")
    row_index = lax.axis_index("batch")
    batch_count = lax.axis_size("batch")
    seq_count = lax.axis_size("seq")
    core_mask, far_mask = 1, 2
    on_core, on_far = bit_of("batch", core_mask), bit_of("batch", far_mask)
    low = LOW
    f32 = F32
    local_len = token_ids.shape[1]
    vrows, width = embed.shape
    shard = w_qkv.shape[0]
    half = shard // 2
    ff_part = FF // seq_count
    ff_wide = -(-ff_part // LANES) * LANES
    capacity = max(2, 2 * local_len // owners)
    kv_width = KV * HD
    q_width = H * HD
    n_picks = picks.shape[1]
    row_count = seq_count * n_picks

    requests, placer = in_vmem(
        functools.partial(request_body, vrows, capacity),
        [like((1, owners * capacity), jnp.int32), like((local_len, owners * capacity), low)],
        [token_ids],
        "requests",
    )
    sent_requests = exchange(requests.reshape(owners, capacity), both)

    stages = seq_stages_of(seq_count)
    core_row = lax.axis_index("batch") & core_mask
    qkv_cut = -(-(q_width + 2 * kv_width) // (2 * LANES)) * LANES
    out_cut = -(-width // (2 * LANES)) * LANES

    def part_of(value, columns):
        start = jnp.where(on_core, value.shape[1] - columns, 0)
        return lax.dynamic_slice(value, (jnp.where(on_far, half, 0), start), (half, columns)).astype(low)

    def widened(value):
        return jnp.pad(value, [(0, 0)] * (value.ndim - 1) + [(0, ff_wide - ff_part)])

    proj_parts = spread(
        jnp.concatenate([part_of(w_qkv, qkv_cut), part_of(w_out, out_cut)], axis=1),
        "seq",
        stages[:-1],
    )
    my_kv = lax.dynamic_slice(
        w_qkv, (0, jnp.where(on_core, q_width + kv_width, q_width)), (shard, kv_width)
    ).astype(low)
    my_kv = jnp.concatenate([my_kv[:half], my_kv[half:]], axis=1)
    pieces = jnp.transpose(part_of(w_gateup, FF).reshape(half, seq_count, ff_part), (1, 0, 2))
    pieces = jnp.concatenate(
        [widened(pieces), jnp.broadcast_to(my_kv[None], (seq_count,) + my_kv.shape)], axis=2
    )
    w_down_low = jnp.pad(w_down.astype(low), ((0, ff_wide - ff_part), (0, 0)))
    sent_requests, pieces, w_down_low, proj_parts = together(
        sent_requests, pieces, w_down_low, proj_parts
    )
    proj_others = [partner(proj_parts, "seq", mask) for mask in stages[-1]]

    def far_rows(value):
        return jnp.stack(double(value, "batch", far_mask), axis=1).reshape(width, -1)

    def core_columns(value, whole):
        first, second = double(value, "batch", core_mask)
        return jnp.concatenate([first, second[:, 2 * value.shape[1] - whole :]], axis=1)

    wanted = sent_requests.reshape(-1)
    found = embed.at[wanted].get(mode="promise_in_bounds").astype(low)
    found, pieces, proj_parts, proj_others = together(
        found.reshape(owners, capacity, width), exchange(pieces, "seq"), proj_parts, proj_others
    )
    returned = exchange(found, both)
    my_kv = pieces[..., ff_wide:].reshape(seq_count, half, 2, kv_width)
    my_kv = jnp.transpose(my_kv, (0, 2, 1, 3)).reshape(width, kv_width)
    other_kv = partner(my_kv, "batch", core_mask)
    my_gu = pieces[..., :ff_wide]
    proj_parts = to_index_order(jnp.concatenate([proj_parts] + proj_others), "seq", stages)
    my_q = proj_parts[..., :qkv_cut]
    other_q = partner(my_q, "batch", far_mask)
    out_parts = proj_parts[..., qkv_cut:]
    returned, my_kv, other_kv, my_gu, my_q, other_q, out_parts = together(
        returned, my_kv, other_kv, my_gu, my_q, other_q, out_parts
    )
    w_kv_full = jnp.concatenate(ordered(my_kv, other_kv, "batch", core_mask), axis=1)
    w_q_far = jnp.stack(ordered(my_q, other_q, "batch", far_mask), axis=1)
    w_q_far = w_q_far.reshape(width, qkv_cut)
    returned = returned.reshape(owners * capacity, width)
    w_q_full = core_columns(w_q_far, q_width + 2 * kv_width)[:, :q_width]
    w_out_far = far_rows(out_parts)
    other_gu = partner(after(my_gu, w_out_far), "batch", far_mask)

    places = seq_index * local_len + jnp.arange(local_len, dtype=jnp.int32)
    pick_places = seq_index * local_len + picks
    row_names = jnp.arange(batch_count, dtype=jnp.int32) == row_index
    prompt_here = jnp.sum(jnp.where(row_names, prompt_lengths, 0))
    length_here = jnp.sum(jnp.where(row_names, row_lengths, 0))
    live = ((pick_places >= prompt_here) & (pick_places + 1 < length_here)).astype(f32)
    advantage = (
        jnp.sum(jnp.where(row_names, rewards, 0.0)) - jnp.mean(rewards)
    ).reshape(1, 1)

    def rope_factors(slots):
        lane = jnp.arange(LANES, dtype=jnp.int32)
        frequency = ROPE_BASE ** (-2.0 * (lane % (HD // 2)).astype(f32) / HD)
        angles = slots.astype(f32)[:, None] * frequency[None, :]
        sign = jnp.where(lane % HD < HD // 2, -1.0, 1.0)
        return jnp.cos(angles), jnp.sin(angles) * sign[None, :]

    slot_cos, slot_sin = rope_factors(places)
    pick_cos, pick_sin = rope_factors(pick_places[0])
    bias_row = bias.reshape(1, -1)

    x_zero, normed_one, kv_low = in_vmem(
        embed_body,
        [like((local_len, width), low), like((local_len, width), low), like((seq_count, local_len, 2 * kv_width), low)],
        [returned, placer, w_kv_full, bias_row[:, q_width:], gains[:1], slot_cos, slot_sin],
        "keys_values",
        flops=2 * local_len * width * (owners * capacity + 2 * kv_width),
    )
    kv_all = exchange(kv_low, "seq")
    w_out_full = core_columns(w_out_far, width)
    picked_zero, target_rows, normed_picked, queries = in_vmem(
        pick_body,
        [
            like((n_picks, width)),
            like((n_picks, width)),
            like((n_picks, width), low),
            like((n_picks, q_width), low),
        ],
        [x_zero, normed_one, picks, w_q_full, bias_row[:, :q_width], pick_cos, pick_sin],
        "scored_queries",
        flops=2 * n_picks * width * (q_width + 3 * local_len),
    )
    kv_all, picked_zero, target_rows, normed_picked, queries, w_out_full, my_gu, other_gu = together(
        kv_all, picked_zero, target_rows, normed_picked, queries, w_out_full, my_gu, other_gu
    )
    gu_columns = jnp.stack(ordered(my_gu, other_gu, "batch", far_mask), axis=1)
    gu_columns = gu_columns.reshape(width, ff_wide)
    gu_others = partner(gu_columns, "batch", core_mask)
    kv_all = kv_all.reshape(seq_count * local_len, 2 * kv_width)
    length = kv_all.shape[0]
    limit = 24
    mixed, attended, stream_one, normed_two = in_vmem(
        attend_body,
        [
            like((n_picks, q_width), low),
            like((n_picks, q_width)),
            like((n_picks, width)),
            like((seq_count, n_picks, width), low),
        ],
        [queries, kv_all, pick_places, w_out_full, picked_zero, gains[1:2]],
        "attention",
        flops=4 * n_picks * q_width * length + 2 * n_picks * q_width * width,
        exps=n_picks * H * length,
        limit=limit,
    )


    def shard_columns(value):
        return jnp.transpose(value.reshape(n_picks, seq_count, shard), (1, 0, 2))

    normed_two_all, gu_columns, gu_others, column_pieces = together(
        exchange(normed_two, "seq"),
        gu_columns,
        gu_others,
        jnp.concatenate([shard_columns(normed_picked), shard_columns(mixed)], axis=1),
    )
    w_gate, w_up = ordered(gu_columns, gu_others, "batch", core_mask)
    normed_two_all = normed_two_all.reshape(row_count, width)
    gate_part, up_part, hidden, down_part = in_vmem(
        feed_body,
        [
            like((row_count, ff_wide)),
            like((row_count, ff_wide)),
            like((row_count, ff_wide), low),
            like((row_count, width), low),
        ],
        [normed_two_all, w_gate, w_up, w_down_low],
        "feed_forward",
        flops=6 * row_count * width * ff_part,
        limit=24,
        kept=(3,),
    )
    stream_two, final = in_vmem(
        feed_sum_body,
        [like((n_picks, width)), like((n_picks, width), low)],
        [exchange(down_part.reshape(seq_count, n_picks, width), "seq"), stream_one, gains[2:]],
        "final_norm",
    )

    near = jnp.stack([final, partner(final, "batch", far_mask)])
    rows = exchange_copies(near, "seq")
    other = partner(rows, "batch", core_mask)
    block = 1024

    gathered_columns = exchange(after(column_pieces, rows), "seq")

    def merge(*parts):
        return in_vmem(merge_body, [like(parts[0].shape, low)], parts, "merge_means")[0]

    far, gathered_columns = together(head_part(rows, other, 1, embed, block), gathered_columns)
    far_mean = merge(far[2], partner(far[3], "batch", core_mask))
    near_part, far_mean = together(
        head_part(after(rows, far_mean), other, 0, embed, block),
        partner(far_mean, "batch", far_mask),
    )
    means = merge(near_part[2], partner(near_part[3], "batch", core_mask), far_mean)
    mean_parts, gathered_columns = together(
        exchange(means.reshape(seq_count, n_picks, width + LANES), "seq"),
        to_xor_order(gathered_columns, "seq", stages),
    )
    message, grad_two, grad_gain_two, added, loss_here = in_vmem(
        loss_body,
        [
            like((seq_count, n_picks, width + LANES), low),
            like((n_picks, width)),
            like((1, width)),
            like((n_picks, width)),
            like((1, LANES)),
        ],
        [
            mean_parts,
            final,
            target_rows,
            stream_two,
            gains[2:],
            live,
            old_logp,
            ref_logp,
            advantage,
        ],
        "loss",
        kept=(2, 3, 4, 5, 6, 7),
    )

    messages = exchange(message, "seq").reshape(row_count, width + LANES)
    grad_gate, grad_up, normed_part = in_vmem(
        feed_back_body,
        [
            like((row_count, ff_wide), low),
            like((row_count, ff_wide), low),
            like((row_count, width), low),
        ],
        [messages, hidden, gate_part, up_part, w_gate, w_up, w_down_low],
        "feed_forward_back",
        flops=6 * row_count * width * ff_part,
        limit=28,
        kept=(1, 2, 3, 4, 5, 6),
    )
    normed_part = exchange(normed_part.reshape(seq_count, n_picks, width), "seq")

    layer_grads = in_vmem(
        layer_grads_body,
        [
            like((width, ff_wide), low),
            like((width, ff_wide), low),
            like((ff_part // 2, width), low),
            like((ff_part // 2, width), low),
        ],
        [
            core_row.reshape(1),
            normed_two_all,
            grad_gate,
            grad_up,
            hidden,
            messages,
        ],
        "layer_grads",
        flops=6 * row_count * width * ff_part,
        limit=24,
        kept=(1, 2, 3, 4, 5),
    )
    tails = messages[:, width:]
    tails = jnp.stack([tails, partner(tails, "batch", far_mask)])
    tails_other = partner(tails, "batch", core_mask)
    head_blocks = -(-vrows // (block // 2))
    head_args = (far, near_part, rows, other, tails, tails_other, vrows, block // 2, 2)
    head_cut = -(-head_blocks * 3 // 10)
    grad_head, head_squares = head_grad(*head_args, 0, head_cut, ())
    normed_part, layer_grads, grad_head, head_squares = together(
        normed_part, layer_grads, grad_head, head_squares
    )
    gu_own, gu_send, down_own, down_send = layer_grads
    gu_other = partner(gu_send, "batch", core_mask)
    down_other = partner(down_send, "batch", core_mask)
    grad_one, grad_one_low, grad_gain_one = in_vmem(
        one_back_body,
        [like((n_picks, width)), like((n_picks, width), low), like((1, width))],
        [
            normed_part,
            stream_one,
            grad_two,
            gains[1:2],
        ],
        "second_norm_back",
        kept=(1, 2, 3),
    )
    kv_grad, query_pre, query_bias = in_vmem(
        attend_back_body,
        [
            like((length, 2 * kv_width), low),
            like((n_picks, q_width), low),
            like((1, q_width)),
        ],
        [grad_one_low, w_out_full, queries, kv_all, pick_places, attended, pick_cos, pick_sin],
        "attention_back",
        flops=10 * n_picks * q_width * length,
        exps=n_picks * H * length,
        limit=limit + 4,
        kept=(1, 2, 3, 4, 5, 6, 7),
        scratch=[pltpu.VMEM((n_picks, q_width), f32)],
    )
    def far_cut(value):
        return cut(value[..., 0, :, :], value[..., 1, :, :], "batch", far_mask)

    def far_sides(value):
        front, back = value[..., 0, :, :], value[..., 1, :, :]
        return jnp.where(on_far, back, front), jnp.where(on_far, front, back)

    gu_own, down_own, kv_grad = together(gu_own, down_own, kv_grad)
    own_parts = exchange(kv_grad.reshape(seq_count, local_len, 2 * kv_width), "seq")
    gu_parts = far_sides(total_of([gu_own, gu_other]).reshape(seq_count, 2, half, ff_wide))
    down_parts = far_sides(total_of([down_own, down_other]).reshape(2, -1, width))
    gu_parts, down_parts, rows_late = together(gu_parts, down_parts, rows)
    gu_parts = gu_parts[0], partner(gu_parts[1], "batch", far_mask)
    down_parts = down_parts[0], partner(down_parts[1], "batch", far_mask)
    grad_head, more_squares = head_grad(
        *head_args[:2], rows_late, *head_args[3:],
        head_cut, head_blocks - head_cut, (grad_head,),
    )
    late_rows = spread(jnp.concatenate([query_pre, grad_one_low], axis=0), "seq", stages[:-1])
    late_others = [partner(late_rows, "seq", mask) for mask in stages[-1]]
    own_parts, gu_parts, down_parts, grad_head, more_squares, late_rows, late_others = together(
        own_parts, gu_parts, down_parts, grad_head, more_squares, late_rows, late_others
    )
    kv_pre, sendback, grad_gain_zero, kv_bias = in_vmem(
        zero_back_body,
        [
            like((local_len, 2 * kv_width), low),
            like((owners * capacity, width), low),
            like((1, width)),
            like((1, 2 * kv_width)),
        ],
        [
            own_parts,
            slot_cos,
            slot_sin,
            w_kv_full,
            query_pre,
            w_q_full,
            picks,
            x_zero,
            gains[:1],
            grad_one,
            added,
            placer,
        ],
        "first_norm_back",
        kept=(1, 2, 3, 4, 5, 6, 7, 8, 9, 10, 11),
        flops=2 * local_len * width * (2 * kv_width + owners * capacity + 6 * n_picks),
    )
    gu_part, down_part_w = total_of(gu_parts), total_of(down_parts)

    grad_head, sendback = together(grad_head, sendback)
    arrived = exchange(sendback.reshape(owners, capacity, width), both)
    head_rows = grad_head.at[wanted].get(mode="promise_in_bounds")
    late_rows = jnp.concatenate([late_rows] + late_others)
    q_half = dot_tn(
        gathered_columns[:, :n_picks].reshape(row_count, shard),
        late_rows[:, :n_picks].reshape(row_count, q_width),
    )
    out_half = dot_tn(
        gathered_columns[:, n_picks:].reshape(row_count, shard),
        late_rows[:, n_picks:].reshape(row_count, width),
    )
    proj_part = halve(q_half.astype(low), out_half.astype(low), "batch", core_mask)
    proj_part = total_of(far_cut(proj_part.reshape(2, half, width)))
    kv_w_grad = dot_tn(normed_one, kv_pre).astype(low)
    kv_blocks = jnp.transpose(
        kv_w_grad.reshape(seq_count, 2, half, 2, kv_width), (1, 3, 0, 2, 4)
    ).reshape(batch_count, seq_count, half, kv_width)
    kv_blocks = xor_order(kv_blocks, "batch")
    kv_part = total_of(
        [kv_blocks[0]] + [partner(kv_blocks[at], "batch", at) for at in range(1, batch_count)]
    )
    kv_part = collect(to_xor_order(kv_part, "seq", stages), "seq", stages)
    own_squares = (
        squares_of(gu_part)
        + squares_of(down_part_w)
        + squares_of(proj_part)
        + squares_of(kv_part)
        + jnp.sum(head_squares[0])
        + jnp.sum(more_squares[0])
    )
    arrived, head_rows, own_squares, gu_part, down_part_w, proj_part, kv_part = together(
        arrived, head_rows, own_squares, gu_part, down_part_w, proj_part, kv_part
    )
    arrived = arrived.reshape(-1, width)
    row_squares = in_vmem(
        summary_body, [like((1, 1))], [arrived, head_rows, wanted[None]], "row_squares"
    )
    own_squares = own_squares + row_squares[0][0, 0]
    summary = jnp.concatenate(
        [
            grad_gain_zero[0],
            grad_gain_one[0],
            grad_gain_two[0],
            query_bias[0],
            kv_bias[0],
            jnp.stack([own_squares, loss_here[0, 0], jnp.sum(live)]),
            jnp.zeros((LANES - 3,), f32),
        ]
    ).reshape(-1, LANES)
    totals, stats = in_vmem(
        norm_body,
        [like(summary.shape), like((1, LANES))],
        [exchange_copies(summary, both)],
        "grad_norm",
    )
    totals = totals.reshape(-1)
    grad_gains = totals[: 3 * width].reshape(3, width)
    grad_bias_all = totals[3 * width : -LANES]
    loss_sum, token_count, grad_norm, factor = (stats[0, at] for at in range(4))

    block = 608
    blocks = -(-vrows // block)
    cuts = [0, -(-blocks * 3 // 8), -(-blocks * 6 // 8), blocks]

    def update_rows(at, held, first):
        return table_adam(
            after(factor.reshape(1), first),
            wanted[None],
            arrived,
            grad_head,
            embed,
            embed_m,
            embed_v,
            block,
            cuts[at],
            cuts[at + 1] - cuts[at],
            held,
        )

    def both_halves(value, axis, mask, at):
        return jnp.concatenate(double(value, axis, mask), axis=at)

    gu_rows = exchange(after(gu_part, factor), "seq")
    gu_rows, embed_new, down_part_w, proj_part, kv_part = together(
        gu_rows, update_rows(0, (), factor), down_part_w, proj_part, kv_part
    )
    gu_rows = jnp.transpose(gu_rows[..., :ff_part], (1, 0, 2)).reshape(half, FF)
    gu_far = both_halves(gu_rows, "batch", far_mask, 0)
    down_all = jnp.stack(double(down_part_w, "batch", far_mask), axis=0)
    small = both_halves(jnp.concatenate([proj_part, kv_part], axis=1), "batch", far_mask, 0)
    gu_far, down_all, small, embed_new = together(
        gu_far, down_all, small, update_rows(1, tuple(embed_new), gu_rows)
    )
    gu_all = both_halves(gu_far, "batch", core_mask, 1)
    down_all = jnp.stack(double(down_all, "batch", core_mask), axis=0).reshape(w_down.shape)
    first_small, second_small = double(small, "batch", core_mask)
    qkv_all = jnp.concatenate(
        [first_small[:, :width], first_small[:, width:], second_small[:, width:]], axis=1
    )
    out_all = second_small[:, :width]
    gu_all, down_all, qkv_all, out_all, embed_new = together(
        gu_all, down_all, qkv_all, out_all, update_rows(2, tuple(embed_new), gu_far)
    )

    def update(weight, moment, second, gradient, rate):
        return adam(weight, moment, second, gradient.astype(f32) * factor, rate, DECAY)

    qkv_new = update(w_qkv, w_qkv_m, w_qkv_v, qkv_all, LR_MATRIX)
    out_new = update(w_out, w_out_m, w_out_v, out_all, LR_OUT)
    gateup_new = update(w_gateup, w_gateup_m, w_gateup_v, gu_all, LR_MATRIX)
    down_new = update(w_down, w_down_m, w_down_v, down_all, LR_MATRIX)
    gains_new = adam(gains, gains_m, gains_v, grad_gains * factor, LR_GAIN, 0.0)
    bias_new = adam(bias, bias_m, bias_v, grad_bias_all * factor, LR_BIAS, 0.0)
    return (
        loss_sum,
        token_count,
        grad_norm,
        *embed_new,
        *qkv_new,
        *out_new,
        *gateup_new,
        *down_new,
        *gains_new,
        *bias_new,
    )


def solution(mesh):
    in_specs = (
        P("batch", "seq"),
        P(),
        P(),
        P("batch", "seq"),
        P("batch", "seq"),
        P("batch", "seq"),
        P(),
        P(("batch", "seq"), None),
        P(("batch", "seq"), None),
        P(("batch", "seq"), None),
        P("seq", None),
        P("seq", None),
        P("seq", None),
        P("seq", None),
        P("seq", None),
        P("seq", None),
        P("seq", None),
        P("seq", None),
        P("seq", None),
        P("seq", None),
        P("seq", None),
        P("seq", None),
        P(),
        P(),
        P(),
        P(),
        P(),
        P(),
    )
    out_specs = (
        P(),
        P(),
        P(),
        P(("batch", "seq"), None),
        P(("batch", "seq"), None),
        P(("batch", "seq"), None),
        P("seq", None),
        P("seq", None),
        P("seq", None),
        P("seq", None),
        P("seq", None),
        P("seq", None),
        P("seq", None),
        P("seq", None),
        P("seq", None),
        P("seq", None),
        P("seq", None),
        P("seq", None),
        P(),
        P(),
        P(),
        P(),
        P(),
        P(),
    )
    return jax.shard_map(
        per_device, mesh=mesh, in_specs=in_specs, out_specs=out_specs, check_vma=False
    )
```

```python
import functools

import jax
import jax.numpy as jnp
from jax import lax
from jax.experimental import pallas as pl
from jax.experimental.pallas import tpu as pltpu
from jax.sharding import PartitionSpec as P

H = 14
KV = 2
HD = 64
FF = 4864
STEP = 5


NORM_EPS = 1e-06
ROPE_BASE = 1000000.0
NEG_BIG = -1e30
EPS_LOW = 0.8
EPS_HIGH = 0.28
BETA_KL = 0.1
CLIP_NORM = 0.05
BETA_ONE = 0.9
BETA_TWO = 0.95
ADAM_EPS = 1e-08
DECAY = 0.1
LR_MATRIX = 0.02
LR_OUT = 0.12
LR_GAIN = 1.0
LR_BIAS = 0.5


def norm_rows(values, gain):
    return values * lax.rsqrt(jnp.mean(values * values, axis=-1, keepdims=True) + NORM_EPS) * gain


def partner(value, axis, mask):
    size = lax.axis_size(axis)
    return lax.ppermute(value, axis, [(place, place ^ mask) for place in range(size)])


def masks_of(size):
    masks, mask = [], 1
    while mask < size:
        masks.append(mask)
        mask *= 2
    return masks


def bit_of(axis, mask):
    return (lax.axis_index(axis) & mask) != 0


def xor_order(blocks, axis):
    bits = masks_of(blocks.shape[0])
    held = blocks.reshape((2,) * len(bits) + blocks.shape[1:])
    for at, bit in enumerate(reversed(bits)):
        held = jnp.where(bit_of(axis, bit), jnp.flip(held, at), held)
    return held.reshape(blocks.shape)


def after(value, *first):
    return lax.optimization_barrier((value, first))[0]


def together(*values):
    return lax.optimization_barrier(values)


def seq_stages_of(size):
    bits = masks_of(size)
    stages, rest = [], bits[1:]
    while rest:
        pair, rest = rest[:2], rest[2:]
        stages.append([pair[0], pair[1], pair[0] ^ pair[1]] if len(pair) == 2 else pair)
    return stages + [bits[:1]]


def spread(value, axis, stages):
    held = value[None]
    for masks in stages:
        held = jnp.concatenate([held] + [partner(held, axis, mask) for mask in masks])
    return held


def to_xor_order(blocks, axis, stages):
    bits = masks_of(blocks.shape[0])
    turned = xor_order(blocks, axis).reshape((2,) * len(bits) + blocks.shape[1:])
    place = {bit: at for at, bit in enumerate(reversed(bits))}
    order = [place[mask] for masks in reversed(stages) for mask in reversed(masks) if mask in bits]
    rest = list(range(len(bits), turned.ndim))
    return jnp.transpose(turned, order + rest).reshape(blocks.shape)


def to_index_order(blocks, axis, stages):
    bits = masks_of(blocks.shape[0])
    place = {bit: at for at, bit in enumerate(reversed(bits))}
    order = [place[mask] for masks in reversed(stages) for mask in reversed(masks) if mask in bits]
    back = [order.index(at) for at in range(len(bits))]
    held = blocks.reshape((2,) * len(bits) + blocks.shape[1:])
    held = jnp.transpose(held, back + list(range(len(bits), held.ndim)))
    return xor_order(held.reshape(blocks.shape), axis)


def exchange(value, axes):
    return lax.all_to_all(value, axes, split_axis=0, concat_axis=0, tiled=True)


def exchange_copies(value, axes):
    size = lax.axis_size(axes)
    return exchange(jnp.broadcast_to(value[None], (size,) + value.shape), axes)


def total_of(parts):
    total = parts[0].astype(jnp.float32)
    for part in parts[1:]:
        total = total + part.astype(jnp.float32)
    return total.astype(jnp.bfloat16)


def cut(first, second, axis, mask):
    own = bit_of(axis, mask)
    return jnp.where(own, second, first), partner(jnp.where(own, first, second), axis, mask)


def halve(first, second, axis, mask):
    return total_of(cut(first, second, axis, mask))


def collect(blocks, axis, stages):
    held = blocks
    for masks in reversed(stages):
        count = len(masks) + 1
        held = held.reshape((count, held.shape[0] // count) + held.shape[1:])
        held = total_of(
            [held[0]] + [partner(held[at + 1], axis, mask) for at, mask in enumerate(masks)]
        )
    return held[0]


def ordered(value, other, axis, mask):
    own = bit_of(axis, mask)
    return jnp.where(own, other, value), jnp.where(own, value, other)


def double(value, axis, mask):
    return ordered(value, partner(value, axis, mask), axis, mask)


def dot_nn(left, right):
    return jnp.dot(left, right, preferred_element_type=jnp.float32)


def dot_tn(left, right):
    return lax.dot_general(
        left, right, (((0,), (0,)), ((), ())), preferred_element_type=jnp.float32
    )


def dot_nt(left, right):
    return lax.dot_general(
        left, right, (((1,), (1,)), ((), ())), preferred_element_type=jnp.float32
    )


def squares_of(value):
    value = value.astype(jnp.float32)
    return jnp.sum(value * value)


def adam(weight, moment, second, gradient, learn_rate, decay_rate):
    moment = BETA_ONE * moment + (1.0 - BETA_ONE) * gradient
    second = BETA_TWO * second + (1.0 - BETA_TWO) * gradient * gradient
    corrected = moment / (1.0 - BETA_ONE**STEP)
    scaled = second / (1.0 - BETA_TWO**STEP)
    return (
        weight - learn_rate * (corrected / (jnp.sqrt(scaled) + ADAM_EPS) + decay_rate * weight),
        moment,
        second,
    )


LOW = jnp.bfloat16
F32 = jnp.float32
LANES = 128


def iota(shape, dim):
    return lax.broadcasted_iota(jnp.int32, shape, dim)


def in_hbm(*arrays):
    return tuple(pltpu.with_memory_space_constraint(array, pltpu.HBM) for array in arrays)


def like(shape, dtype=jnp.float32):
    return jax.ShapeDtypeStruct(shape, dtype)


def in_vmem(body, outs, args, name, flops=0, exps=0, limit=16, kept=(), scratch=()):
    moved = sum(a.size * a.dtype.itemsize for a in args) + sum(
        o.size * o.dtype.itemsize for o in outs
    )
    whole = lambda rank: lambda step: (0,) * rank
    near = pl.BlockSpec(memory_space=pltpu.VMEM)
    return pl.pallas_call(
        body,
        grid=(1,),
        in_specs=[
            pl.BlockSpec(a.shape, whole(a.ndim)) if at in kept else near
            for at, a in enumerate(args)
        ],
        out_specs=[near] * len(outs),
        out_shape=outs,
        scratch_shapes=scratch,
        compiler_params=pltpu.CompilerParams(vmem_limit_bytes=limit * 2**20),
        cost_estimate=pl.CostEstimate(flops=flops, bytes_accessed=moved, transcendentals=exps),
        name=name,
    )(*[in_hbm(a)[0] if at in kept else a for at, a in enumerate(args)])


def upright(row):
    count = row.shape[1]
    square = jnp.broadcast_to(row.astype(F32), (count, count))
    return jnp.sum(
        jnp.where(iota((count, count), 0) == iota((count, count), 1), square, 0.0),
        axis=1,
        keepdims=True,
    )


def turned(values, cosine, sine):
    tiles = []
    for at in range(0, values.shape[1], LANES):
        tile = values[:, at : at + LANES]
        front = iota(tile.shape, 1) % HD < HD // 2
        swapped = jnp.where(
            front, pltpu.roll(tile, LANES - HD // 2, 1), pltpu.roll(tile, HD // 2, 1)
        )
        tiles.append(tile * cosine + swapped * sine)
    return tiles[0] if len(tiles) == 1 else jnp.concatenate(tiles, axis=1)


def norm_back(values, gain, grad):
    inverse = lax.rsqrt(jnp.mean(values * values, axis=-1, keepdims=True) + NORM_EPS)
    scaled = grad * gain
    inner = jnp.mean(values * scaled, axis=-1, keepdims=True)
    into = inverse * scaled - values * (inverse * inverse * inverse * inner)
    return into, jnp.sum(grad * values * inverse, axis=0, keepdims=True)


def placed(pick_columns, values):
    high = values.astype(LOW)
    rest = (values - high.astype(F32)).astype(LOW)
    return dot_nn(pick_columns, high) + dot_nn(pick_columns, rest)


def coded(value):
    high = value.astype(LOW).astype(F32)
    middle = (value - high).astype(LOW).astype(F32)
    return high, middle, (value - high - middle).astype(LOW).astype(F32)


def coded_lanes(columns):
    parts = [part for column in columns for part in coded(column)]
    lane = iota((columns[0].shape[0], LANES), 1)
    tail = jnp.zeros(lane.shape, F32)
    for at, part in enumerate(parts):
        tail = jnp.where(lane == at, part, tail)
    return tail.astype(LOW)


def decoded(tail, at):
    tail = tail.astype(F32)
    lane = iota(tail.shape, tail.ndim - 1)
    return jnp.sum(
        jnp.where((lane >= 3 * at) & (lane < 3 * at + 3), tail, 0.0), axis=-1, keepdims=True
    )


def request_body(vrows, capacity, tokens_ref, requests_ref, placer_ref):
    row = tokens_ref[...].astype(F32)
    column = upright(tokens_ref[...])
    count = row.shape[1]
    owner_row = jnp.floor((row + 0.5) / vrows)
    owner = jnp.floor((column + 0.5) / vrows)
    earlier = (owner == owner_row) & (iota((count, count), 1) < iota((count, count), 0))
    slot = jnp.sum(jnp.where(earlier, 1.0, 0.0), axis=1, keepdims=True)
    hit = (owner * capacity + slot) == iota(placer_ref.shape, 1).astype(F32)
    placer_ref[...] = jnp.where(hit, 1.0, 0.0).astype(LOW)
    requests_ref[...] = jnp.sum(
        jnp.where(hit, column - owner * vrows, 0.0), axis=0, keepdims=True
    ).astype(jnp.int32)


def embed_body(
    rows_ref, placer_ref, w_ref, bias_ref, gain_ref, cos_ref, sin_ref, x_ref, normed_ref, kv_ref
):
    x_zero = dot_nn(placer_ref[...], rows_ref[...])
    x_ref[...] = x_zero.astype(LOW)
    normed = norm_rows(x_zero, gain_ref[...]).astype(LOW)
    normed_ref[...] = normed
    kv = dot_nn(normed, w_ref[...]) + bias_ref[...]
    width = KV * HD
    keys = turned(kv[:, :width], cos_ref[...], sin_ref[...]).astype(LOW)
    values = kv[:, width:].astype(LOW)
    for at in range(kv_ref.shape[0]):
        kv_ref[at, :, :width] = keys
        kv_ref[at, :, width:] = values


def pick_columns_of(picks, slots, shift):
    return jnp.where(
        iota((slots, picks.shape[1]), 0) == picks + shift, 1.0, 0.0
    ).astype(LOW)


def pick_body(
    x_ref, normed_ref, picks_ref, w_ref, bias_ref, cos_ref, sin_ref,
    picked_ref, target_ref, picked_normed_ref, query_ref,
):
    slots = x_ref.shape[0]
    here = pick_columns_of(picks_ref[...], slots, 0)
    after = pick_columns_of(picks_ref[...], slots, 1)
    picked_ref[...] = dot_tn(here, x_ref[...])
    target_ref[...] = dot_tn(after, x_ref[...])
    normed = dot_tn(here, normed_ref[...]).astype(LOW)
    picked_normed_ref[...] = normed
    query = dot_nn(normed, w_ref[...]) + bias_ref[...]
    query_ref[...] = turned(query, cos_ref[...], sin_ref[...]).astype(LOW)


def stacked_heads(values, first, count):
    return jnp.concatenate(
        [values[:, (first + at) * HD : (first + at + 1) * HD] for at in range(count)], axis=0
    )


CHUNK = 2048


def scores_of(queries, keys, places, count, start):
    scores = dot_nt(queries, keys) * HD ** (-0.5)
    reach = jnp.concatenate([places] * count, axis=0) - start
    return jnp.where(iota(scores.shape, 1) <= reach, scores, NEG_BIG)


def key_slices(kv_ref, head, start, size):
    rows = pl.ds(start, size)
    return (
        kv_ref[rows, head * HD : (head + 1) * HD],
        kv_ref[rows, (KV + head) * HD : (KV + head + 1) * HD],
    )


def over_keys(length, body, carry):
    if length <= CHUNK:
        return body(0, carry)
    return lax.fori_loop(
        0, length // CHUNK, lambda at, held: body(pl.multiple_of(at * CHUNK, CHUNK), held), carry
    )


def softmax_parts(queries, kv_ref, head, places, count):
    length = kv_ref.shape[0]
    size = min(length, CHUNK)
    if length <= CHUNK:

        def chances(start):
            scores = scores_of(queries, key_slices(kv_ref, head, 0, size)[0], places, count, 0)
            raised = jnp.exp(scores - jnp.max(scores, axis=1, keepdims=True))
            return raised * (1.0 / jnp.sum(raised, axis=1, keepdims=True))

        return chances

    def statistics(start, held):
        top, summed = held
        keys = key_slices(kv_ref, head, start, size)[0]
        scores = scores_of(queries, keys, places, count, start)
        now = jnp.maximum(top, jnp.max(scores, axis=1, keepdims=True))
        raised = jnp.exp(scores - now)
        return now, summed * jnp.exp(top - now) + jnp.sum(raised, axis=1, keepdims=True)

    rows = queries.shape[0]
    top, summed = over_keys(
        length, statistics, (jnp.full((rows, 1), NEG_BIG, F32), jnp.zeros((rows, 1), F32))
    )

    def chances_at(start):
        keys = key_slices(kv_ref, head, start, size)[0]
        return jnp.exp(scores_of(queries, keys, places, count, start) - top) * (1.0 / summed)

    return chances_at


def attend_body(
    query_ref, kv_ref, place_ref, w_ref, picked_ref, gain_ref,
    mixed_ref, attended_ref, one_ref, normed_ref,
):
    places = upright(place_ref[...]).astype(jnp.int32)
    picks = places.shape[0]
    group = H // KV
    length = kv_ref.shape[0]
    size = min(length, CHUNK)
    for head in range(KV):
        queries = stacked_heads(query_ref[...], head * group, group)
        chances = softmax_parts(queries, kv_ref, head, places, group)

        def add(start, total):
            values = key_slices(kv_ref, head, start, size)[1]
            return total + dot_nn(chances(start).astype(LOW), values)

        out = over_keys(length, add, jnp.zeros(queries.shape, F32))
        for at in range(group):
            spot = (head * group + at) * HD
            attended_ref[:, spot : spot + HD] = out[at * picks : (at + 1) * picks]
    mixed = attended_ref[...].astype(LOW)
    mixed_ref[...] = mixed
    one = picked_ref[...] + dot_nn(mixed, w_ref[...])
    one_ref[...] = one
    normed = norm_rows(one, gain_ref[...]).astype(LOW)
    for at in range(normed_ref.shape[0]):
        normed_ref[at] = normed


def feed_body(normed_ref, gate_w_ref, up_w_ref, down_w_ref, gate_ref, up_ref, hidden_ref, out_ref):
    normed = normed_ref[...]
    gate = dot_nn(normed, gate_w_ref[...])
    up = dot_nn(normed, up_w_ref[...])
    gate_ref[...] = gate
    up_ref[...] = up
    hidden = (gate * (1.0 / (1.0 + jnp.exp(-gate))) * up).astype(LOW)
    hidden_ref[...] = hidden
    out_ref[...] = dot_nn(hidden, down_w_ref[...]).astype(LOW)


def feed_sum_body(parts_ref, one_ref, gain_ref, two_ref, final_ref):
    two = one_ref[...] + jnp.sum(parts_ref[...].astype(F32), axis=0)
    two_ref[...] = two
    final_ref[...] = norm_rows(two, gain_ref[...]).astype(LOW)


def head_body(
    vrows, rows_ref, other_ref, table_ref, raised_ref, tops_ref, own_ref, send_ref, top, summed, total
):
    step = pl.program_id(0)
    block = table_ref.shape[0]
    width = table_ref.shape[1]
    half = own_ref.shape[0]

    @pl.when(step == 0)
    def _():
        top[...] = jnp.full(top.shape, NEG_BIG, F32)
        summed[...] = jnp.zeros(summed.shape, F32)
        total[...] = jnp.zeros(total.shape, F32)

    left = vrows - step * block
    entries = jnp.where(iota((block, 1), 0) < left, table_ref[...], 0.0).astype(LOW)
    inside = iota((1, block), 1) < left
    part = min(256, half)
    pieces = []
    for ref, start in ((rows_ref, 0), (other_ref, half)):
        tokens = ref[...].reshape(half, width)
        pieces += [
            (slice(start + at, start + at + part), tokens[at : at + part])
            for at in range(0, half, part)
        ]
    logits_of = [dot_nt(tokens, entries) for _, tokens in pieces]
    for (piece, _), logits in zip(pieces, logits_of):
        logits = jnp.where(inside, logits, NEG_BIG)
        before = top[piece, :1]
        now = jnp.maximum(before, jnp.max(logits, axis=1, keepdims=True))
        raised = jnp.exp(logits - now)
        shrink = jnp.exp(before - now)
        low = raised.astype(LOW)
        raised_ref[piece] = low
        summed[piece] = summed[piece] * shrink + jnp.sum(raised, axis=1, keepdims=True)
        total[piece] = total[piece] * shrink + dot_nn(low, entries)
        top[piece] = jnp.broadcast_to(now, (part, LANES))
        column = iota((part, LANES), 1) == step
        tops_ref[piece] = jnp.where(column, now, tops_ref[piece])

    @pl.when(step == pl.num_programs(0) - 1)
    def _():
        for ref, at in ((own_ref, 0), (send_ref, half)):
            here = slice(at, at + half)
            ref[:, :width] = (total[here] / summed[here, :1]).astype(LOW)
            ref[:, width:] = coded_lanes([top[here, :1] + jnp.log(summed[here, :1])])


def head_part(rows, other, group, table, block):
    seqs, _, picks, width = rows.shape
    half = seqs * picks
    vrows = table.shape[0]
    steps = -(-vrows // block)
    whole = lambda step: (0, 0)
    states = pl.BlockSpec((seqs, 1, picks, width), lambda step: (0, group, 0, 0))
    mean = pl.BlockSpec((half, width + LANES), whole)
    return pl.pallas_call(
        functools.partial(head_body, vrows),
        grid=(steps,),
        in_specs=[states, states, pl.BlockSpec((block, width), lambda step: (step, 0))],
        out_specs=[
            pl.BlockSpec((2 * half, block), lambda step: (0, step)),
            pl.BlockSpec((2 * half, LANES), whole),
            mean,
            mean,
        ],
        out_shape=[
            pltpu.HBM((2 * half, steps * block), LOW),
            like((2 * half, LANES)),
            like((half, width + LANES), LOW),
            like((half, width + LANES), LOW),
        ],
        scratch_shapes=[
            pltpu.VMEM((2 * half, LANES), F32),
            pltpu.VMEM((2 * half, LANES), F32),
            pltpu.VMEM((2 * half, width), F32),
        ],
        compiler_params=pltpu.CompilerParams(vmem_limit_bytes=(28 if half <= 256 else 60) * 2**20),
        cost_estimate=pl.CostEstimate(
            flops=8 * half * vrows * width,
            bytes_accessed=vrows * width * 4 + half * vrows * 4,
            transcendentals=2 * half * vrows,
        ),
        name="head_part",
    )(rows, other, *in_hbm(table))


def merge_values(parts):
    highest = parts[0][1]
    for _, log in parts[1:]:
        highest = jnp.maximum(highest, log)
    summed, total = 0.0, 0.0
    for mean, log in parts:
        share = jnp.exp(log - highest)
        summed = summed + share
        total = total + share * mean
    return total * (1.0 / summed), highest + jnp.log(summed)


def merge_body(*refs):
    out_ref = refs[-1]
    width = out_ref.shape[1] - LANES
    mean, log = merge_values(
        [(ref[:, :width].astype(F32), decoded(ref[:, width:], 0)) for ref in refs[:-1]]
    )
    out_ref[:, :width] = mean.astype(LOW)
    out_ref[:, width:] = coded_lanes([log])


def loss_body(
    parts_ref, final_ref, target_ref, two_ref, gain_ref, live_ref, old_ref, ref_ref, advantage_ref,
    message_ref, grad_ref, gain_grad_ref, added_ref, loss_ref,
):
    width = final_ref.shape[1]
    mean, log_total = merge_values(
        [
            (parts_ref[at, :, :width].astype(F32), decoded(parts_ref[at, :, width:], 0))
            for at in range(parts_ref.shape[0])
        ]
    )
    final = final_ref[...].astype(F32)
    target = target_ref[...]
    live = upright(live_ref[...])
    to_ref = jnp.sum(final * target, axis=1, keepdims=True) - log_total
    logp = to_ref
    to_ref = logp - upright(ref_ref[...])
    advantage = advantage_ref[...]
    weight = jnp.clip(jnp.exp(logp - upright(old_ref[...])), 1.0 - EPS_LOW, 1.0 + EPS_HIGH)
    coefficient = live * (-weight * advantage + BETA_KL * to_ref)
    loss = live * (-weight * advantage * logp + 0.5 * BETA_KL * to_ref * to_ref)
    loss_ref[...] = jnp.broadcast_to(jnp.sum(loss, axis=0, keepdims=True), loss_ref.shape)
    added_ref[...] = coefficient * final
    grad, gain_grad_ref[...] = norm_back(
        two_ref[...], gain_ref[...], coefficient * (target - mean)
    )
    grad_ref[...] = grad
    low = grad.astype(LOW)
    tail = coded_lanes([log_total, coefficient])
    for at in range(message_ref.shape[0]):
        message_ref[at, :, :width] = low
        message_ref[at, :, width:] = tail


def feed_back_body(
    message_ref, hidden_ref, gate_ref, up_ref, gate_w_ref, up_w_ref, down_w_ref,
    grad_gate_ref, grad_up_ref, out_ref,
):
    width = out_ref.shape[1]
    grad_hidden = dot_nt(message_ref[:, :width], down_w_ref[...])
    gate = gate_ref[...]
    up = up_ref[...]
    sigmoid = 1.0 / (1.0 + jnp.exp(-gate))
    grad_gate = (grad_hidden * up * sigmoid * (1.0 + gate * (1.0 - sigmoid))).astype(LOW)
    grad_up = (grad_hidden * gate * sigmoid).astype(LOW)
    grad_gate_ref[...] = grad_gate
    grad_up_ref[...] = grad_up
    out_ref[...] = (
        dot_nt(grad_gate, gate_w_ref[...]) + dot_nt(grad_up, up_w_ref[...])
    ).astype(LOW)


def one_back_body(parts_ref, one_ref, grad_two_ref, gain_ref, grad_ref, low_ref, gain_grad_ref):
    into, gain_grad_ref[...] = norm_back(
        one_ref[...], gain_ref[...], jnp.sum(parts_ref[...].astype(F32), axis=0)
    )
    grad = grad_two_ref[...] + into
    grad_ref[...] = grad
    low_ref[...] = grad.astype(LOW)


def attend_back_body(
    grad_ref, w_ref, query_ref, kv_ref, place_ref, attended_ref, cos_ref, sin_ref,
    kv_grad_ref, query_pre_ref, bias_ref, query_grad,
):
    places = upright(place_ref[...]).astype(jnp.int32)
    picks = places.shape[0]
    into = dot_nt(grad_ref[...], w_ref[...]).astype(LOW)
    group = H // KV
    length = kv_ref.shape[0]
    size = min(length, CHUNK)
    for head in range(KV):
        queries = stacked_heads(query_ref[...], head * group, group)
        grads = stacked_heads(into, head * group, group)
        inner = jnp.sum(
            grads.astype(F32) * stacked_heads(attended_ref[...], head * group, group),
            axis=1,
            keepdims=True,
        )
        chances = softmax_parts(queries, kv_ref, head, places, group)

        def add(start, total):
            keys, values = key_slices(kv_ref, head, start, size)
            chance = chances(start)
            scores = (chance * (dot_nt(grads, values) - inner)).astype(LOW)
            rows = pl.ds(start, size)
            kv_grad_ref[rows, head * HD : (head + 1) * HD] = (
                dot_tn(scores, queries) * HD ** (-0.5)
            ).astype(LOW)
            kv_grad_ref[rows, (KV + head) * HD : (KV + head + 1) * HD] = dot_tn(
                chance.astype(LOW), grads
            ).astype(LOW)
            return total + dot_nn(scores, keys) * HD ** (-0.5)

        query_part = over_keys(length, add, jnp.zeros(queries.shape, F32))
        for at in range(group):
            spot = (head * group + at) * HD
            query_grad[:, spot : spot + HD] = query_part[at * picks : (at + 1) * picks]
    query_pre = turned(query_grad[...], cos_ref[...], -sin_ref[...]).astype(LOW)
    query_pre_ref[...] = query_pre
    bias_ref[...] = jnp.sum(query_pre.astype(F32), axis=0, keepdims=True)


def zero_back_body(
    parts_ref, cos_ref, sin_ref, kv_w_ref, query_pre_ref, q_w_ref, picks_ref, x_ref, gain_ref,
    grad_one_ref, added_ref, placer_ref,
    kv_pre_ref, back_ref, gain_grad_ref, bias_ref,
):
    width = KV * HD
    slots = x_ref.shape[0]
    own = jnp.sum(parts_ref[...].astype(F32), axis=0)
    kv_pre_ref[:, :width] = turned(own[:, :width], cos_ref[...], -sin_ref[...]).astype(LOW)
    kv_pre_ref[:, width:] = own[:, width:].astype(LOW)
    kv_pre = kv_pre_ref[...]
    bias_ref[...] = jnp.sum(kv_pre.astype(F32), axis=0, keepdims=True)
    here = pick_columns_of(picks_ref[...], slots, 0)
    after = pick_columns_of(picks_ref[...], slots, 1)
    grad_normed = dot_nt(kv_pre, kv_w_ref[...]) + placed(
        here, dot_nt(query_pre_ref[...], q_w_ref[...])
    )
    into, gain_grad_ref[...] = norm_back(x_ref[...].astype(F32), gain_ref[...], grad_normed)
    grad = into + placed(here, grad_one_ref[...]) + placed(after, added_ref[...])
    back_ref[...] = dot_tn(placer_ref[...], grad.astype(LOW)).astype(LOW)


def layer_grads_body(
    core_ref, normed_ref, gate_ref, up_ref, hidden_ref, message_ref,
    own_ref, send_ref, own_down_ref, send_down_ref,
):
    second = core_ref[0] > 0
    gate, up = gate_ref[...], up_ref[...]
    normed = normed_ref[...]
    own_ref[...] = dot_tn(normed, jnp.where(second, up, gate)).astype(LOW)
    send_ref[...] = dot_tn(normed, jnp.where(second, gate, up)).astype(LOW)
    half = own_down_ref.shape[0]
    grads = message_ref[:, : own_down_ref.shape[1]]
    front, back = hidden_ref[:, :half], hidden_ref[:, half : 2 * half]
    own_down_ref[...] = dot_tn(jnp.where(second, back, front), grads).astype(LOW)
    send_down_ref[...] = dot_tn(jnp.where(second, front, back), grads).astype(LOW)


def summary_body(arrived_ref, rows_ref, names_ref, out_ref):
    arrived = arrived_ref[...]
    names = names_ref[...].astype(F32)
    cross = jnp.sum(arrived.astype(F32) * rows_ref[...].astype(F32), axis=0, keepdims=True)
    same = jnp.where(upright(names_ref[...]) == names, dot_nt(arrived, arrived), 0.0)
    out_ref[...] = 2.0 * jnp.sum(cross, axis=1, keepdims=True) + jnp.sum(
        jnp.sum(same, axis=0, keepdims=True), axis=1, keepdims=True
    )


def norm_body(parts_ref, totals_ref, stats_ref):
    totals = jnp.sum(parts_ref[...], axis=0)
    totals_ref[...] = totals
    last = totals.shape[0] - 1
    own = totals[last:]
    lane = iota(own.shape, 1)

    def entry(at):
        return jnp.sum(jnp.where(lane == at, own, 0.0), axis=1, keepdims=True)

    others = jnp.where(iota(totals.shape, 0) < last, totals * totals, 0.0)
    squares = entry(0) + jnp.sum(
        jnp.sum(others, axis=0, keepdims=True), axis=1, keepdims=True
    )
    count = jnp.maximum(entry(2), 1.0)
    norm = jnp.sqrt(squares) / count
    factor = jnp.minimum(1.0, CLIP_NORM / (norm + 1e-06)) / count
    out = jnp.where(lane == 0, entry(1), jnp.where(lane == 1, count, norm))
    stats_ref[...] = jnp.where(lane == 3, factor, out)


def head_grad_body(
    span, first, far_ref, near_ref, far_tops_ref, near_tops_ref, rows_ref, other_ref, tails_ref, tails_other_ref,
    grad_ref, squares_ref,
):
    step = pl.program_id(0)
    block = step + first
    width = grad_ref.shape[1]
    half = far_ref.shape[0] // 2
    grad = 0.0
    for group, raised_ref, tops_ref in ((1, far_ref, far_tops_ref), (0, near_ref, near_tops_ref)):
        for at, (states_ref, tail_ref) in enumerate(
            ((rows_ref, tails_ref), (other_ref, tails_other_ref))
        ):
            here = slice(at * half, (at + 1) * half)
            tops = tops_ref[here]
            top = jnp.sum(
                jnp.where(iota(tops.shape, 1) == block // span, tops, 0.0), axis=1, keepdims=True
            )
            tail = tail_ref[group]
            scale = -decoded(tail, 1) * jnp.exp(top - decoded(tail, 0))
            states = states_ref[:, group].reshape(half, width).astype(F32)
            grad = grad + dot_tn(raised_ref[here], (states * scale).astype(LOW))
    grad_ref[...] = grad.astype(LOW)

    @pl.when(step == 0)
    def _():
        squares_ref[...] = jnp.zeros(squares_ref.shape, F32)

    squares_ref[...] += jnp.sum(grad * grad, axis=0, keepdims=True)


def head_grad(far, near, rows, other, tails, tails_other, vrows, block, span, first, steps, held):
    width = rows.shape[-1]
    tokens = far[0].shape[0]
    whole = lambda count: lambda step: (0,) * count
    raised = pl.BlockSpec((tokens, block), lambda step: (0, step + first))
    fixed = lambda array: pl.BlockSpec(array.shape, whole(array.ndim))
    return pl.pallas_call(
        lambda *refs: head_grad_body(span, first, *refs[:8], *refs[-2:]),
        grid=(steps,),
        in_specs=[
            raised,
            raised,
            fixed(far[1]),
            fixed(near[1]),
            fixed(rows),
            fixed(other),
            fixed(tails),
            fixed(tails_other),
        ]
        + [pl.BlockSpec(memory_space=pl.ANY)] * len(held),
        out_specs=[
            pl.BlockSpec((block, width), lambda step: (step + first, 0)),
            pl.BlockSpec((8, width), whole(2)),
        ],
        out_shape=[pltpu.HBM((vrows, width), LOW), like((8, width))],
        input_output_aliases={8 + at: at for at in range(len(held))},
        compiler_params=pltpu.CompilerParams(vmem_limit_bytes=(28 if tokens <= 512 else 60) * 2**20),
        cost_estimate=pl.CostEstimate(
            flops=4 * tokens * steps * block * width,
            bytes_accessed=steps * block * (4 * tokens + 2 * width),
            transcendentals=0,
        ),
        name="head_grad",
    )(*in_hbm(far[0], near[0], far[1], near[1], rows, other, tails, tails_other), *held)


def table_adam_body(first, scale_ref, names_ref, added_ref, grad_ref, w_ref, m_ref, v_ref, *refs):
    w_out, m_out, v_out = refs[-3:]
    rows = grad_ref.shape[0]
    here = iota((rows, names_ref.shape[1]), 0) + (pl.program_id(0) + first) * rows
    picker = jnp.where(here == names_ref[...], 1.0, 0.0).astype(LOW)
    grad = grad_ref[...].astype(F32) + dot_nn(picker, added_ref[...])
    w_out[...], m_out[...], v_out[...] = adam(
        w_ref[...], m_ref[...], v_ref[...], grad * scale_ref[0], LR_MATRIX, DECAY
    )


def table_adam(scale, names, added, grad, weight, moment, second, rows, first, steps, held):
    vrows, width = weight.shape
    whole = lambda step: (0, 0)
    here = pl.BlockSpec((rows, width), lambda step: (step + first, 0))
    return pl.pallas_call(
        functools.partial(table_adam_body, first),
        grid=(steps,),
        in_specs=[
            pl.BlockSpec(memory_space=pltpu.SMEM),
            pl.BlockSpec((1, names.shape[1]), whole),
            pl.BlockSpec(added.shape, whole),
            here,
            here,
            here,
            here,
        ]
        + [pl.BlockSpec(memory_space=pl.ANY)] * len(held),
        out_specs=[here, here, here],
        out_shape=[pltpu.HBM((vrows, width), F32)] * 3,
        input_output_aliases={7 + at: at for at in range(len(held))},
        compiler_params=pltpu.CompilerParams(vmem_limit_bytes=44 * 2**20),
        cost_estimate=pl.CostEstimate(
            flops=2 * names.shape[1] * steps * rows * width,
            bytes_accessed=steps * rows * width * 26,
            transcendentals=steps * rows * width,
        ),
        name="table_adam",
    )(scale, names, added, *in_hbm(grad, weight, moment, second), *held)


def per_device(
    token_ids,
    row_lengths,
    prompt_lengths,
    picks,
    old_logp,
    ref_logp,
    rewards,
    embed,
    embed_m,
    embed_v,
    w_qkv,
    w_qkv_m,
    w_qkv_v,
    w_out,
    w_out_m,
    w_out_v,
    w_gateup,
    w_gateup_m,
    w_gateup_v,
    w_down,
    w_down_m,
    w_down_v,
    gains,
    gains_m,
    gains_v,
    bias,
    bias_m,
    bias_v,
):
    both = ("batch", "seq")
    owners = lax.axis_size(both)
    seq_index = lax.axis_index("seq")
    row_index = lax.axis_index("batch")
    batch_count = lax.axis_size("batch")
    seq_count = lax.axis_size("seq")
    core_mask, far_mask = 1, 2
    on_core, on_far = bit_of("batch", core_mask), bit_of("batch", far_mask)
    low = LOW
    f32 = F32
    local_len = token_ids.shape[1]
    vrows, width = embed.shape
    shard = w_qkv.shape[0]
    half = shard // 2
    ff_part = FF // seq_count
    ff_wide = -(-ff_part // LANES) * LANES
    capacity = max(2, 2 * local_len // owners)
    kv_width = KV * HD
    q_width = H * HD
    n_picks = picks.shape[1]
    row_count = seq_count * n_picks

    requests, placer = in_vmem(
        functools.partial(request_body, vrows, capacity),
        [like((1, owners * capacity), jnp.int32), like((local_len, owners * capacity), low)],
        [token_ids],
        "requests",
    )
    sent_requests = exchange(requests.reshape(owners, capacity), both)

    stages = seq_stages_of(seq_count)
    core_row = lax.axis_index("batch") & core_mask
    qkv_cut = -(-(q_width + 2 * kv_width) // (2 * LANES)) * LANES
    out_cut = -(-width // (2 * LANES)) * LANES

    def part_of(value, columns):
        start = jnp.where(on_core, value.shape[1] - columns, 0)
        return lax.dynamic_slice(value, (jnp.where(on_far, half, 0), start), (half, columns)).astype(low)

    def widened(value):
        return jnp.pad(value, [(0, 0)] * (value.ndim - 1) + [(0, ff_wide - ff_part)])

    proj_parts = spread(
        jnp.concatenate([part_of(w_qkv, qkv_cut), part_of(w_out, out_cut)], axis=1),
        "seq",
        stages[:-1],
    )
    my_kv = lax.dynamic_slice(
        w_qkv, (0, jnp.where(on_core, q_width + kv_width, q_width)), (shard, kv_width)
    ).astype(low)
    my_kv = jnp.concatenate([my_kv[:half], my_kv[half:]], axis=1)
    pieces = jnp.transpose(part_of(w_gateup, FF).reshape(half, seq_count, ff_part), (1, 0, 2))
    pieces = jnp.concatenate(
        [widened(pieces), jnp.broadcast_to(my_kv[None], (seq_count,) + my_kv.shape)], axis=2
    )
    w_down_low = jnp.pad(w_down.astype(low), ((0, ff_wide - ff_part), (0, 0)))
    sent_requests, pieces, w_down_low, proj_parts = together(
        sent_requests, pieces, w_down_low, proj_parts
    )
    proj_others = [partner(proj_parts, "seq", mask) for mask in stages[-1]]

    def far_rows(value):
        return jnp.stack(double(value, "batch", far_mask), axis=1).reshape(width, -1)

    def core_columns(value, whole):
        first, second = double(value, "batch", core_mask)
        return jnp.concatenate([first, second[:, 2 * value.shape[1] - whole :]], axis=1)

    wanted = sent_requests.reshape(-1)
    found = embed.at[wanted].get(mode="promise_in_bounds").astype(low)
    found, pieces, proj_parts, proj_others = together(
        found.reshape(owners, capacity, width), exchange(pieces, "seq"), proj_parts, proj_others
    )
    returned = exchange(found, both)
    my_kv = pieces[..., ff_wide:].reshape(seq_count, half, 2, kv_width)
    my_kv = jnp.transpose(my_kv, (0, 2, 1, 3)).reshape(width, kv_width)
    other_kv = partner(my_kv, "batch", core_mask)
    my_gu = pieces[..., :ff_wide]
    proj_parts = to_index_order(jnp.concatenate([proj_parts] + proj_others), "seq", stages)
    my_q = proj_parts[..., :qkv_cut]
    other_q = partner(my_q, "batch", far_mask)
    out_parts = proj_parts[..., qkv_cut:]
    returned, my_kv, other_kv, my_gu, my_q, other_q, out_parts = together(
        returned, my_kv, other_kv, my_gu, my_q, other_q, out_parts
    )
    w_kv_full = jnp.concatenate(ordered(my_kv, other_kv, "batch", core_mask), axis=1)
    w_q_far = jnp.stack(ordered(my_q, other_q, "batch", far_mask), axis=1)
    w_q_far = w_q_far.reshape(width, qkv_cut)
    returned = returned.reshape(owners * capacity, width)
    w_q_full = core_columns(w_q_far, q_width + 2 * kv_width)[:, :q_width]
    w_out_far = far_rows(out_parts)
    other_gu = partner(after(my_gu, w_out_far), "batch", far_mask)

    places = seq_index * local_len + jnp.arange(local_len, dtype=jnp.int32)
    pick_places = seq_index * local_len + picks
    row_names = jnp.arange(batch_count, dtype=jnp.int32) == row_index
    prompt_here = jnp.sum(jnp.where(row_names, prompt_lengths, 0))
    length_here = jnp.sum(jnp.where(row_names, row_lengths, 0))
    live = ((pick_places >= prompt_here) & (pick_places + 1 < length_here)).astype(f32)
    advantage = (
        jnp.sum(jnp.where(row_names, rewards, 0.0)) - jnp.mean(rewards)
    ).reshape(1, 1)

    def rope_factors(slots):
        lane = jnp.arange(LANES, dtype=jnp.int32)
        frequency = ROPE_BASE ** (-2.0 * (lane % (HD // 2)).astype(f32) / HD)
        angles = slots.astype(f32)[:, None] * frequency[None, :]
        sign = jnp.where(lane % HD < HD // 2, -1.0, 1.0)
        return jnp.cos(angles), jnp.sin(angles) * sign[None, :]

    slot_cos, slot_sin = rope_factors(places)
    pick_cos, pick_sin = rope_factors(pick_places[0])
    bias_row = bias.reshape(1, -1)

    x_zero, normed_one, kv_low = in_vmem(
        embed_body,
        [like((local_len, width), low), like((local_len, width), low), like((seq_count, local_len, 2 * kv_width), low)],
        [returned, placer, w_kv_full, bias_row[:, q_width:], gains[:1], slot_cos, slot_sin],
        "keys_values",
        flops=2 * local_len * width * (owners * capacity + 2 * kv_width),
    )
    kv_all = exchange(kv_low, "seq")
    w_out_full = core_columns(w_out_far, width)
    picked_zero, target_rows, normed_picked, queries = in_vmem(
        pick_body,
        [
            like((n_picks, width)),
            like((n_picks, width)),
            like((n_picks, width), low),
            like((n_picks, q_width), low),
        ],
        [x_zero, normed_one, picks, w_q_full, bias_row[:, :q_width], pick_cos, pick_sin],
        "scored_queries",
        flops=2 * n_picks * width * (q_width + 3 * local_len),
    )
    kv_all, picked_zero, target_rows, normed_picked, queries, w_out_full, my_gu, other_gu = together(
        kv_all, picked_zero, target_rows, normed_picked, queries, w_out_full, my_gu, other_gu
    )
    gu_columns = jnp.stack(ordered(my_gu, other_gu, "batch", far_mask), axis=1)
    gu_columns = gu_columns.reshape(width, ff_wide)
    gu_others = partner(gu_columns, "batch", core_mask)
    kv_all = kv_all.reshape(seq_count * local_len, 2 * kv_width)
    length = kv_all.shape[0]
    limit = 24
    mixed, attended, stream_one, normed_two = in_vmem(
        attend_body,
        [
            like((n_picks, q_width), low),
            like((n_picks, q_width)),
            like((n_picks, width)),
            like((seq_count, n_picks, width), low),
        ],
        [queries, kv_all, pick_places, w_out_full, picked_zero, gains[1:2]],
        "attention",
        flops=4 * n_picks * q_width * length + 2 * n_picks * q_width * width,
        exps=n_picks * H * length,
        limit=limit,
    )


    def shard_columns(value):
        return jnp.transpose(value.reshape(n_picks, seq_count, shard), (1, 0, 2))

    normed_two_all, gu_columns, gu_others, column_pieces = together(
        exchange(normed_two, "seq"),
        gu_columns,
        gu_others,
        jnp.concatenate([shard_columns(normed_picked), shard_columns(mixed)], axis=1),
    )
    w_gate, w_up = ordered(gu_columns, gu_others, "batch", core_mask)
    normed_two_all = normed_two_all.reshape(row_count, width)
    gate_part, up_part, hidden, down_part = in_vmem(
        feed_body,
        [
            like((row_count, ff_wide)),
            like((row_count, ff_wide)),
            like((row_count, ff_wide), low),
            like((row_count, width), low),
        ],
        [normed_two_all, w_gate, w_up, w_down_low],
        "feed_forward",
        flops=6 * row_count * width * ff_part,
        limit=24,
        kept=(3,),
    )
    stream_two, final = in_vmem(
        feed_sum_body,
        [like((n_picks, width)), like((n_picks, width), low)],
        [exchange(down_part.reshape(seq_count, n_picks, width), "seq"), stream_one, gains[2:]],
        "final_norm",
    )

    near = jnp.stack([final, partner(final, "batch", far_mask)])
    rows = exchange_copies(near, "seq")
    other = partner(rows, "batch", core_mask)
    block = 1024

    gathered_columns = exchange(after(column_pieces, rows), "seq")

    def merge(*parts):
        return in_vmem(merge_body, [like(parts[0].shape, low)], parts, "merge_means")[0]

    far, gathered_columns = together(head_part(rows, other, 1, embed, block), gathered_columns)
    far_mean = merge(far[2], partner(far[3], "batch", core_mask))
    near_part, far_mean = together(
        head_part(after(rows, far_mean), other, 0, embed, block),
        partner(far_mean, "batch", far_mask),
    )
    means = merge(near_part[2], partner(near_part[3], "batch", core_mask), far_mean)
    mean_parts, gathered_columns = together(
        exchange(means.reshape(seq_count, n_picks, width + LANES), "seq"),
        to_xor_order(gathered_columns, "seq", stages),
    )
    message, grad_two, grad_gain_two, added, loss_here = in_vmem(
        loss_body,
        [
            like((seq_count, n_picks, width + LANES), low),
            like((n_picks, width)),
            like((1, width)),
            like((n_picks, width)),
            like((1, LANES)),
        ],
        [
            mean_parts,
            final,
            target_rows,
            stream_two,
            gains[2:],
            live,
            old_logp,
            ref_logp,
            advantage,
        ],
        "loss",
        kept=(2, 3, 4, 5, 6, 7),
    )

    messages = exchange(message, "seq").reshape(row_count, width + LANES)
    grad_gate, grad_up, normed_part = in_vmem(
        feed_back_body,
        [
            like((row_count, ff_wide), low),
            like((row_count, ff_wide), low),
            like((row_count, width), low),
        ],
        [messages, hidden, gate_part, up_part, w_gate, w_up, w_down_low],
        "feed_forward_back",
        flops=6 * row_count * width * ff_part,
        limit=28,
        kept=(1, 2, 3, 4, 5, 6),
    )
    normed_part = exchange(normed_part.reshape(seq_count, n_picks, width), "seq")

    layer_grads = in_vmem(
        layer_grads_body,
        [
            like((width, ff_wide), low),
            like((width, ff_wide), low),
            like((ff_part // 2, width), low),
            like((ff_part // 2, width), low),
        ],
        [
            core_row.reshape(1),
            normed_two_all,
            grad_gate,
            grad_up,
            hidden,
            messages,
        ],
        "layer_grads",
        flops=6 * row_count * width * ff_part,
        limit=24,
        kept=(1, 2, 3, 4, 5),
    )
    tails = messages[:, width:]
    tails = jnp.stack([tails, partner(tails, "batch", far_mask)])
    tails_other = partner(tails, "batch", core_mask)
    head_blocks = -(-vrows // (block // 2))
    head_args = (far, near_part, rows, other, tails, tails_other, vrows, block // 2, 2)
    head_cut = -(-head_blocks * 3 // 10)
    grad_head, head_squares = head_grad(*head_args, 0, head_cut, ())
    normed_part, layer_grads, grad_head, head_squares = together(
        normed_part, layer_grads, grad_head, head_squares
    )
    gu_own, gu_send, down_own, down_send = layer_grads
    gu_other = partner(gu_send, "batch", core_mask)
    down_other = partner(down_send, "batch", core_mask)
    grad_one, grad_one_low, grad_gain_one = in_vmem(
        one_back_body,
        [like((n_picks, width)), like((n_picks, width), low), like((1, width))],
        [
            normed_part,
            stream_one,
            grad_two,
            gains[1:2],
        ],
        "second_norm_back",
        kept=(1, 2, 3),
    )
    kv_grad, query_pre, query_bias = in_vmem(
        attend_back_body,
        [
            like((length, 2 * kv_width), low),
            like((n_picks, q_width), low),
            like((1, q_width)),
        ],
        [grad_one_low, w_out_full, queries, kv_all, pick_places, attended, pick_cos, pick_sin],
        "attention_back",
        flops=10 * n_picks * q_width * length,
        exps=n_picks * H * length,
        limit=limit + 4,
        kept=(1, 2, 3, 4, 5, 6, 7),
        scratch=[pltpu.VMEM((n_picks, q_width), f32)],
    )
    def far_cut(value):
        return cut(value[..., 0, :, :], value[..., 1, :, :], "batch", far_mask)

    def far_sides(value):
        front, back = value[..., 0, :, :], value[..., 1, :, :]
        return jnp.where(on_far, back, front), jnp.where(on_far, front, back)

    gu_own, down_own, kv_grad = together(gu_own, down_own, kv_grad)
    own_parts = exchange(kv_grad.reshape(seq_count, local_len, 2 * kv_width), "seq")
    gu_parts = far_sides(total_of([gu_own, gu_other]).reshape(seq_count, 2, half, ff_wide))
    down_parts = far_sides(total_of([down_own, down_other]).reshape(2, -1, width))
    gu_parts, down_parts, rows_late = together(gu_parts, down_parts, rows)
    gu_parts = gu_parts[0], partner(gu_parts[1], "batch", far_mask)
    down_parts = down_parts[0], partner(down_parts[1], "batch", far_mask)
    grad_head, more_squares = head_grad(
        *head_args[:2], rows_late, *head_args[3:],
        head_cut, head_blocks - head_cut, (grad_head,),
    )
    late_rows = spread(jnp.concatenate([query_pre, grad_one_low], axis=0), "seq", stages[:-1])
    late_others = [partner(late_rows, "seq", mask) for mask in stages[-1]]
    own_parts, gu_parts, down_parts, grad_head, more_squares, late_rows, late_others = together(
        own_parts, gu_parts, down_parts, grad_head, more_squares, late_rows, late_others
    )
    kv_pre, sendback, grad_gain_zero, kv_bias = in_vmem(
        zero_back_body,
        [
            like((local_len, 2 * kv_width), low),
            like((owners * capacity, width), low),
            like((1, width)),
            like((1, 2 * kv_width)),
        ],
        [
            own_parts,
            slot_cos,
            slot_sin,
            w_kv_full,
            query_pre,
            w_q_full,
            picks,
            x_zero,
            gains[:1],
            grad_one,
            added,
            placer,
        ],
        "first_norm_back",
        kept=(1, 2, 3, 4, 5, 6, 7, 8, 9, 10, 11),
        flops=2 * local_len * width * (2 * kv_width + owners * capacity + 6 * n_picks),
    )
    gu_part, down_part_w = total_of(gu_parts), total_of(down_parts)

    grad_head, sendback = together(grad_head, sendback)
    arrived = exchange(sendback.reshape(owners, capacity, width), both)
    head_rows = grad_head.at[wanted].get(mode="promise_in_bounds")
    late_rows = jnp.concatenate([late_rows] + late_others)
    q_half = dot_tn(
        gathered_columns[:, :n_picks].reshape(row_count, shard),
        late_rows[:, :n_picks].reshape(row_count, q_width),
    )
    out_half = dot_tn(
        gathered_columns[:, n_picks:].reshape(row_count, shard),
        late_rows[:, n_picks:].reshape(row_count, width),
    )
    proj_part = halve(q_half.astype(low), out_half.astype(low), "batch", core_mask)
    proj_part = total_of(far_cut(proj_part.reshape(2, half, width)))
    kv_w_grad = dot_tn(normed_one, kv_pre).astype(low)
    kv_blocks = jnp.transpose(
        kv_w_grad.reshape(seq_count, 2, half, 2, kv_width), (1, 3, 0, 2, 4)
    ).reshape(batch_count, seq_count, half, kv_width)
    kv_blocks = xor_order(kv_blocks, "batch")
    kv_part = total_of(
        [kv_blocks[0]] + [partner(kv_blocks[at], "batch", at) for at in range(1, batch_count)]
    )
    kv_part = collect(to_xor_order(kv_part, "seq", stages), "seq", stages)
    own_squares = (
        squares_of(gu_part)
        + squares_of(down_part_w)
        + squares_of(proj_part)
        + squares_of(kv_part)
        + jnp.sum(head_squares[0])
        + jnp.sum(more_squares[0])
    )
    arrived, head_rows, own_squares, gu_part, down_part_w, proj_part, kv_part = together(
        arrived, head_rows, own_squares, gu_part, down_part_w, proj_part, kv_part
    )
    arrived = arrived.reshape(-1, width)
    row_squares = in_vmem(
        summary_body, [like((1, 1))], [arrived, head_rows, wanted[None]], "row_squares"
    )
    own_squares = own_squares + row_squares[0][0, 0]
    summary = jnp.concatenate(
        [
            grad_gain_zero[0],
            grad_gain_one[0],
            grad_gain_two[0],
            query_bias[0],
            kv_bias[0],
            jnp.stack([own_squares, loss_here[0, 0], jnp.sum(live)]),
            jnp.zeros((LANES - 3,), f32),
        ]
    ).reshape(-1, LANES)
    totals, stats = in_vmem(
        norm_body,
        [like(summary.shape), like((1, LANES))],
        [exchange_copies(summary, both)],
        "grad_norm",
    )
    totals = totals.reshape(-1)
    grad_gains = totals[: 3 * width].reshape(3, width)
    grad_bias_all = totals[3 * width : -LANES]
    loss_sum, token_count, grad_norm, factor = (stats[0, at] for at in range(4))

    block = 608
    blocks = -(-vrows // block)
    cuts = [0, -(-blocks // 2), blocks]

    def update_rows(at, held, first):
        return table_adam(
            after(factor.reshape(1), first),
            wanted[None],
            arrived,
            grad_head,
            embed,
            embed_m,
            embed_v,
            block,
            cuts[at],
            cuts[at + 1] - cuts[at],
            held,
        )

    def both_halves(value, axis, mask, at):
        return jnp.concatenate(double(value, axis, mask), axis=at)

    gu_part, down_part_w, proj_part, kv_part, factor = together(
        gu_part, down_part_w, proj_part, kv_part, factor
    )
    gu_rows = exchange(gu_part, "seq")
    down_all = jnp.stack(double(down_part_w, "batch", far_mask), axis=0)
    small = both_halves(jnp.concatenate([proj_part, kv_part], axis=1), "batch", far_mask, 0)
    gu_rows, embed_new, down_all, small = together(
        gu_rows, update_rows(0, (), factor), down_all, small
    )
    gu_rows = jnp.transpose(gu_rows[..., :ff_part], (1, 0, 2)).reshape(half, FF)
    gu_far = both_halves(gu_rows, "batch", far_mask, 0)
    down_all = jnp.stack(double(down_all, "batch", core_mask), axis=0).reshape(w_down.shape)
    first_small, second_small = double(small, "batch", core_mask)
    qkv_all = jnp.concatenate(
        [first_small[:, :width], first_small[:, width:], second_small[:, width:]], axis=1
    )
    out_all = second_small[:, :width]
    gu_far, down_all, qkv_all, out_all, embed_new = together(
        gu_far, down_all, qkv_all, out_all, update_rows(1, tuple(embed_new), gu_rows)
    )
    gu_all = both_halves(gu_far, "batch", core_mask, 1)

    def update(weight, moment, second, gradient, rate):
        return adam(weight, moment, second, gradient.astype(f32) * factor, rate, DECAY)

    qkv_new = update(w_qkv, w_qkv_m, w_qkv_v, qkv_all, LR_MATRIX)
    out_new = update(w_out, w_out_m, w_out_v, out_all, LR_OUT)
    gateup_new = update(w_gateup, w_gateup_m, w_gateup_v, gu_all, LR_MATRIX)
    down_new = update(w_down, w_down_m, w_down_v, down_all, LR_MATRIX)
    gains_new = adam(gains, gains_m, gains_v, grad_gains * factor, LR_GAIN, 0.0)
    bias_new = adam(bias, bias_m, bias_v, grad_bias_all * factor, LR_BIAS, 0.0)
    return (
        loss_sum,
        token_count,
        grad_norm,
        *embed_new,
        *qkv_new,
        *out_new,
        *gateup_new,
        *down_new,
        *gains_new,
        *bias_new,
    )


def solution(mesh):
    in_specs = (
        P("batch", "seq"),
        P(),
        P(),
        P("batch", "seq"),
        P("batch", "seq"),
        P("batch", "seq"),
        P(),
        P(("batch", "seq"), None),
        P(("batch", "seq"), None),
        P(("batch", "seq"), None),
        P("seq", None),
        P("seq", None),
        P("seq", None),
        P("seq", None),
        P("seq", None),
        P("seq", None),
        P("seq", None),
        P("seq", None),
        P("seq", None),
        P("seq", None),
        P("seq", None),
        P("seq", None),
        P(),
        P(),
        P(),
        P(),
        P(),
        P(),
    )
    out_specs = (
        P(),
        P(),
        P(),
        P(("batch", "seq"), None),
        P(("batch", "seq"), None),
        P(("batch", "seq"), None),
        P("seq", None),
        P("seq", None),
        P("seq", None),
        P("seq", None),
        P("seq", None),
        P("seq", None),
        P("seq", None),
        P("seq", None),
        P("seq", None),
        P("seq", None),
        P("seq", None),
        P("seq", None),
        P(),
        P(),
        P(),
        P(),
        P(),
        P(),
    )
    return jax.shard_map(
        per_device, mesh=mesh, in_specs=in_specs, out_specs=out_specs, check_vma=False
    )
```
